512 devices in a mesh: seq: 64 (over z, x), expert: 8 (over y, core).
Axes of the slice: x: 4, y: 4, z: 16, core: 2. Of those that a mesh axis runs over, the one named last changes fastest.
Arguments:
- queries: bfloat16 [2, 16384, 4096], P(None, 'seq', 'expert'), may hold values from -6 to 6
- keys: bfloat16 [2, 16384, 4096], P(None, 'seq', 'expert'), may hold values from -6 to 6
- values: bfloat16 [2, 16384, 4096], P(None, 'seq', 'expert'), may hold values from -6 to 6
- log_decay: float32 [2, 16384, 32], P(None, 'seq', 'expert'), may hold values from -1 to 0
- norm_gain: float32 [4096], P('expert'), may hold values from 0.25 to 1.75
- expert_ids: int32 [512, 2], P('seq'), may hold values from 0 to 7, as said below
- gate_weights: float32 [512, 2], P('seq'), may hold values from 0.2 to 1
- w_gate: bfloat16 [8, 4096, 8192], P('expert', None, 'seq'), may hold values from -0.09375 to 0.09375
- w_up: bfloat16 [8, 4096, 8192], P('expert', None, 'seq'), may hold values from -0.09375 to 0.09375
- w_down: bfloat16 [8, 8192, 4096], P('expert', 'seq'), may hold values from -0.1875 to 0.1875
Outputs:
- attn_out: bfloat16 [2, 16384, 4096], P(None, 'seq', 'expert')
- moe_out: bfloat16 [512, 4096], P('seq', 'expert')
The draws below stay inside these ranges and needn't reach their ends.
Inputs may be any that keep to these rules, and one draw needn't show every extreme that they name: `expert_ids`: in each aligned block of 8 rows the two experts of a row differ and each expert is named at most 4 times; one expert, the same in every block, is named exactly 4 times in every block.
All inputs are finite; a program needn't handle non-finite values.
Results may differ from the reference program's by a relative error of at most 0.012.
Values may be sent and summed in bfloat16 or wider, within the bound.
No kernel may reach another device: no remote copies, remote signals or barrier semaphores. Data moves between devices by JAX's collectives and lax.ppermute only.
A program may use at most 128 MiB of HBM per device.

```python
import math
import jax
import jax.numpy as jnp
from jax import lax

HEAD_TOTAL = 32
HD = 128
D = 4096
FF = 8192
EXPERTS = 8
TOK_DEV = 256
MROWS = 8
SEQUENCE_LENGTH = 16384
MTOK = 512
CAP = 4


def draw_log_decay(key, part):
    sequence_lanes = jax.random.split(key, 7)
    fast_share = 5
    is_fast = jax.random.randint(sequence_lanes[0], (HEAD_TOTAL,), 0, 10) < fast_share
    fast_rate = jnp.exp(jax.random.uniform(sequence_lanes[1], (HEAD_TOTAL,), jnp.float32, math.log(1.0 / 50.0), math.log(1.0 / 30.0)))
    slow_rate = jax.random.uniform(sequence_lanes[2], (HEAD_TOTAL,), jnp.float32, 0.1, 0.5) / SEQUENCE_LENGTH
    base_rate = jnp.where(is_fast, fast_rate, slow_rate)
    block_total = SEQUENCE_LENGTH // TOK_DEV
    block_factor = jnp.exp(jax.random.uniform(sequence_lanes[3], (2, block_total, HEAD_TOTAL), jnp.float32, math.log(0.5), math.log(2.0)))
    token_factor = jax.random.uniform(sequence_lanes[4], (2, SEQUENCE_LENGTH, HEAD_TOTAL), jnp.float32, 0.5, 1.5)
    decay_speed = base_rate[None, None, :] * jnp.repeat(block_factor, TOK_DEV, axis=1) * token_factor
    spike_position = jax.random.randint(sequence_lanes[5], (2, 2, HEAD_TOTAL), 0, SEQUENCE_LENGTH)
    spike_loss = -jnp.log(1.0 - jax.random.uniform(sequence_lanes[6], (2, 2, HEAD_TOTAL), jnp.float32, 0.2, 0.4))
    inner_position = jnp.arange(SEQUENCE_LENGTH, dtype=jnp.int32)
    match_flags = inner_position[None, :, None, None] == spike_position[:, None, :, :]
    spike_groups = jnp.sum(jnp.where(match_flags, spike_loss[:, None, :, :], 0.0), axis=2)
    return -(decay_speed + spike_groups)


def draw_expert_ids(key, part):
    base_key = jax.random.fold_in(key, 7)
    heavy = jax.random.randint(jax.random.fold_in(base_key, 1), (), 0, EXPERTS)
    popular = jax.random.randint(jax.random.fold_in(base_key, 2), (EXPERTS,), 0, 4) * 64
    block_total = MTOK // MROWS
    needed = 2 * MROWS - CAP

    def one_block(index):
        block_key = jax.random.fold_in(base_key, 100 + index)
        sequence_lanes = jax.random.split(block_key, 3)
        ticket = jnp.arange(EXPERTS * CAP, dtype=jnp.int32)
        owner = ticket // CAP
        score = popular[owner] + jax.random.randint(sequence_lanes[0], (EXPERTS * CAP,), 0, 64)
        score = jnp.where(owner == heavy, -1, score)
        order = jnp.argsort(-(score * (EXPERTS * CAP) + ticket))
        chosen = owner[order[:needed]]
        pool = jnp.sort(jnp.concatenate([jnp.full((CAP,), heavy, jnp.int32), chosen]))
        pairs = jnp.stack([pool[:MROWS], pool[MROWS:]], axis=1)
        shuffled = pairs[jax.random.permutation(sequence_lanes[1], MROWS)]
        flip = jax.random.randint(sequence_lanes[2], (MROWS, 1), 0, 2)
        return jnp.where(flip == 1, shuffled[:, ::-1], shuffled)
    blocks = jax.vmap(one_block)(jnp.arange(block_total, dtype=jnp.int32))
    return blocks.reshape(MTOK, 2).astype(jnp.int32)


def raised(entries, key, source, target, shards_of, factor):
    owner, partner = [(jnp.arange(entries.shape[dim]) // (entries.shape[dim] // shards_of)).reshape([-1 if axis == dim else 1 for axis in range(entries.ndim)]) for dim in (source, target)]
    chosen = jax.random.permutation(key, shards_of)[partner]
    strong = (owner == chosen) | (owner == (partner + shards_of // 2) % shards_of)
    return jnp.where(strong, factor * entries, entries)


def levels(stream_key, shape, shards, low, high):
    def one(position, parts):
        draws = jax.random.uniform(jax.random.fold_in(jax.random.fold_in(stream_key, 6), position), (parts,), jnp.float32, low / len(shards), high / len(shards))
        return jnp.repeat(jnp.exp(draws), shape[position] // parts).reshape((-1,) + (1,) * (len(shape) - position - 1))

    gain = one(*shards[0])
    for cut in shards[1:]:
        gain = gain * one(*cut)
    return gain


def centred(own_key, dims, spread, bound, cuts=(), kind=jnp.bfloat16):
    loudness = levels(own_key, dims, cuts, -0.22, 0.18) if cuts else 1.0
    values = jax.random.normal(own_key, dims, jnp.float32) * spread * loudness
    return jnp.minimum(jnp.maximum(values, -bound), bound).astype(kind)


def gaussian_with(rng, shape, scale, limit, pieces, heavy, held_as=jnp.bfloat16):
    values = scale * jax.random.normal(rng, shape, jnp.float32)
    if pieces:
        values = values * levels(rng, shape, pieces, -0.22, 0.18)
    return jnp.clip(raised(values, jax.random.fold_in(rng, 3), *heavy), -limit, limit).astype(held_as)


def setup_inputs(seed: int = 0) -> dict:
    seeds = jax.random.split(jax.random.key(seed), 11)
    return {
        "queries": centred(seeds[0], (2, SEQUENCE_LENGTH, HEAD_TOTAL * HD), 1.0, 6.0, ((1, 64), (2, 8))),
        "keys": centred(seeds[1], (2, SEQUENCE_LENGTH, HEAD_TOTAL * HD), 1.0, 6.0, ((1, 64), (2, 8))),
        "values": centred(seeds[2], (2, SEQUENCE_LENGTH, HEAD_TOTAL * HD), 1.0, 6.0, ((1, 64), (2, 8))),
        "log_decay": draw_log_decay(jax.random.fold_in(seeds[10], 71), 0),
        "norm_gain": jnp.clip(1.0 + 0.15 * jax.random.normal(seeds[4], (HEAD_TOTAL * HD,), jnp.float32), 0.25, 1.75),
        "expert_ids": draw_expert_ids(jax.random.fold_in(seeds[10], 71), 0),
        "gate_weights": jnp.clip(0.2 + 0.8 * jax.random.uniform(seeds[6], (MTOK, 2), jnp.float32) ** levels(seeds[6], (MTOK, 2), ((0, 64),), -0.2, 0.2), 0.2, 1.0),
        "w_gate": centred(seeds[7], (EXPERTS, D, FF), D ** -0.5, 0.09375, ((0, 8), (2, 64))),
        "w_up": centred(seeds[8], (EXPERTS, D, FF), D ** -0.5, 0.09375, ((0, 8), (2, 64))),
        "w_down": gaussian_with(seeds[9], (EXPERTS, FF, D), FF ** -0.5, 0.1875, ((0, 8), (1, 64)), (1, 2, 64, 4.0)),
    }


def to_bf16(array):
    return lax.optimization_barrier(array.astype(jnp.bfloat16)).astype(jnp.float32)

def block_attention(query_f, key_f, value_f, decay_log, carried):
    running = jnp.cumsum(decay_log, axis=1)
    block_end = running[:, -1:, :]
    length = query_f.shape[1]
    causal = jnp.arange(length, dtype=jnp.int32)[:, None] >= jnp.arange(length, dtype=jnp.int32)[None, :]
    run_heads = jnp.transpose(running, (0, 2, 1))
    spread_log = run_heads[:, :, :, None] - run_heads[:, :, None, :]
    fading = jnp.where(causal[None, None, :, :], jnp.exp(jnp.minimum(spread_log, 0.0)), 0.0)
    scores = jnp.einsum('bthd,bshd->bhts', query_f, key_f)
    weights = to_bf16(scores * fading)
    local_part = jnp.einsum('bhts,bshd->bthd', weights, value_f)
    decayed_queries = to_bf16(query_f * jnp.exp(running)[..., None])
    carried_part = jnp.einsum('bthd,bhde->bthe', decayed_queries, to_bf16(carried))
    decayed_keys = to_bf16(key_f * jnp.exp(block_end - running)[..., None])
    update = jnp.einsum('bshd,bshe->bhde', decayed_keys, value_f)
    factor = jnp.exp(block_end[:, 0, :])
    new_state = factor[:, :, None, None] * carried + update
    combined = local_part + carried_part
    inverse_rms = lax.rsqrt(lax.optimization_barrier(jnp.mean(combined * combined, axis=-1, keepdims=True)) + 1e-06)
    return (combined * inverse_rms, new_state)

def reference(queries, keys, values, log_decay, norm_gain, expert_ids, gate_weights, w_gate, w_up, w_down):
    block_count = SEQUENCE_LENGTH // TOK_DEV

    def to_blocks(array):
        shaped = array.astype(jnp.float32).reshape(2, block_count, TOK_DEV, HEAD_TOTAL, HD)
        return jnp.transpose(shaped, (1, 0, 2, 3, 4))
    decay_blocks = jnp.transpose(log_decay.reshape(2, block_count, TOK_DEV, HEAD_TOTAL), (1, 0, 2, 3))

    def advance(state, block_inputs):
        query_f, key_f, value_f, decay_log = block_inputs
        normed, new_state = block_attention(query_f, key_f, value_f, decay_log, state)
        return (new_state, normed)
    empty_state = jnp.zeros((2, HEAD_TOTAL, HD, HD), jnp.float32)
    _, block_outputs = lax.scan(advance, empty_state, (to_blocks(queries), to_blocks(keys), to_blocks(values), decay_blocks))
    gain_heads = norm_gain.reshape(HEAD_TOTAL, HD)
    attn_full = (block_outputs * gain_heads).astype(jnp.bfloat16)
    attn_out = jnp.transpose(attn_full, (1, 0, 2, 3, 4)).reshape(2, SEQUENCE_LENGTH, HEAD_TOTAL * HD)
    half_rows = MROWS // 2
    heads_rows = attn_out.reshape(2, block_count, TOK_DEV, D)[:, :, :half_rows, :]
    moe_in = jnp.transpose(heads_rows, (1, 0, 2, 3)).reshape(MTOK, D)
    source_blocks = MTOK // MROWS
    pair_ids = expert_ids.reshape(source_blocks, 2 * MROWS)
    onehot = (pair_ids[:, :, None] == jnp.arange(EXPERTS, dtype=jnp.int32)[None, None, :]).astype(jnp.int32)
    before = jnp.cumsum(onehot, axis=1) - onehot
    slot_index = lax.optimization_barrier(jnp.sum(before * onehot, axis=2))
    slot_row = (jnp.arange(source_blocks, dtype=jnp.int32)[:, None] * CAP + slot_index).reshape(MTOK, 2).astype(jnp.int32)
    dump_row = source_blocks * CAP
    source = jnp.broadcast_to(moe_in[:, None, :], (MTOK, 2, D)).reshape(MTOK * 2, D)
    summed = jnp.zeros((MTOK, D), jnp.float32)
    for expert in range(EXPERTS):
        match_flags = expert_ids == expert
        target = jnp.where(match_flags, slot_row, dump_row).astype(jnp.int32)
        buffer = jnp.zeros((dump_row + 1, D), jnp.bfloat16).at[target.reshape(-1)].set(source)[:-1]
        gate_act = jnp.dot(buffer, w_gate[expert], preferred_element_type=jnp.float32)
        up_act = jnp.dot(buffer, w_up[expert], preferred_element_type=jnp.float32)
        hidden = (jax.nn.silu(gate_act) * up_act).astype(jnp.bfloat16)
        result = jnp.dot(hidden, w_down[expert], preferred_element_type=jnp.float32).astype(jnp.bfloat16)
        picked = result[jnp.minimum(target, dump_row - 1)].astype(jnp.float32)
        summed = summed + lax.optimization_barrier(jnp.sum(jnp.where(match_flags[:, :, None], gate_weights[:, :, None] * picked, 0.0), axis=1))
    moe_out = summed.astype(jnp.bfloat16)
    return (attn_out, moe_out)
```

```python
import jax
import jax.numpy as jnp
from jax import lax
from jax.experimental import pallas as pl
from jax.experimental.pallas import tpu as pltpu
from jax.sharding import Mesh
from jax.sharding import PartitionSpec as P

HD = 128
HEADS = 4
PAIRS = 8
TOK = 256
Z, X, Y, CORE = 16, 4, 4, 2
EXPERTS = Y * CORE
MROWS = 8
CAP = 4
COLS = HEADS * HD
OWN = PAIRS // X
PART = OWN * HD // Z
SLOTS = Z * CAP
GROUP = Z * MROWS
INFO = 128
F32 = jnp.float32
BF16 = jnp.bfloat16


def call(kernel, out, name):
    vmem = pl.BlockSpec(memory_space=pltpu.VMEM)
    return pl.pallas_call(
        kernel,
        out_shape=out,
        out_specs=jax.tree.map(lambda _: vmem, out),
        compiler_params=pltpu.CompilerParams(vmem_limit_bytes=40 * 2**20),
        name=name,
    )


def split_log(log):
    first = jnp.floor(log * 0.125) * 8.0
    rest = log - first
    second = jnp.floor(rest * 32.0) * (1.0 / 32.0)
    rest = rest - second
    third = jnp.floor(rest * 8192.0) * (1.0 / 8192.0)
    return first, second, third, rest - third


def stacked_rows(rows):
    index = lax.broadcasted_iota(jnp.int32, (8, HD), 0)
    total = jnp.zeros((8, HD), F32)
    for i, row in enumerate(rows):
        total = jnp.where(index == i, jnp.broadcast_to(row, (8, HD)), total)
    return total


def joined_log(rows, first):
    return (rows[first : first + 1] + rows[first + 1 : first + 2]) + (
        rows[first + 2 : first + 3] + rows[first + 3 : first + 4]
    )


def update_kernel(decay_ref, k_ref, v_ref, run_ref, msg_ref):
    running = decay_ref[...]
    lane = lax.broadcasted_iota(jnp.int32, (PAIRS, TOK), 1)
    shift = 1
    while shift < TOK:
        running = running + jnp.where(lane >= shift, pltpu.roll(running, shift, 1), 0.0)
        shift *= 2
    run_ref[...] = running
    end = running[:, TOK - 1 :]
    to_end = jnp.exp(end - running).T
    for owner in range(X):
        parts, logs = [], []
        for i in range(OWN):
            pair = owner * OWN + i
            b, cols = pair // HEADS, pl.ds(pair % HEADS * HD, HD)
            decayed = (k_ref[b, :, cols].astype(F32) * to_end[:, pair : pair + 1]).astype(BF16)
            parts.append(
                lax.dot_general(
                    decayed, v_ref[b, :, cols], (((0,), (0,)), ((), ())), preferred_element_type=F32
                )
            )
            logs += [jnp.broadcast_to(p, (1, HD)) for p in split_log(end[pair : pair + 1])]
        msg_ref[owner] = jnp.concatenate(parts + [stacked_rows(logs)], axis=0).astype(BF16)


def group_kernel(msg_ref, out_ref):
    total = [None] * OWN
    logs = [None] * OWN
    for x in range(X):
        part = msg_ref[x].astype(F32)
        for i in range(OWN):
            update = part[i * HD : (i + 1) * HD]
            log = joined_log(part, OWN * HD + 4 * i)
            if x == 0:
                total[i], logs[i] = update, log
            else:
                total[i], logs[i] = jnp.exp(log) * total[i] + update, logs[i] + log
    for i in range(OWN):
        info = stacked_rows(split_log(logs[i]))
        for g in range(HD // PART):
            out_ref[i * (HD // PART) + g] = jnp.concatenate(
                [total[i][g * PART : (g + 1) * PART], info], axis=0
            ).astype(BF16)


def scan_kernel(msg_ref, out_ref):
    state = jnp.zeros((PART, HD), F32)
    for z in range(Z):
        out_ref[z] = state.astype(BF16)
        part = msg_ref[z].astype(F32)
        state = jnp.exp(joined_log(part, PART)) * state + part[:PART]


def expand_kernel(prefix_ref, msg_ref, out_ref):
    prefix = prefix_ref[...].astype(F32)
    state = [prefix[i * HD : (i + 1) * HD] for i in range(OWN)]
    for x in range(X):
        out_ref[x] = jnp.concatenate(state, axis=0).astype(BF16)
        if x < X - 1:
            part = msg_ref[x].astype(F32)
            for i in range(OWN):
                factor = jnp.exp(joined_log(part, OWN * HD + 4 * i))
                state[i] = factor * state[i] + part[i * HD : (i + 1) * HD]


def attention_kernel(
    q_ref, k_ref, v_ref, run_ref, state_ref, gain_ref, ids_ref, gates_ref, out_ref, rows_ref
):
    running = run_ref[...]
    columns = running.T
    causal = lax.broadcasted_iota(jnp.int32, (TOK, TOK), 0) >= lax.broadcasted_iota(
        jnp.int32, (TOK, TOK), 1
    )
    for pair in range(PAIRS):
        b, cols = pair // HEADS, pl.ds(pair % HEADS * HD, HD)
        q, v = q_ref[b, :, cols], v_ref[b, :, cols]
        scores = lax.dot_general(
            q, k_ref[b, :, cols], (((1,), (1,)), ((), ())), preferred_element_type=F32
        )
        column = columns[:, pair : pair + 1]
        spread = jnp.minimum(column - running[pair : pair + 1], 0.0)
        weights = jnp.where(causal, scores * jnp.exp(spread), 0.0).astype(BF16)
        decayed = (q.astype(F32) * jnp.exp(column)).astype(BF16)
        o = jnp.dot(weights, v, preferred_element_type=F32) + jnp.dot(
            decayed, state_ref[pair], preferred_element_type=F32
        )
        scale = lax.rsqrt(jnp.mean(o * o, axis=1, keepdims=True) + 1e-6)
        out_ref[b, :, cols] = (o * scale * gain_ref[:, cols]).astype(BF16)
    half = MROWS // 2
    one = out_ref[0, :16].astype(F32)[:MROWS]
    two = out_ref[1, :16].astype(F32)[:MROWS]
    token = lax.broadcasted_iota(jnp.int32, (MROWS, COLS), 0)
    routed = jnp.where(token < half, one, pltpu.roll(two, half, 0))
    ids = ids_ref[...]
    names = [ids[:, 0:1], ids[:, 1:2]]
    earlier = lax.broadcasted_iota(jnp.int32, (MROWS, 1), 0)
    slots = [jnp.zeros((MROWS, 1), jnp.int32), (names[0] == names[1]).astype(jnp.int32)]
    for t in range(MROWS - 1):
        for c in range(2):
            other = jnp.broadcast_to(names[c][t : t + 1], (MROWS, 1))
            for j in range(2):
                same = (other == names[j]) & (earlier > t)
                slots[j] = slots[j] + same.astype(jnp.int32)
    gates = gates_ref[...]
    lane = lax.broadcasted_iota(jnp.int32, (MROWS, INFO), 1)
    info = jnp.zeros((MROWS, INFO), F32)
    facts = [names[0].astype(F32), slots[0].astype(F32), names[1].astype(F32), slots[1].astype(F32)]
    facts += [gates[:, 0:1], gates[:, 1:2]]
    for i, fact in enumerate(facts):
        info = jnp.where(lane == i, jnp.broadcast_to(fact, (MROWS, INFO)), info)
    message = jnp.concatenate([routed, info], axis=1).astype(BF16)
    for z in range(Z):
        rows_ref[z] = message


def slot_lanes(info):
    place = (lax.broadcasted_iota(jnp.int32, (GROUP, 1), 0) // MROWS) * CAP
    lanes = []
    for j in range(2):
        name, slot = info[:, 2 * j : 2 * j + 1], info[:, 2 * j + 1 : 2 * j + 2]
        lanes.append((name * float(SLOTS) + slot).astype(jnp.int32) + place)
    return lanes


def dispatch_kernel(rows_ref, out_ref):
    lane = lax.broadcasted_iota(jnp.int32, (GROUP, EXPERTS * SLOTS), 1)
    for x in range(X):
        first, second = slot_lanes(rows_ref[x, :, COLS:].astype(F32))
        chosen = jnp.where((lane == first) | (lane == second), 1.0, 0.0).astype(BF16)
        sent = lax.dot_general(
            chosen, rows_ref[x, :, :COLS], (((0,), (0,)), ((), ())), preferred_element_type=F32
        ).astype(BF16)
        for e in range(EXPERTS):
            out_ref[e, x * SLOTS : (x + 1) * SLOTS] = sent[e * SLOTS : (e + 1) * SLOTS]


def expert_kernel(rows_ref, gate_ref, up_ref, down_ref, out_ref):
    total = None
    for j in range(EXPERTS):
        part = pl.ds(j * COLS, COLS)
        both = jnp.concatenate([gate_ref[part, :], up_ref[part, :]], axis=1)
        term = jnp.dot(rows_ref[j], both, preferred_element_type=F32)
        total = term if total is None else total + term
    width = gate_ref.shape[1]
    gate, up = total[:, :width], total[:, width:]
    hidden = (gate / (1.0 + jnp.exp(-gate)) * up).astype(BF16)
    for j in range(EXPERTS):
        out_ref[j] = jnp.dot(
            hidden, down_ref[:, pl.ds(j * COLS, COLS)], preferred_element_type=F32
        ).astype(BF16)


def combine_kernel(rows_ref, info_ref, out_ref):
    lane = lax.broadcasted_iota(jnp.int32, (GROUP, EXPERTS * SLOTS), 1)
    for x in range(X):
        info = info_ref[x, :, COLS:].astype(F32)
        first, second = slot_lanes(info)
        mix = jnp.where(lane == first, info[:, 4:5], 0.0) + jnp.where(
            lane == second, info[:, 5:6], 0.0
        )
        own = jnp.concatenate(
            [rows_ref[e, x * SLOTS : (x + 1) * SLOTS] for e in range(EXPERTS)], axis=0
        )
        out_ref[x] = jnp.dot(mix.astype(BF16), own, preferred_element_type=F32).astype(BF16)


def sum_kernel(parts_ref, out_ref):
    total = parts_ref[0].astype(F32)
    for i in range(1, parts_ref.shape[0]):
        total = total + parts_ref[i].astype(F32)
    out_ref[...] = total.astype(BF16)


def swap(array, axis):
    return lax.all_to_all(array, axis, 0, 0, tiled=True)


def body(
    queries, keys, values, log_decay, norm_gain, expert_ids, gate_weights, w_gate, w_up, w_down
):
    shape = jax.ShapeDtypeStruct
    decay = jnp.transpose(log_decay, (0, 2, 1)).reshape(PAIRS, TOK)
    running, message = call(
        update_kernel,
        (shape((PAIRS, TOK), F32), shape((X, OWN * HD + 8, HD), BF16)),
        "update",
    )(decay, keys, values)
    message = swap(message, "x")
    groups = call(group_kernel, shape((Z, PART + 8, HD), BF16), "group")(message)
    groups = swap(groups, "z")
    prefix = call(scan_kernel, shape((Z, PART, HD), BF16), "scan")(groups)
    prefix = swap(prefix, "z").reshape(OWN * HD, HD)
    states = call(expand_kernel, shape((X, OWN * HD, HD), BF16), "expand")(prefix, message)
    states = swap(states, "x").reshape(PAIRS, HD, HD)
    attn_out, rows = call(
        attention_kernel,
        (shape((2, TOK, COLS), BF16), shape((Z, MROWS, COLS + INFO), BF16)),
        "attention",
    )(
        queries, keys, values, running, states, norm_gain.reshape(1, COLS), expert_ids, gate_weights
    )
    rows = swap(rows, "z").reshape(GROUP, COLS + INFO)
    rows = lax.all_gather(rows, "x", axis=0)
    slots = call(dispatch_kernel, shape((EXPERTS, X * SLOTS, COLS), BF16), "dispatch")(rows)
    slots = swap(slots, ("y", "core"))
    slots = call(expert_kernel, shape((EXPERTS, X * SLOTS, COLS), BF16), "experts")(
        slots, w_gate[0], w_up[0], w_down[0]
    )
    slots = swap(slots, ("y", "core"))
    share = call(combine_kernel, shape((X, GROUP, COLS), BF16), "combine")(slots, rows)
    share = swap(share, "x")
    share = call(sum_kernel, shape((GROUP, COLS), BF16), "sum_x")(share)
    share = swap(share.reshape(Z, MROWS, COLS), "z")
    moe_out = call(sum_kernel, shape((MROWS, COLS), BF16), "sum_z")(share)
    return (attn_out, moe_out)


def solution(mesh):
    fine = Mesh(mesh.devices.reshape(Z, X, Y, CORE), ("z", "x", "y", "core"))
    seq, expert = ("z", "x"), ("y", "core")
    placed = (
        P(None, seq, expert),
        P(None, seq, expert),
        P(None, seq, expert),
        P(None, seq, expert),
        P(expert),
        P(seq, None),
        P(seq, None),
        P(expert, None, seq),
        P(expert, None, seq),
        P(expert, seq, None),
    )
    return jax.shard_map(
        body,
        mesh=fine,
        in_specs=placed,
        out_specs=(P(None, seq, expert), P(seq, expert)),
        check_vma=False,
    )
```

```python
import jax
import jax.numpy as jnp
from jax import lax
from jax.experimental import pallas as pl
from jax.experimental.pallas import tpu as pltpu
from jax.sharding import Mesh
from jax.sharding import PartitionSpec as P

HD = 128
HEADS = 4
PAIRS = 8
TOK = 256
Z, X, Y, CORE = 16, 4, 4, 2
EXPERTS = Y * CORE
MROWS = 8
CAP = 4
COLS = HEADS * HD
OWN = PAIRS // X
PART = OWN * HD // Z
HALF = MROWS // 2
FEW = 16
GROUP = Z * MROWS
AT_LOGS = OWN * HD
AT_Q = AT_LOGS + 8
AT_LOCAL = AT_Q + 8
AT_FACTS = AT_LOCAL + 16
F32 = jnp.float32
BF16 = jnp.bfloat16


def call(kernel, out, name, scratch=()):
    vmem = pl.BlockSpec(memory_space=pltpu.VMEM)
    return pl.pallas_call(
        kernel,
        out_shape=out,
        out_specs=jax.tree.map(lambda _: vmem, out),
        scratch_shapes=scratch,
        compiler_params=pltpu.CompilerParams(vmem_limit_bytes=40 * 2**20),
        name=name,
    )


def split_log(log):
    first = jnp.floor(log * 0.125) * 8.0
    rest = log - first
    second = jnp.floor(rest * 32.0) * (1.0 / 32.0)
    rest = rest - second
    third = jnp.floor(rest * 8192.0) * (1.0 / 8192.0)
    return first, second, third, rest - third


def stacked_rows(rows):
    index = lax.broadcasted_iota(jnp.int32, (8, HD), 0)
    total = jnp.zeros((8, HD), F32)
    for i, row in enumerate(rows):
        total = jnp.where(index == i, jnp.broadcast_to(row, (8, HD)), total)
    return total


def joined_log(rows, first):
    return (rows[first : first + 1] + rows[first + 1 : first + 2]) + (
        rows[first + 2 : first + 3] + rows[first + 3 : first + 4]
    )


def prefix_sums(rows):
    lane = lax.broadcasted_iota(jnp.int32, rows.shape, 1)
    shift = 1
    while shift < TOK:
        rows = rows + jnp.where(lane >= shift, pltpu.roll(rows, shift, 1), 0.0)
        shift *= 2
    return rows


def fading_scores(q, k, column, row):
    scores = lax.dot_general(q, k, (((1,), (1,)), ((), ())), preferred_element_type=F32)
    causal = lax.broadcasted_iota(jnp.int32, scores.shape, 0) >= lax.broadcasted_iota(
        jnp.int32, scores.shape, 1
    )
    fading = jnp.exp(jnp.minimum(column - row, 0.0))
    return jnp.where(causal, scores * fading, 0.0).astype(BF16)


def beside(one, two):
    row = lax.broadcasted_iota(jnp.int32, one.shape, 0)
    return jnp.where(row < HALF, one, pltpu.roll(two, HALF, 0))


def two_parts(array):
    coarse = array.astype(BF16).astype(F32)
    return coarse, array - coarse


def route_facts(ids_ref, gates_ref, facts_ref):
    facts_ref[...] = jnp.zeros((8, HD), F32)
    facts_ref[0:2, 0:MROWS] = ids_ref[...].astype(F32)
    facts_ref[6:8, 0:MROWS] = gates_ref[...]
    names = facts_ref[0:2, :]
    lane = lax.broadcasted_iota(jnp.int32, (2, HD), 1)
    choice = lax.broadcasted_iota(jnp.int32, (2, HD), 0)
    slots = jnp.where((choice == 1) & (names[0:1] == names[1:2]), 1.0, 0.0)
    for t in range(MROWS - 1):
        for c in range(2):
            same = (names[c : c + 1, t : t + 1] == names) & (lane > t)
            slots = slots + jnp.where(same, 1.0, 0.0)
    facts_ref[4:6, :] = jnp.where(lane < MROWS, names * float(CAP) + slots, 0.0)
    facts_ref[0:2, :] = jnp.zeros((2, HD), F32)


def update_kernel(
    decay_ref, q_ref, k_ref, v_ref, ids_ref, gates_ref, run_ref, msg_ref, facts_ref
):
    running = prefix_sums(decay_ref[...])
    run_ref[...] = running
    end = running[:, TOK - 1 :]
    to_end = jnp.exp(end - running).T
    columns = running.T[:FEW]
    route_facts(ids_ref, gates_ref, facts_ref)
    for owner in range(X):
        parts, logs, qs, locals_ = [], [], [], []
        for i in range(OWN):
            pair = owner * OWN + i
            b, cols = pair // HEADS, pl.ds(pair % HEADS * HD, HD)
            decayed = (k_ref[b, :, cols].astype(F32) * to_end[:, pair : pair + 1]).astype(BF16)
            parts.append(
                lax.dot_general(
                    v_ref[b, :, cols], decayed, (((0,), (0,)), ((), ())), preferred_element_type=F32
                )
            )
            logs += [jnp.broadcast_to(p, (1, HD)) for p in split_log(end[pair : pair + 1])]
            q, column = q_ref[b, :FEW, cols], columns[:, pair : pair + 1]
            weights = fading_scores(
                q, k_ref[b, :FEW, cols], column, running[pair : pair + 1, :FEW]
            )
            local = jnp.dot(weights, v_ref[b, :FEW, cols], preferred_element_type=F32)
            locals_.append(local[:8])
            qs.append((q.astype(F32) * jnp.exp(column))[:8])
        local = two_parts(beside(*locals_))
        msg_ref[owner] = jnp.concatenate(
            parts + [stacked_rows(logs), beside(*qs), local[0], local[1], facts_ref[...]], axis=0
        ).astype(BF16)


def placed(rows, i, x):
    row = lax.broadcasted_iota(jnp.int32, rows.shape, 0)
    moved = rows if i == x % 2 else pltpu.roll(rows, HALF, 0)
    moved = jnp.where(row // HALF == x % 2, moved, 0.0)
    zero = jnp.zeros_like(moved)
    return jnp.concatenate([moved, zero] if x < 2 else [zero, moved], axis=0)


def tall(rows):
    return jnp.concatenate([rows, jnp.zeros((HD - rows.shape[0], HD), F32)], axis=0)


def group_kernel(msg_ref, out_ref):
    lane = lax.broadcasted_iota(jnp.int32, (8, HD), 1)
    facts = jnp.zeros((8, HD), F32)
    for x in range(X):
        own = msg_ref[x].astype(F32)[AT_FACTS:]
        for b in range(2):
            only = jnp.where(lane // HALF == b, own, 0.0)
            shift = b * 16 + x * HALF - b * HALF
            facts = facts + (pltpu.roll(only, shift, 1) if shift else only)
    for i in range(OWN):
        total, log, queries, near, inner = None, None, 0.0, 0.0, 0.0
        for x in range(X):
            part = msg_ref[x].astype(F32)
            update = part[i * HD : (i + 1) * HD]
            own_log = joined_log(part, AT_LOGS + 4 * i)
            q = placed(part[AT_Q : AT_Q + 8], i, x)
            local = part[AT_LOCAL : AT_LOCAL + 8] + part[AT_LOCAL + 8 : AT_LOCAL + 16]
            near = near + placed(local, i, x)
            if x == 0:
                queries = q
                total, log = update, own_log
            else:
                inner = inner + lax.dot_general(
                    total.astype(BF16),
                    tall(q).astype(BF16),
                    (((1,), (1,)), ((), ())),
                    preferred_element_type=F32,
                )
                queries = queries + q * jnp.exp(log)
                total, log = jnp.exp(own_log) * total + update, log + own_log
        coarse, rest = two_parts(inner + tall(near).T)
        rows = coarse + pltpu.roll(rest, 16, 1)
        info = stacked_rows(split_log(log)) + facts
        for g in range(HD // PART):
            piece = slice(g * PART, (g + 1) * PART)
            out_ref[i * (HD // PART) + g] = jnp.concatenate(
                [total[piece], info, queries, rows[piece]], axis=0
            ).astype(BF16)


def scan_kernel(msg_ref, out_ref, facts_ref):
    state = jnp.zeros((PART, HD), F32)
    lane = lax.broadcasted_iota(jnp.int32, (16, HD), 1)
    states, queries = [], []
    near = [jnp.zeros((PART, HD), F32) for _ in range(2)]
    facts = [jnp.zeros((8, HD), F32) for _ in range(4)]
    for z in range(Z):
        states.append(state)
        part = msg_ref[z].astype(F32)
        info, query, rows = part[16:24], part[24:40], part[40:56]
        queries.append(query)
        half, shift = z // 8, z % 8 * 16
        rows = jnp.where(lane < 16, rows + pltpu.roll(rows, HD - 16, 1), 0.0)
        near[half] = near[half] + (pltpu.roll(rows, shift, 1) if shift else rows)
        for b in range(2):
            only = jnp.where(lane[:8] // 16 == b, info, 0.0)
            move = (shift - b * 16) % HD
            place = half * 2 + b
            facts[place] = facts[place] + (pltpu.roll(only, move, 1) if move else only)
        state = jnp.exp(joined_log(part, PART)) * state + part[:PART]
    far = lax.dot_general(
        jnp.concatenate(states, axis=0).astype(BF16),
        jnp.concatenate(queries, axis=0).astype(BF16),
        (((1,), (1,)), ((), ())),
        preferred_element_type=F32,
    )
    row = lax.broadcasted_iota(jnp.int32, far.shape, 0)
    column = lax.broadcasted_iota(jnp.int32, far.shape, 1)
    far = jnp.where(row // 16 == column // 16, far, 0.0)
    total = jnp.concatenate(near, axis=1)
    for z in range(Z):
        total = total + far[z * PART : (z + 1) * PART]
    for z in range(Z):
        out_ref[z] = jnp.concatenate(
            [states[z], total[:, :HD], total[:, HD:]], axis=0
        ).astype(BF16)
    facts_ref[...] = jnp.concatenate(facts, axis=1)


def expand_kernel(back_ref, msg_ref, gain_ref, out_ref):
    odd = lax.rem(lax.axis_index("x"), 2)
    gain = jnp.where(odd == 1, gain_ref[:, OWN * HD :], gain_ref[:, : OWN * HD])
    back = [back_ref[c].astype(F32) for c in range(Z)]
    each = Z // OWN
    state, rows = [], []
    for i in range(OWN):
        mine = back[i * each : (i + 1) * each]
        state.append(jnp.concatenate([part[:PART] for part in mine], axis=0))
        for half in range(2):
            first = PART * (1 + half)
            o = jnp.concatenate([part[first : first + PART] for part in mine], axis=0).T
            scale = lax.rsqrt(jnp.mean(o * o, axis=1, keepdims=True) + 1e-6)
            rows.append((o * scale * gain[:, i * HD : (i + 1) * HD]).astype(BF16))
    for x in range(X):
        out_ref[x] = jnp.concatenate([part.astype(BF16) for part in state] + rows, axis=0)
        if x < X - 1:
            part = msg_ref[x].astype(F32)
            for i in range(OWN):
                factor = jnp.exp(joined_log(part, AT_LOGS + 4 * i))
                state[i] = factor * state[i] + part[i * HD : (i + 1) * HD]


def attention_kernel(q_ref, k_ref, v_ref, run_ref, state_ref, gain_ref, out_ref):
    running = run_ref[...]
    columns = running.T
    for pair in range(PAIRS):
        b, cols = pair // HEADS, pl.ds(pair % HEADS * HD, HD)
        q, column = q_ref[b, :, cols], columns[:, pair : pair + 1]
        state = state_ref[pair // OWN, pair % OWN * HD : (pair % OWN + 1) * HD]
        weights = fading_scores(q, k_ref[b, :, cols], column, running[pair : pair + 1])
        decayed = (q.astype(F32) * jnp.exp(column)).astype(BF16)
        o = jnp.dot(
            weights, v_ref[b, :, cols], preferred_element_type=F32
        ) + lax.dot_general(
            decayed, state, (((1,), (1,)), ((), ())), preferred_element_type=F32
        )
        scale = lax.rsqrt(jnp.mean(o * o, axis=1, keepdims=True) + 1e-6)
        out_ref[b, :, cols] = (o * scale * gain_ref[:, cols]).astype(BF16)


def slot_rows(facts_ref, half):
    facts = facts_ref[:, half * 2 * HD : (half + 1) * 2 * HD]
    lane = lax.broadcasted_iota(jnp.int32, (1, 2 * HD), 1)
    place = lane % HD // CAP * CAP
    rows = []
    for j in range(2):
        code = facts[4 + j : 5 + j].astype(jnp.int32)
        rows.append(code // CAP * HD + code % CAP + place)
    return rows, [facts[6:7], facts[7:8]]


def dispatch_kernel(rows_ref, facts_ref, out_ref):
    index = lax.broadcasted_iota(jnp.int32, (EXPERTS * HD, 2 * HD), 0)
    for half in range(2):
        (first, second), _ = slot_rows(facts_ref, half)
        chosen = jnp.where((index == first) | (index == second), 1.0, 0.0).astype(BF16)
        tokens = pl.ds(half * HD, HD)
        rows = jnp.concatenate(
            [
                jnp.concatenate(
                    [
                        rows_ref[2 * b + h // OWN, pl.ds((OWN + h % OWN * 2 + half) * HD, HD)]
                        for h in range(HEADS)
                    ],
                    axis=1,
                )
                for b in range(2)
            ],
            axis=0,
        )
        sent = jnp.dot(chosen, rows, preferred_element_type=F32).astype(BF16)
        for e in range(EXPERTS):
            out_ref[e, tokens] = sent[e * HD : (e + 1) * HD]


def expert_kernel(rows_ref, gate_ref, up_ref, down_ref, out_ref):
    total = None
    for j in range(EXPERTS):
        part = pl.ds(j * COLS, COLS)
        both = jnp.concatenate([gate_ref[part, :], up_ref[part, :]], axis=1)
        term = jnp.dot(rows_ref[j], both, preferred_element_type=F32)
        total = term if total is None else total + term
    width = gate_ref.shape[1]
    gate, up = total[:, :width], total[:, width:]
    hidden = (gate / (1.0 + jnp.exp(-gate)) * up).astype(BF16)
    for j in range(EXPERTS):
        out_ref[j] = jnp.dot(
            hidden, down_ref[:, pl.ds(j * COLS, COLS)], preferred_element_type=F32
        ).astype(BF16)


def combine_kernel(rows_ref, facts_ref, out_ref):
    index = lax.broadcasted_iota(jnp.int32, (EXPERTS * HD, 2 * HD), 0)
    for half in range(2):
        (first, second), gates = slot_rows(facts_ref, half)
        mix = jnp.where(index == first, gates[0], 0.0) + jnp.where(index == second, gates[1], 0.0)
        own = jnp.concatenate(
            [rows_ref[e, half * HD : (half + 1) * HD] for e in range(EXPERTS)], axis=0
        )
        total = lax.dot_general(
            mix.astype(BF16), own, (((0,), (0,)), ((), ())), preferred_element_type=F32
        )
        for k in range(16):
            one, two = total[k * 8 : (k + 1) * 8], total[HD + k * 8 : HD + (k + 1) * 8]
            row = lax.broadcasted_iota(jnp.int32, one.shape, 0)
            even = jnp.where(row < HALF, one, pltpu.roll(two, HALF, 0))
            odd = jnp.where(row < HALF, pltpu.roll(one, HALF, 0), two)
            z, x = half * 8 + k // 2, k % 2 * 2
            out_ref[x, z] = even.astype(BF16)
            out_ref[x + 1, z] = odd.astype(BF16)


def sum_kernel(parts_ref, out_ref):
    total = parts_ref[0].astype(F32)
    for i in range(1, parts_ref.shape[0]):
        total = total + parts_ref[i].astype(F32)
    out_ref[...] = total.astype(BF16)


def swap(array, axis):
    return lax.all_to_all(array, axis, 0, 0, tiled=True)


def body(
    queries, keys, values, log_decay, norm_gain, expert_ids, gate_weights, w_gate, w_up, w_down
):
    shape = jax.ShapeDtypeStruct
    decay = jnp.transpose(log_decay, (0, 2, 1)).reshape(PAIRS, TOK)
    gain = norm_gain.reshape(1, COLS)
    running, message = call(
        update_kernel,
        (shape((PAIRS, TOK), F32), shape((X, AT_FACTS + 8, HD), BF16)),
        "update",
        [pltpu.VMEM((8, HD), F32)],
    )(decay, queries, keys, values, expert_ids.T, gate_weights.T)
    message = swap(message, "x")
    groups = call(group_kernel, shape((Z, PART + 40, HD), BF16), "group")(message)
    groups = swap(groups, "z")
    back, facts = call(
        scan_kernel,
        (shape((Z, 3 * PART, HD), BF16), shape((8, 4 * HD), F32)),
        "scan",
    )(groups)
    back = swap(back, "z")
    back = call(expand_kernel, shape((X, 3 * OWN * HD, HD), BF16), "expand")(back, message, gain)
    rows = swap(back, "x")
    attn_out = call(attention_kernel, shape((2, TOK, COLS), BF16), "attention")(
        queries, keys, values, running, rows, gain
    )
    slots = call(dispatch_kernel, shape((EXPERTS, 2 * HD, COLS), BF16), "dispatch")(rows, facts)
    slots = swap(slots, ("y", "core"))
    slots = call(expert_kernel, shape((EXPERTS, 2 * HD, COLS), BF16), "experts")(
        slots, w_gate[0], w_up[0], w_down[0]
    )
    slots = swap(slots, ("y", "core"))
    share = call(combine_kernel, shape((X, Z, MROWS, COLS), BF16), "combine")(slots, facts)
    share = swap(share.reshape(X, GROUP, COLS), "x")
    share = call(sum_kernel, shape((GROUP, COLS), BF16), "sum_x")(share)
    share = swap(share.reshape(Z, MROWS, COLS), "z")
    moe_out = call(sum_kernel, shape((MROWS, COLS), BF16), "sum_z")(share)
    return (attn_out, moe_out)


def solution(mesh):
    fine = Mesh(mesh.devices.reshape(Z, X, Y, CORE), ("z", "x", "y", "core"))
    seq, expert = ("z", "x"), ("y", "core")
    placed = (
        P(None, seq, expert),
        P(None, seq, expert),
        P(None, seq, expert),
        P(None, seq, expert),
        P(expert),
        P(seq, None),
        P(seq, None),
        P(expert, None, seq),
        P(expert, None, seq),
        P(expert, seq, None),
    )
    return jax.shard_map(
        body,
        mesh=fine,
        in_specs=placed,
        out_specs=(P(None, seq, expert), P(seq, expert)),
        check_vma=False,
    )
```

```python
import jax
import jax.numpy as jnp
from jax import lax
from jax.experimental import pallas as pl
from jax.experimental.pallas import tpu as pltpu
from jax.sharding import Mesh
from jax.sharding import PartitionSpec as P

HD = 128
HEADS = 4
PAIRS = 8
TOK = 256
Z, X, Y, CORE = 16, 4, 4, 2
EXPERTS = Y * CORE
MROWS = 8
CAP = 4
COLS = HEADS * HD
OWN = PAIRS // X
PART = OWN * HD // Z
SLOTS = Z * CAP
HALF = MROWS // 2
FEW = 16
GROUP = Z * MROWS
AT_LOGS = OWN * HD
AT_Q = AT_LOGS + 8
AT_LOCAL = AT_Q + 8
AT_FACTS = AT_LOCAL + 16
AT_ROUTE = 64
AT_MINE = 96
F32 = jnp.float32
BF16 = jnp.bfloat16


def call(kernel, out, name, scratch=(), fetch=False):
    vmem = pl.BlockSpec(memory_space=pltpu.VMEM)
    specs = {"in_specs": [pl.BlockSpec(memory_space=pl.ANY)] * 6} if fetch else {}
    return pl.pallas_call(
        kernel,
        out_shape=out,
        out_specs=jax.tree.map(lambda _: vmem, out),
        scratch_shapes=scratch,
        compiler_params=pltpu.CompilerParams(vmem_limit_bytes=(60 if fetch else 40) * 2**20),
        name=name,
        **specs,
    )


def split_log(log):
    first = jnp.floor(log * 0.125) * 8.0
    rest = log - first
    second = jnp.floor(rest * 32.0) * (1.0 / 32.0)
    rest = rest - second
    third = jnp.floor(rest * 8192.0) * (1.0 / 8192.0)
    return first, second, third, rest - third


def stacked_rows(rows):
    index = lax.broadcasted_iota(jnp.int32, (8, HD), 0)
    total = jnp.zeros((8, HD), F32)
    for i, row in enumerate(rows):
        total = jnp.where(index == i, jnp.broadcast_to(row, (8, HD)), total)
    return total


def joined_log(rows, first):
    return (rows[first : first + 1] + rows[first + 1 : first + 2]) + (
        rows[first + 2 : first + 3] + rows[first + 3 : first + 4]
    )


def prefix_sums(rows):
    lane = lax.broadcasted_iota(jnp.int32, rows.shape, 1)
    shift = 1
    while shift < TOK:
        rows = rows + jnp.where(lane >= shift, pltpu.roll(rows, shift, 1), 0.0)
        shift *= 2
    return rows


def fading_scores(q, k, column, row):
    scores = lax.dot_general(q, k, (((1,), (1,)), ((), ())), preferred_element_type=F32)
    causal = lax.broadcasted_iota(jnp.int32, scores.shape, 0) >= lax.broadcasted_iota(
        jnp.int32, scores.shape, 1
    )
    fading = jnp.exp(jnp.minimum(column - row, 0.0))
    return jnp.where(causal, scores * fading, 0.0).astype(BF16)


def beside(one, two):
    row = lax.broadcasted_iota(jnp.int32, one.shape, 0)
    return jnp.where(row < HALF, one, pltpu.roll(two, HALF, 0))


def two_parts(array):
    coarse = array.astype(BF16).astype(F32)
    return coarse, array - coarse


def route_facts(ids_ref, gates_ref, facts_ref):
    facts_ref[...] = jnp.zeros((8, HD), F32)
    facts_ref[0:2, 0:MROWS] = ids_ref[...].astype(F32)
    facts_ref[6:8, 0:MROWS] = gates_ref[...]
    names = facts_ref[0:2, :]
    lane = lax.broadcasted_iota(jnp.int32, (2, HD), 1)
    choice = lax.broadcasted_iota(jnp.int32, (2, HD), 0)
    slots = jnp.where((choice == 1) & (names[0:1] == names[1:2]), 1.0, 0.0)
    for t in range(MROWS - 1):
        for c in range(2):
            same = (names[c : c + 1, t : t + 1] == names) & (lane > t)
            slots = slots + jnp.where(same, 1.0, 0.0)
    facts_ref[4:6, :] = jnp.where(lane < MROWS, names * float(CAP) + slots, 0.0)
    facts_ref[0:2, :] = jnp.zeros((2, HD), F32)


def update_kernel(*refs):
    sources, (run_ref, msg_ref), fetched = refs[:6], refs[6:8], refs[8:14]
    facts_ref, semaphores = refs[14:]
    copies = []
    for i, (source, target) in enumerate(zip(sources, fetched)):
        part = source.at[:, pl.ds(0, FEW)] if i == 1 else source
        copies.append(pltpu.make_async_copy(part, target, semaphores.at[i]))
    for copy in copies:
        copy.start()
    for copy in copies:
        copy.wait()
    decay_ref, q_ref, k_ref, v_ref, ids_ref, gates_ref = fetched
    running = prefix_sums(jnp.concatenate([decay_ref[0], decay_ref[1]], axis=0))
    run_ref[...] = running
    end = running[:, TOK - 1 :]
    to_end = jnp.exp(end - running).T
    columns = running.T[:FEW]
    route_facts(ids_ref, gates_ref, facts_ref)
    for owner in range(X):
        parts, logs, qs, locals_ = [], [], [], []
        for i in range(OWN):
            pair = owner * OWN + i
            b, cols = pair // HEADS, pl.ds(pair % HEADS * HD, HD)
            decayed = (k_ref[b, :, cols].astype(F32) * to_end[:, pair : pair + 1]).astype(BF16)
            parts.append(
                lax.dot_general(
                    v_ref[b, :, cols], decayed, (((0,), (0,)), ((), ())), preferred_element_type=F32
                )
            )
            logs += [jnp.broadcast_to(p, (1, HD)) for p in split_log(end[pair : pair + 1])]
            q, column = q_ref[b, :FEW, cols], columns[:, pair : pair + 1]
            weights = fading_scores(
                q, k_ref[b, :FEW, cols], column, running[pair : pair + 1, :FEW]
            )
            local = jnp.dot(weights, v_ref[b, :FEW, cols], preferred_element_type=F32)
            locals_.append(local[:8])
            qs.append((q.astype(F32) * jnp.exp(column))[:8])
        local = two_parts(beside(*locals_))
        msg_ref[owner] = jnp.concatenate(
            parts + [stacked_rows(logs), beside(*qs), local[0], local[1], facts_ref[...]], axis=0
        ).astype(BF16)


def placed(rows, i, x):
    row = lax.broadcasted_iota(jnp.int32, rows.shape, 0)
    moved = rows if i == x % 2 else pltpu.roll(rows, HALF, 0)
    moved = jnp.where(row // HALF == x % 2, moved, 0.0)
    zero = jnp.zeros_like(moved)
    return jnp.concatenate([moved, zero] if x < 2 else [zero, moved], axis=0)


def tall(rows):
    return jnp.concatenate([rows, jnp.zeros((HD - rows.shape[0], HD), F32)], axis=0)


def group_kernel(msg_ref, out_ref):
    lane = lax.broadcasted_iota(jnp.int32, (8, HD), 1)
    facts = jnp.zeros((8, HD), F32)
    for x in range(X):
        own = msg_ref[x].astype(F32)[AT_FACTS:]
        for b in range(2):
            only = jnp.where(lane // HALF == b, own, 0.0)
            shift = b * 16 + x * HALF - b * HALF
            facts = facts + pltpu.roll(only, AT_ROUTE + shift, 1)
        mine = jnp.where((lane < MROWS) & (lax.axis_index("x") == x), own, 0.0)
        facts = facts + pltpu.roll(mine, AT_MINE, 1)
    for i in range(OWN):
        total, log, queries, near, inner = None, None, 0.0, 0.0, 0.0
        for x in range(X):
            part = msg_ref[x].astype(F32)
            update = part[i * HD : (i + 1) * HD]
            own_log = joined_log(part, AT_LOGS + 4 * i)
            q = placed(part[AT_Q : AT_Q + 8], i, x)
            local = part[AT_LOCAL : AT_LOCAL + 8] + part[AT_LOCAL + 8 : AT_LOCAL + 16]
            near = near + placed(local, i, x)
            if x == 0:
                queries = q
                total, log = update, own_log
            else:
                inner = inner + lax.dot_general(
                    total.astype(BF16),
                    tall(q).astype(BF16),
                    (((1,), (1,)), ((), ())),
                    preferred_element_type=F32,
                )
                queries = queries + q * jnp.exp(log)
                total, log = jnp.exp(own_log) * total + update, log + own_log
        coarse, rest = two_parts(inner + tall(near).T)
        rows = coarse + pltpu.roll(rest, 16, 1)
        info = jnp.where(lane < AT_ROUTE, 0.0, stacked_rows(split_log(log)) + facts)
        for g in range(HD // PART):
            at = g * PART
            near = rows[at : at + 8] + pltpu.roll(rows[at + 8 : at + PART], 32, 1)
            out_ref[i * (HD // PART) + g] = jnp.concatenate(
                [total[at : at + PART], info + near, queries], axis=0
            ).astype(BF16)


def scan_kernel(msg_ref, out_ref, facts_ref):
    state = jnp.zeros((PART, HD), F32)
    lane = lax.broadcasted_iota(jnp.int32, (16, HD), 1)
    states, queries = [], []
    near = [jnp.zeros((PART, HD), F32) for _ in range(2)]
    facts = [jnp.zeros((8, HD), F32) for _ in range(5)]
    for z in range(Z):
        states.append(state)
        part = msg_ref[z].astype(F32)
        info = part[16:24]
        queries.append(part[24:40])
        half, shift = z // 8, z % 8 * 16
        rows = jnp.concatenate([info, pltpu.roll(info, HD - 32, 1)], axis=0)
        rows = jnp.where(lane < 16, rows + pltpu.roll(rows, HD - 16, 1), 0.0)
        near[half] = near[half] + (pltpu.roll(rows, shift, 1) if shift else rows)
        for b in range(2):
            only = jnp.where(lane[:8] // 16 == AT_ROUTE // 16 + b, info, 0.0)
            move = (shift - AT_ROUTE - b * 16) % HD
            place = half * 2 + b
            facts[place] = facts[place] + (pltpu.roll(only, move, 1) if move else only)
        only = jnp.where(lane[:8] // MROWS == AT_MINE // MROWS, info, 0.0)
        move = (z * MROWS - AT_MINE) % HD
        facts[4] = facts[4] + (pltpu.roll(only, move, 1) if move else only)
        factor = jnp.exp(joined_log(part, PART))[:, AT_ROUTE : AT_ROUTE + 1]
        state = factor * state + part[:PART]
    far = lax.dot_general(
        jnp.concatenate(states, axis=0).astype(BF16),
        jnp.concatenate(queries, axis=0).astype(BF16),
        (((1,), (1,)), ((), ())),
        preferred_element_type=F32,
    )
    row = lax.broadcasted_iota(jnp.int32, far.shape, 0)
    column = lax.broadcasted_iota(jnp.int32, far.shape, 1)
    far = jnp.where(row // 16 == column // 16, far, 0.0)
    total = jnp.concatenate(near, axis=1)
    for z in range(Z):
        total = total + far[z * PART : (z + 1) * PART]
    for z in range(Z):
        out_ref[z] = jnp.concatenate(
            [states[z], total[:, :HD], total[:, HD:]], axis=0
        ).astype(BF16)
    facts_ref[...] = jnp.concatenate(facts, axis=1)


def expand_kernel(back_ref, msg_ref, gain_ref, out_ref):
    odd = lax.rem(lax.axis_index("x"), 2)
    gain = jnp.where(odd == 1, gain_ref[:, OWN * HD :], gain_ref[:, : OWN * HD])
    back = [back_ref[c].astype(F32) for c in range(Z)]
    each = Z // OWN
    state, rows = [], []
    for i in range(OWN):
        mine = back[i * each : (i + 1) * each]
        state.append(jnp.concatenate([part[:PART] for part in mine], axis=0))
        for half in range(2):
            first = PART * (1 + half)
            o = jnp.concatenate([part[first : first + PART] for part in mine], axis=0).T
            scale = lax.rsqrt(jnp.mean(o * o, axis=1, keepdims=True) + 1e-6)
            rows.append((o * scale * gain[:, i * HD : (i + 1) * HD]).astype(BF16))
    for x in range(X):
        out_ref[x] = jnp.concatenate([part.astype(BF16) for part in state] + rows, axis=0)
        if x < X - 1:
            part = msg_ref[x].astype(F32)
            for i in range(OWN):
                factor = jnp.exp(joined_log(part, AT_LOGS + 4 * i))
                state[i] = factor * state[i] + part[i * HD : (i + 1) * HD]


def attention_kernel(q_ref, k_ref, v_ref, run_ref, state_ref, gain_ref, out_ref):
    running = run_ref[...]
    columns = running.T
    for pair in range(PAIRS):
        b, cols = pair // HEADS, pl.ds(pair % HEADS * HD, HD)
        q, column = q_ref[b, :, cols], columns[:, pair : pair + 1]
        state = state_ref[pair // OWN, pair % OWN * HD : (pair % OWN + 1) * HD]
        weights = fading_scores(q, k_ref[b, :, cols], column, running[pair : pair + 1])
        decayed = (q.astype(F32) * jnp.exp(column)).astype(BF16)
        o = jnp.dot(
            weights, v_ref[b, :, cols], preferred_element_type=F32
        ) + lax.dot_general(
            decayed, state, (((1,), (1,)), ((), ())), preferred_element_type=F32
        )
        scale = lax.rsqrt(jnp.mean(o * o, axis=1, keepdims=True) + 1e-6)
        out_ref[b, :, cols] = (o * scale * gain_ref[:, cols]).astype(BF16)


def slot_rows(facts, place, slots):
    rows = []
    for j in range(2):
        code = facts[4 + j : 5 + j].astype(jnp.int32)
        rows.append(code // CAP * slots + code % CAP + place)
    return rows, [facts[6:7], facts[7:8]]


def dispatch_kernel(rows_ref, facts_ref, out_ref):
    index = lax.broadcasted_iota(jnp.int32, (EXPERTS * HD, 2 * HD), 0)
    lane = lax.broadcasted_iota(jnp.int32, (1, 2 * HD), 1)
    place = lane // HALF % X * 32 + lane % HD // 16 * CAP
    for half in range(2):
        (first, second), _ = slot_rows(
            facts_ref[:, half * 2 * HD : (half + 1) * 2 * HD], place, HD
        )
        chosen = jnp.where((index == first) | (index == second), 1.0, 0.0).astype(BF16)
        tokens = pl.ds(half * HD, HD)
        rows = jnp.concatenate(
            [
                jnp.concatenate(
                    [
                        rows_ref[2 * b + h // OWN, pl.ds((OWN + h % OWN * 2 + half) * HD, HD)]
                        for h in range(HEADS)
                    ],
                    axis=1,
                )
                for b in range(2)
            ],
            axis=0,
        )
        sent = jnp.dot(chosen, rows, preferred_element_type=F32).astype(BF16)
        for e in range(EXPERTS):
            for x in range(X):
                at = e * HD + x * 32
                out_ref[e, pl.ds(x * SLOTS + half * 32, 32)] = sent[at : at + 32]


def expert_kernel(rows_ref, gate_ref, up_ref, down_ref, out_ref):
    total = None
    for j in range(EXPERTS):
        part = pl.ds(j * COLS, COLS)
        both = jnp.concatenate([gate_ref[part, :], up_ref[part, :]], axis=1)
        term = jnp.dot(rows_ref[j], both, preferred_element_type=F32)
        total = term if total is None else total + term
    width = gate_ref.shape[1]
    gate, up = total[:, :width], total[:, width:]
    hidden = (gate / (1.0 + jnp.exp(-gate)) * up).astype(BF16)
    for j in range(EXPERTS):
        out = jnp.dot(hidden, down_ref[:, pl.ds(j * COLS, COLS)], preferred_element_type=F32)
        for x in range(X):
            out_ref[x * EXPERTS + j] = out[x * SLOTS : (x + 1) * SLOTS].astype(BF16)


def combine_kernel(parts_ref, facts_ref, out_ref):
    index = lax.broadcasted_iota(jnp.int32, (EXPERTS * SLOTS, GROUP), 0)
    place = lax.broadcasted_iota(jnp.int32, (1, GROUP), 1) // MROWS * CAP
    (first, second), gates = slot_rows(facts_ref[:, 4 * HD :], place, SLOTS)
    mix = jnp.where(index == first, gates[0], 0.0) + jnp.where(index == second, gates[1], 0.0)
    rows = []
    for e in range(EXPERTS):
        total = parts_ref[e].astype(F32)
        for x in range(1, X):
            total = total + parts_ref[x * EXPERTS + e].astype(F32)
        rows.append(total.astype(BF16))
    out_ref[...] = lax.dot_general(
        mix.astype(BF16),
        jnp.concatenate(rows, axis=0),
        (((0,), (0,)), ((), ())),
        preferred_element_type=F32,
    ).astype(BF16)


def sum_kernel(parts_ref, out_ref):
    total = parts_ref[0].astype(F32)
    for i in range(1, parts_ref.shape[0]):
        total = total + parts_ref[i].astype(F32)
    out_ref[...] = total.astype(BF16)


def swap(array, axis):
    return lax.all_to_all(array, axis, 0, 0, tiled=True)


def body(
    queries, keys, values, log_decay, norm_gain, expert_ids, gate_weights, w_gate, w_up, w_down
):
    shape = jax.ShapeDtypeStruct
    decay = jnp.transpose(log_decay, (0, 2, 1))
    gain = norm_gain.reshape(1, COLS)
    running, message = call(
        update_kernel,
        (shape((PAIRS, TOK), F32), shape((X, AT_FACTS + 8, HD), BF16)),
        "update",
        [
            pltpu.VMEM((2, HEADS, TOK), F32),
            pltpu.VMEM((2, FEW, COLS), BF16),
            pltpu.VMEM((2, TOK, COLS), BF16),
            pltpu.VMEM((2, TOK, COLS), BF16),
            pltpu.VMEM((2, MROWS), jnp.int32),
            pltpu.VMEM((2, MROWS), F32),
            pltpu.VMEM((8, HD), F32),
            pltpu.SemaphoreType.DMA((6,)),
        ],
        True,
    )(decay, queries, keys, values, expert_ids.T, gate_weights.T)
    message = swap(message, "x")
    groups = call(group_kernel, shape((Z, PART + 24, HD), BF16), "group")(message)
    groups = swap(groups, "z")
    back, facts = call(
        scan_kernel,
        (shape((Z, 3 * PART, HD), BF16), shape((8, 5 * HD), F32)),
        "scan",
    )(groups)
    back = swap(back, "z")
    back = call(expand_kernel, shape((X, 3 * OWN * HD, HD), BF16), "expand")(back, message, gain)
    rows = swap(back, "x")
    attn_out = call(attention_kernel, shape((2, TOK, COLS), BF16), "attention")(
        queries, keys, values, running, rows, gain
    )
    slots = call(dispatch_kernel, shape((EXPERTS, 2 * HD, COLS), BF16), "dispatch")(rows, facts)
    slots = swap(slots, ("y", "core"))
    parts = call(expert_kernel, shape((X * EXPERTS, SLOTS, COLS), BF16), "experts")(
        slots, w_gate[0], w_up[0], w_down[0]
    )
    parts = swap(parts, ("x", "y", "core"))
    share = call(combine_kernel, shape((GROUP, COLS), BF16), "combine")(parts, facts)
    share = swap(share.reshape(Z, MROWS, COLS), "z")
    moe_out = call(sum_kernel, shape((MROWS, COLS), BF16), "sum_z")(share)
    return (attn_out, moe_out)


def solution(mesh):
    fine = Mesh(mesh.devices.reshape(Z, X, Y, CORE), ("z", "x", "y", "core"))
    seq, expert = ("z", "x"), ("y", "core")
    placed = (
        P(None, seq, expert),
        P(None, seq, expert),
        P(None, seq, expert),
        P(None, seq, expert),
        P(expert),
        P(seq, None),
        P(seq, None),
        P(expert, None, seq),
        P(expert, None, seq),
        P(expert, seq, None),
    )
    return jax.shard_map(
        body,
        mesh=fine,
        in_specs=placed,
        out_specs=(P(None, seq, expert), P(seq, expert)),
        check_vma=False,
    )
```

```python
import jax
import jax.numpy as jnp
from jax import lax
from jax.experimental import pallas as pl
from jax.experimental.pallas import tpu as pltpu
from jax.sharding import Mesh
from jax.sharding import PartitionSpec as P

HD = 128
HEADS = 4
PAIRS = 8
TOK = 256
Z, X, Y, CORE = 16, 4, 4, 2
EXPERTS = Y * CORE
MROWS = 8
CAP = 4
COLS = HEADS * HD
OWN = PAIRS // X
PART = OWN * HD // Z
SLOTS = Z * CAP
HALF = MROWS // 2
FEW = 16
GROUP = Z * MROWS
AT_LOGS = OWN * HD
AT_Q = AT_LOGS + 8
AT_LOCAL = AT_Q + 8
AT_FACTS = AT_LOCAL + 16
AT_ROUTE = 64
AT_MINE = 96
F32 = jnp.float32
BF16 = jnp.bfloat16


def call(kernel, out, name, scratch=(), fetch=False):
    vmem = pl.BlockSpec(memory_space=pltpu.VMEM)
    specs = {"in_specs": [pl.BlockSpec(memory_space=pl.ANY)] * 6} if fetch else {}
    return pl.pallas_call(
        kernel,
        out_shape=out,
        out_specs=jax.tree.map(lambda _: vmem, out),
        scratch_shapes=scratch,
        compiler_params=pltpu.CompilerParams(vmem_limit_bytes=(60 if fetch else 40) * 2**20),
        name=name,
        **specs,
    )


def split_log(log):
    first = jnp.floor(log * 0.125) * 8.0
    rest = log - first
    second = jnp.floor(rest * 32.0) * (1.0 / 32.0)
    rest = rest - second
    third = jnp.floor(rest * 8192.0) * (1.0 / 8192.0)
    return first, second, third, rest - third


def stacked_rows(rows):
    index = lax.broadcasted_iota(jnp.int32, (8, HD), 0)
    total = jnp.zeros((8, HD), F32)
    for i, row in enumerate(rows):
        total = jnp.where(index == i, jnp.broadcast_to(row, (8, HD)), total)
    return total


def joined_log(rows, first):
    return (rows[first : first + 1] + rows[first + 1 : first + 2]) + (
        rows[first + 2 : first + 3] + rows[first + 3 : first + 4]
    )


def prefix_sums(rows):
    lane = lax.broadcasted_iota(jnp.int32, rows.shape, 1)
    shift = 1
    while shift < TOK:
        rows = rows + jnp.where(lane >= shift, pltpu.roll(rows, shift, 1), 0.0)
        shift *= 2
    return rows


def fading_scores(q, k, column, row):
    scores = lax.dot_general(q, k, (((1,), (1,)), ((), ())), preferred_element_type=F32)
    causal = lax.broadcasted_iota(jnp.int32, scores.shape, 0) >= lax.broadcasted_iota(
        jnp.int32, scores.shape, 1
    )
    fading = jnp.exp(jnp.minimum(column - row, 0.0))
    return jnp.where(causal, scores * fading, 0.0).astype(BF16)


def beside(one, two):
    row = lax.broadcasted_iota(jnp.int32, one.shape, 0)
    return jnp.where(row < HALF, one, pltpu.roll(two, HALF, 0))


def two_parts(array):
    coarse = array.astype(BF16).astype(F32)
    return coarse, array - coarse


def route_facts(ids_ref, gates_ref, facts_ref):
    facts_ref[...] = jnp.zeros((8, HD), F32)
    facts_ref[0:2, 0:MROWS] = ids_ref[...].astype(F32)
    facts_ref[6:8, 0:MROWS] = gates_ref[...]
    names = facts_ref[0:2, :]
    lane = lax.broadcasted_iota(jnp.int32, (2, HD), 1)
    choice = lax.broadcasted_iota(jnp.int32, (2, HD), 0)
    slots = jnp.where((choice == 1) & (names[0:1] == names[1:2]), 1.0, 0.0)
    for t in range(MROWS - 1):
        for c in range(2):
            same = (names[c : c + 1, t : t + 1] == names) & (lane > t)
            slots = slots + jnp.where(same, 1.0, 0.0)
    facts_ref[4:6, :] = jnp.where(lane < MROWS, names * float(CAP) + slots, 0.0)
    facts_ref[0:2, :] = jnp.zeros((2, HD), F32)


def update_kernel(*refs):
    sources, (run_ref, msg_ref), fetched = refs[:6], refs[6:8], refs[8:14]
    facts_ref, semaphores = refs[14:]
    copies = []
    for i, (source, target) in enumerate(zip(sources, fetched)):
        part = source.at[:, pl.ds(0, FEW)] if i == 1 else source
        copies.append(pltpu.make_async_copy(part, target, semaphores.at[i]))
    for copy in copies:
        copy.start()
    for copy in copies:
        copy.wait()
    decay_ref, q_ref, k_ref, v_ref, ids_ref, gates_ref = fetched
    running = prefix_sums(jnp.concatenate([decay_ref[0], decay_ref[1]], axis=0))
    run_ref[...] = running
    end = running[:, TOK - 1 :]
    to_end = jnp.exp(end - running).T
    columns = running.T[:FEW]
    route_facts(ids_ref, gates_ref, facts_ref)
    for owner in range(X):
        parts, logs, qs, locals_ = [], [], [], []
        for i in range(OWN):
            b, pair, cols = i, i * HEADS + owner, pl.ds(owner * HD, HD)
            decayed = (k_ref[b, :, cols].astype(F32) * to_end[:, pair : pair + 1]).astype(BF16)
            parts.append(
                lax.dot_general(
                    v_ref[b, :, cols], decayed, (((0,), (0,)), ((), ())), preferred_element_type=F32
                )
            )
            logs += [jnp.broadcast_to(p, (1, HD)) for p in split_log(end[pair : pair + 1])]
            q, column = q_ref[b, :FEW, cols], columns[:, pair : pair + 1]
            weights = fading_scores(
                q, k_ref[b, :FEW, cols], column, running[pair : pair + 1, :FEW]
            )
            local = jnp.dot(weights, v_ref[b, :FEW, cols], preferred_element_type=F32)
            locals_.append(local[:8])
            qs.append((q.astype(F32) * jnp.exp(column))[:8])
        local = two_parts(beside(*locals_))
        msg_ref[owner] = jnp.concatenate(
            parts + [stacked_rows(logs), beside(*qs), local[0], local[1], facts_ref[...]], axis=0
        ).astype(BF16)


def placed(rows, i, x):
    row = lax.broadcasted_iota(jnp.int32, rows.shape, 0)
    moved = rows if i == x % 2 else pltpu.roll(rows, HALF, 0)
    moved = jnp.where(row // HALF == x % 2, moved, 0.0)
    zero = jnp.zeros_like(moved)
    return jnp.concatenate([moved, zero] if x < 2 else [zero, moved], axis=0)


def tall(rows):
    return jnp.concatenate([rows, jnp.zeros((HD - rows.shape[0], HD), F32)], axis=0)


def group_kernel(msg_ref, out_ref):
    lane = lax.broadcasted_iota(jnp.int32, (8, HD), 1)
    facts = jnp.zeros((8, HD), F32)
    for x in range(X):
        own = msg_ref[x].astype(F32)[AT_FACTS:]
        for b in range(2):
            only = jnp.where(lane // HALF == b, own, 0.0)
            shift = b * 16 + x * HALF - b * HALF
            facts = facts + pltpu.roll(only, AT_ROUTE + shift, 1)
        mine = jnp.where((lane < MROWS) & (lax.axis_index("x") == x), own, 0.0)
        facts = facts + pltpu.roll(mine, AT_MINE, 1)
    for i in range(OWN):
        total, log, queries, near, inner = None, None, 0.0, 0.0, 0.0
        for x in range(X):
            part = msg_ref[x].astype(F32)
            update = part[i * HD : (i + 1) * HD]
            own_log = joined_log(part, AT_LOGS + 4 * i)
            q = placed(part[AT_Q : AT_Q + 8], i, x)
            local = part[AT_LOCAL : AT_LOCAL + 8] + part[AT_LOCAL + 8 : AT_LOCAL + 16]
            near = near + placed(local, i, x)
            if x == 0:
                queries = q
                total, log = update, own_log
            else:
                inner = inner + lax.dot_general(
                    total.astype(BF16),
                    tall(q).astype(BF16),
                    (((1,), (1,)), ((), ())),
                    preferred_element_type=F32,
                )
                queries = queries + q * jnp.exp(log)
                total, log = jnp.exp(own_log) * total + update, log + own_log
        coarse, rest = two_parts(inner + tall(near).T)
        rows = coarse + pltpu.roll(rest, 16, 1)
        info = jnp.where(lane < AT_ROUTE, 0.0, stacked_rows(split_log(log)) + facts)
        for g in range(HD // PART):
            at = g * PART
            near = rows[at : at + 8] + pltpu.roll(rows[at + 8 : at + PART], 32, 1)
            out_ref[i * (HD // PART) + g] = jnp.concatenate(
                [total[at : at + PART], info + near, queries], axis=0
            ).astype(BF16)


def scan_kernel(msg_ref, out_ref, facts_ref):
    state = jnp.zeros((PART, HD), F32)
    lane = lax.broadcasted_iota(jnp.int32, (16, HD), 1)
    states, queries = [], []
    near = [jnp.zeros((PART, HD), F32) for _ in range(2)]
    facts = [jnp.zeros((8, HD), F32) for _ in range(5)]
    for z in range(Z):
        states.append(state)
        part = msg_ref[z].astype(F32)
        info = part[16:24]
        queries.append(part[24:40])
        half, shift = z // 8, z % 8 * 16
        rows = jnp.concatenate([info, pltpu.roll(info, HD - 32, 1)], axis=0)
        rows = jnp.where(lane < 16, rows + pltpu.roll(rows, HD - 16, 1), 0.0)
        near[half] = near[half] + (pltpu.roll(rows, shift, 1) if shift else rows)
        for b in range(2):
            only = jnp.where(lane[:8] // 16 == AT_ROUTE // 16 + b, info, 0.0)
            move = (shift - AT_ROUTE - b * 16) % HD
            place = half * 2 + b
            facts[place] = facts[place] + (pltpu.roll(only, move, 1) if move else only)
        only = jnp.where(lane[:8] // MROWS == AT_MINE // MROWS, info, 0.0)
        move = (z * MROWS - AT_MINE) % HD
        facts[4] = facts[4] + (pltpu.roll(only, move, 1) if move else only)
        factor = jnp.exp(joined_log(part, PART))[:, AT_ROUTE : AT_ROUTE + 1]
        state = factor * state + part[:PART]
    far = lax.dot_general(
        jnp.concatenate(states, axis=0).astype(BF16),
        jnp.concatenate(queries, axis=0).astype(BF16),
        (((1,), (1,)), ((), ())),
        preferred_element_type=F32,
    )
    row = lax.broadcasted_iota(jnp.int32, far.shape, 0)
    column = lax.broadcasted_iota(jnp.int32, far.shape, 1)
    far = jnp.where(row // 16 == column // 16, far, 0.0)
    total = jnp.concatenate(near, axis=1)
    for z in range(Z):
        total = total + far[z * PART : (z + 1) * PART]
    for z in range(Z):
        out_ref[z] = jnp.concatenate(
            [states[z], total[:, :HD], total[:, HD:]], axis=0
        ).astype(BF16)
    facts_ref[...] = jnp.concatenate(facts, axis=1)


def expand_kernel(back_ref, msg_ref, gain_ref, facts_ref, state_ref, slots_ref):
    gain = gain_ref[:, :HD]
    for x in range(1, X):
        gain = jnp.where(lax.axis_index("x") == x, gain_ref[:, x * HD : (x + 1) * HD], gain)
    back = [back_ref[c].astype(F32) for c in range(Z)]
    each = Z // OWN
    state, rows = [], []
    for i in range(OWN):
        mine = back[i * each : (i + 1) * each]
        state.append(jnp.concatenate([part[:PART] for part in mine], axis=0))
        for half in range(2):
            first = PART * (1 + half)
            o = jnp.concatenate([part[first : first + PART] for part in mine], axis=0).T
            scale = lax.rsqrt(jnp.mean(o * o, axis=1, keepdims=True) + 1e-6)
            rows.append((o * scale * gain).astype(BF16))
    index = lax.broadcasted_iota(jnp.int32, (EXPERTS * HD, 2 * HD), 0)
    lane = lax.broadcasted_iota(jnp.int32, (1, 2 * HD), 1)
    place = lane // HALF % X * 32 + lane % HD // 16 * CAP
    for half in range(2):
        (first, second), _ = slot_rows(
            facts_ref[:, half * 2 * HD : (half + 1) * 2 * HD], place, HD
        )
        chosen = jnp.where((index == first) | (index == second), 1.0, 0.0).astype(BF16)
        both = jnp.concatenate([rows[half], rows[2 + half]], axis=0)
        sent = jnp.dot(chosen, both, preferred_element_type=F32).astype(BF16)
        for e in range(EXPERTS):
            for x in range(X):
                at = e * HD + x * 32
                for target in range(X):
                    slots_ref[target * EXPERTS + e, pl.ds(x * SLOTS + half * 32, 32)] = sent[
                        at : at + 32
                    ]
    for x in range(X):
        state_ref[x] = jnp.concatenate(state, axis=0).astype(BF16)
        if x < X - 1:
            part = msg_ref[x].astype(F32)
            for i in range(OWN):
                factor = jnp.exp(joined_log(part, AT_LOGS + 4 * i))
                state[i] = factor * state[i] + part[i * HD : (i + 1) * HD]


def attention_kernel(q_ref, k_ref, v_ref, run_ref, state_ref, gain_ref, out_ref):
    here = lax.axis_index("x")
    running = run_ref[...]
    columns = running.T
    for pair in range(PAIRS):
        b, cols = pair // HEADS, pl.ds(pair % HEADS * HD, HD)
        q, column = q_ref[b, :, cols], columns[:, pair : pair + 1]
        state = state_ref[pair % HEADS, here, b * HD : (b + 1) * HD]
        weights = fading_scores(q, k_ref[b, :, cols], column, running[pair : pair + 1])
        decayed = (q.astype(F32) * jnp.exp(column)).astype(BF16)
        o = jnp.dot(
            weights, v_ref[b, :, cols], preferred_element_type=F32
        ) + lax.dot_general(
            decayed, state, (((1,), (1,)), ((), ())), preferred_element_type=F32
        )
        scale = lax.rsqrt(jnp.mean(o * o, axis=1, keepdims=True) + 1e-6)
        out_ref[b, :, cols] = (o * scale * gain_ref[:, cols]).astype(BF16)


def slot_rows(facts, place, slots):
    rows = []
    for j in range(2):
        code = facts[4 + j : 5 + j].astype(jnp.int32)
        rows.append(code // CAP * slots + code % CAP + place)
    return rows, [facts[6:7], facts[7:8]]


def expert_kernel(rows_ref, gate_ref, up_ref, down_ref, out_ref):
    total = None
    for j in range(EXPERTS):
        part = pl.ds(j * COLS, COLS)
        both = jnp.concatenate([gate_ref[part, :], up_ref[part, :]], axis=1)
        rows = jnp.concatenate([rows_ref[x * EXPERTS + j] for x in range(X)], axis=1)
        term = jnp.dot(rows, both, preferred_element_type=F32)
        total = term if total is None else total + term
    width = gate_ref.shape[1]
    gate, up = total[:, :width], total[:, width:]
    hidden = (gate / (1.0 + jnp.exp(-gate)) * up).astype(BF16)
    for j in range(EXPERTS):
        out = jnp.dot(hidden, down_ref[:, pl.ds(j * COLS, COLS)], preferred_element_type=F32)
        for x in range(X):
            out_ref[x * EXPERTS + j] = out[x * SLOTS : (x + 1) * SLOTS].astype(BF16)


def combine_kernel(parts_ref, facts_ref, out_ref):
    index = lax.broadcasted_iota(jnp.int32, (EXPERTS * SLOTS, GROUP), 0)
    place = lax.broadcasted_iota(jnp.int32, (1, GROUP), 1) // MROWS * CAP
    (first, second), gates = slot_rows(facts_ref[:, 4 * HD :], place, SLOTS)
    mix = jnp.where(index == first, gates[0], 0.0) + jnp.where(index == second, gates[1], 0.0)
    rows = []
    for e in range(EXPERTS):
        total = parts_ref[e].astype(F32)
        for x in range(1, X):
            total = total + parts_ref[x * EXPERTS + e].astype(F32)
        rows.append(total.astype(BF16))
    out_ref[...] = lax.dot_general(
        mix.astype(BF16),
        jnp.concatenate(rows, axis=0),
        (((0,), (0,)), ((), ())),
        preferred_element_type=F32,
    ).astype(BF16)


def sum_kernel(parts_ref, out_ref):
    total = parts_ref[0].astype(F32)
    for i in range(1, parts_ref.shape[0]):
        total = total + parts_ref[i].astype(F32)
    out_ref[...] = total.astype(BF16)


def swap(array, axis):
    return lax.all_to_all(array, axis, 0, 0, tiled=True)


def body(
    queries, keys, values, log_decay, norm_gain, expert_ids, gate_weights, w_gate, w_up, w_down
):
    shape = jax.ShapeDtypeStruct
    decay = jnp.transpose(log_decay, (0, 2, 1))
    gain = norm_gain.reshape(1, COLS)
    running, message = call(
        update_kernel,
        (shape((PAIRS, TOK), F32), shape((X, AT_FACTS + 8, HD), BF16)),
        "update",
        [
            pltpu.VMEM((2, HEADS, TOK), F32),
            pltpu.VMEM((2, FEW, COLS), BF16),
            pltpu.VMEM((2, TOK, COLS), BF16),
            pltpu.VMEM((2, TOK, COLS), BF16),
            pltpu.VMEM((2, MROWS), jnp.int32),
            pltpu.VMEM((2, MROWS), F32),
            pltpu.VMEM((8, HD), F32),
            pltpu.SemaphoreType.DMA((6,)),
        ],
        True,
    )(decay, queries, keys, values, expert_ids.T, gate_weights.T)
    message = swap(message, "x")
    groups = call(group_kernel, shape((Z, PART + 24, HD), BF16), "group")(message)
    groups = swap(groups, "z")
    back, facts = call(
        scan_kernel,
        (shape((Z, 3 * PART, HD), BF16), shape((8, 5 * HD), F32)),
        "scan",
    )(groups)
    back = swap(back, "z")
    states, slots = call(
        expand_kernel,
        (shape((X, OWN * HD, HD), BF16), shape((X * EXPERTS, X * SLOTS, HD), BF16)),
        "expand",
    )(back, message, gain, facts)
    slots = swap(slots, ("x", "y", "core"))
    states = lax.all_gather(states, "x", axis=0)
    attn_out = call(attention_kernel, shape((2, TOK, COLS), BF16), "attention")(
        queries, keys, values, running, states, gain
    )
    parts = call(expert_kernel, shape((X * EXPERTS, SLOTS, COLS), BF16), "experts")(
        slots, w_gate[0], w_up[0], w_down[0]
    )
    parts = swap(parts, ("x", "y", "core"))
    share = call(combine_kernel, shape((GROUP, COLS), BF16), "combine")(parts, facts)
    share = swap(share.reshape(Z, MROWS, COLS), "z")
    moe_out = call(sum_kernel, shape((MROWS, COLS), BF16), "sum_z")(share)
    return (attn_out, moe_out)


def solution(mesh):
    fine = Mesh(mesh.devices.reshape(Z, X, Y, CORE), ("z", "x", "y", "core"))
    seq, expert = ("z", "x"), ("y", "core")
    placed = (
        P(None, seq, expert),
        P(None, seq, expert),
        P(None, seq, expert),
        P(None, seq, expert),
        P(expert),
        P(seq, None),
        P(seq, None),
        P(expert, None, seq),
        P(expert, None, seq),
        P(expert, seq, None),
    )
    return jax.shard_map(
        body,
        mesh=fine,
        in_specs=placed,
        out_specs=(P(None, seq, expert), P(seq, expert)),
        check_vma=False,
    )
```

```python
import jax
import jax.numpy as jnp
from jax import lax
from jax.experimental import pallas as pl
from jax.experimental.pallas import tpu as pltpu
from jax.sharding import Mesh
from jax.sharding import PartitionSpec as P

HD = 128
HEADS = 4
PAIRS = 8
TOK = 256
Z, X, Y, CORE = 16, 4, 4, 2
EXPERTS = Y * CORE
MROWS = 8
CAP = 4
COLS = HEADS * HD
OWN = PAIRS // X
PART = OWN * HD // Z
SLOTS = Z * CAP
HALF = MROWS // 2
FEW = 16
GROUP = Z * MROWS
AT_LOGS = OWN * HD
AT_Q = AT_LOGS + 8
AT_LOCAL = AT_Q + 8
AT_FACTS = AT_LOCAL + 16
AT_ROUTE = 64
AT_MINE = 96
F32 = jnp.float32
BF16 = jnp.bfloat16


def call(kernel, out, name, scratch=(), places=None):
    vmem = pl.BlockSpec(memory_space=pltpu.VMEM)
    specs = {}
    if places:
        specs["in_specs"] = [pl.BlockSpec(memory_space=pl.ANY) if p else vmem for p in places]
    return pl.pallas_call(
        kernel,
        out_shape=out,
        out_specs=jax.tree.map(lambda _: vmem, out),
        scratch_shapes=scratch,
        compiler_params=pltpu.CompilerParams(vmem_limit_bytes=(56 if places else 40) * 2**20),
        name=name,
        **specs,
    )


def split_log(log):
    first = jnp.floor(log * 0.125) * 8.0
    rest = log - first
    second = jnp.floor(rest * 32.0) * (1.0 / 32.0)
    rest = rest - second
    third = jnp.floor(rest * 8192.0) * (1.0 / 8192.0)
    return first, second, third, rest - third


def stacked_rows(rows):
    index = lax.broadcasted_iota(jnp.int32, (8, HD), 0)
    total = jnp.zeros((8, HD), F32)
    for i, row in enumerate(rows):
        total = jnp.where(index == i, jnp.broadcast_to(row, (8, HD)), total)
    return total


def joined_log(rows, first):
    return (rows[first : first + 1] + rows[first + 1 : first + 2]) + (
        rows[first + 2 : first + 3] + rows[first + 3 : first + 4]
    )


def prefix_sums(rows):
    lane = lax.broadcasted_iota(jnp.int32, rows.shape, 1)
    shift = 1
    while shift < TOK:
        rows = rows + jnp.where(lane >= shift, pltpu.roll(rows, shift, 1), 0.0)
        shift *= 2
    return rows


def fading_scores(q, k, column, row):
    scores = lax.dot_general(q, k, (((1,), (1,)), ((), ())), preferred_element_type=F32)
    causal = lax.broadcasted_iota(jnp.int32, scores.shape, 0) >= lax.broadcasted_iota(
        jnp.int32, scores.shape, 1
    )
    fading = jnp.exp(jnp.minimum(column - row, 0.0))
    return jnp.where(causal, scores * fading, 0.0).astype(BF16)


def beside(one, two):
    row = lax.broadcasted_iota(jnp.int32, one.shape, 0)
    return jnp.where(row < HALF, one, pltpu.roll(two, HALF, 0))


def two_parts(array):
    coarse = array.astype(BF16).astype(F32)
    return coarse, array - coarse


def route_facts(ids_ref, gates_ref, facts_ref):
    facts_ref[...] = jnp.zeros((8, HD), F32)
    facts_ref[0:2, 0:MROWS] = ids_ref[...].astype(F32)
    facts_ref[6:8, 0:MROWS] = gates_ref[...]
    names = facts_ref[0:2, :]
    lane = lax.broadcasted_iota(jnp.int32, (2, HD), 1)
    choice = lax.broadcasted_iota(jnp.int32, (2, HD), 0)
    slots = jnp.where((choice == 1) & (names[0:1] == names[1:2]), 1.0, 0.0)
    for t in range(MROWS - 1):
        for c in range(2):
            same = (names[c : c + 1, t : t + 1] == names) & (lane > t)
            slots = slots + jnp.where(same, 1.0, 0.0)
    facts_ref[4:6, :] = jnp.where(lane < MROWS, names * float(CAP) + slots, 0.0)
    facts_ref[0:2, :] = jnp.zeros((2, HD), F32)


def update_kernel(*refs):
    sources, (run_ref, msg_ref), fetched = refs[:6], refs[6:8], refs[8:14]
    facts_ref, semaphores = refs[14:]
    copies = []
    for i, (source, target) in enumerate(zip(sources, fetched)):
        part = source.at[:, pl.ds(0, FEW)] if i == 1 else source
        copies.append(pltpu.make_async_copy(part, target, semaphores.at[i]))
    for copy in copies:
        copy.start()
    decay_ref, q_ref, k_ref, v_ref, ids_ref, gates_ref = fetched
    for i in (0, 4, 5):
        copies[i].wait()
    running = prefix_sums(jnp.concatenate([decay_ref[0], decay_ref[1]], axis=0))
    run_ref[...] = running
    end = running[:, TOK - 1 :]
    to_end = jnp.exp(end - running).T
    columns = running.T[:FEW]
    route_facts(ids_ref, gates_ref, facts_ref)
    for i in (1, 2, 3):
        copies[i].wait()
    for owner in range(X):
        parts, logs, qs, locals_ = [], [], [], []
        for i in range(OWN):
            b, pair, cols = i, i * HEADS + owner, pl.ds(owner * HD, HD)
            decayed = (k_ref[b, :, cols].astype(F32) * to_end[:, pair : pair + 1]).astype(BF16)
            parts.append(
                lax.dot_general(
                    v_ref[b, :, cols], decayed, (((0,), (0,)), ((), ())), preferred_element_type=F32
                )
            )
            logs += [jnp.broadcast_to(p, (1, HD)) for p in split_log(end[pair : pair + 1])]
            q, column = q_ref[b, :FEW, cols], columns[:, pair : pair + 1]
            weights = fading_scores(
                q, k_ref[b, :FEW, cols], column, running[pair : pair + 1, :FEW]
            )
            local = jnp.dot(weights, v_ref[b, :FEW, cols], preferred_element_type=F32)
            locals_.append(local[:8])
            qs.append((q.astype(F32) * jnp.exp(column))[:8])
        local = two_parts(beside(*locals_))
        msg_ref[owner] = jnp.concatenate(
            parts + [stacked_rows(logs), beside(*qs), local[0], local[1], facts_ref[...]], axis=0
        ).astype(BF16)


def placed(rows, i, x):
    row = lax.broadcasted_iota(jnp.int32, rows.shape, 0)
    moved = rows if i == x % 2 else pltpu.roll(rows, HALF, 0)
    moved = jnp.where(row // HALF == x % 2, moved, 0.0)
    zero = jnp.zeros_like(moved)
    return jnp.concatenate([moved, zero] if x < 2 else [zero, moved], axis=0)


def tall(rows):
    return jnp.concatenate([rows, jnp.zeros((HD - rows.shape[0], HD), F32)], axis=0)


def group_kernel(msg_ref, out_ref):
    lane = lax.broadcasted_iota(jnp.int32, (8, HD), 1)
    facts = jnp.zeros((8, HD), F32)
    for x in range(X):
        own = msg_ref[x].astype(F32)[AT_FACTS:]
        for b in range(2):
            only = jnp.where(lane // HALF == b, own, 0.0)
            shift = b * 16 + x * HALF - b * HALF
            facts = facts + pltpu.roll(only, AT_ROUTE + shift, 1)
        mine = jnp.where((lane < MROWS) & (lax.axis_index("x") == x), own, 0.0)
        facts = facts + pltpu.roll(mine, AT_MINE, 1)
    for i in range(OWN):
        total, log, queries, near, inner = None, None, 0.0, 0.0, 0.0
        for x in range(X):
            part = msg_ref[x].astype(F32)
            update = part[i * HD : (i + 1) * HD]
            own_log = joined_log(part, AT_LOGS + 4 * i)
            q = placed(part[AT_Q : AT_Q + 8], i, x)
            local = part[AT_LOCAL : AT_LOCAL + 8] + part[AT_LOCAL + 8 : AT_LOCAL + 16]
            near = near + placed(local, i, x)
            if x == 0:
                queries = q
                total, log = update, own_log
            else:
                inner = inner + lax.dot_general(
                    total.astype(BF16),
                    tall(q).astype(BF16),
                    (((1,), (1,)), ((), ())),
                    preferred_element_type=F32,
                )
                queries = queries + q * jnp.exp(log)
                total, log = jnp.exp(own_log) * total + update, log + own_log
        coarse, rest = two_parts(inner + tall(near).T)
        rows = coarse + pltpu.roll(rest, 16, 1)
        info = jnp.where(lane < AT_ROUTE, 0.0, stacked_rows(split_log(log)) + facts)
        for g in range(HD // PART):
            at = g * PART
            near = rows[at : at + 8] + pltpu.roll(rows[at + 8 : at + PART], 32, 1)
            out_ref[i * (HD // PART) + g] = jnp.concatenate(
                [total[at : at + PART], info + near, queries], axis=0
            ).astype(BF16)


def scan_kernel(msg_ref, out_ref, facts_ref):
    state = jnp.zeros((PART, HD), F32)
    lane = lax.broadcasted_iota(jnp.int32, (16, HD), 1)
    states, queries = [], []
    near = [jnp.zeros((PART, HD), F32) for _ in range(2)]
    facts = [jnp.zeros((8, HD), F32) for _ in range(5)]
    for z in range(Z):
        states.append(state)
        part = msg_ref[z].astype(F32)
        info = part[16:24]
        queries.append(part[24:40])
        half, shift = z // 8, z % 8 * 16
        rows = jnp.concatenate([info, pltpu.roll(info, HD - 32, 1)], axis=0)
        rows = jnp.where(lane < 16, rows + pltpu.roll(rows, HD - 16, 1), 0.0)
        near[half] = near[half] + (pltpu.roll(rows, shift, 1) if shift else rows)
        for b in range(2):
            only = jnp.where(lane[:8] // 16 == AT_ROUTE // 16 + b, info, 0.0)
            move = (shift - AT_ROUTE - b * 16) % HD
            place = half * 2 + b
            facts[place] = facts[place] + (pltpu.roll(only, move, 1) if move else only)
        only = jnp.where(lane[:8] // MROWS == AT_MINE // MROWS, info, 0.0)
        move = (z * MROWS - AT_MINE) % HD
        facts[4] = facts[4] + (pltpu.roll(only, move, 1) if move else only)
        factor = jnp.exp(joined_log(part, PART))[:, AT_ROUTE : AT_ROUTE + 1]
        state = factor * state + part[:PART]
    far = lax.dot_general(
        jnp.concatenate(states, axis=0).astype(BF16),
        jnp.concatenate(queries, axis=0).astype(BF16),
        (((1,), (1,)), ((), ())),
        preferred_element_type=F32,
    )
    row = lax.broadcasted_iota(jnp.int32, far.shape, 0)
    column = lax.broadcasted_iota(jnp.int32, far.shape, 1)
    far = jnp.where(row // 16 == column // 16, far, 0.0)
    total = jnp.concatenate(near, axis=1)
    for z in range(Z):
        total = total + far[z * PART : (z + 1) * PART]
    for z in range(Z):
        out_ref[z] = jnp.concatenate(
            [states[z], total[:, :HD], total[:, HD:]], axis=0
        ).astype(BF16)
    facts_ref[...] = jnp.concatenate(facts, axis=1)


def expand_kernel(back_ref, msg_ref, gain_ref, facts_ref, state_ref, slots_ref):
    gain = gain_ref[:, :HD]
    for x in range(1, X):
        gain = jnp.where(lax.axis_index("x") == x, gain_ref[:, x * HD : (x + 1) * HD], gain)
    back = [back_ref[c].astype(F32) for c in range(Z)]
    each = Z // OWN
    state, rows = [], []
    for i in range(OWN):
        mine = back[i * each : (i + 1) * each]
        state.append(jnp.concatenate([part[:PART] for part in mine], axis=0))
        for half in range(2):
            first = PART * (1 + half)
            o = jnp.concatenate([part[first : first + PART] for part in mine], axis=0).T
            scale = lax.rsqrt(jnp.mean(o * o, axis=1, keepdims=True) + 1e-6)
            rows.append((o * scale * gain).astype(BF16))
    index = lax.broadcasted_iota(jnp.int32, (EXPERTS * HD, 2 * HD), 0)
    lane = lax.broadcasted_iota(jnp.int32, (1, 2 * HD), 1)
    place = lane // HALF % X * 32 + lane % HD // 16 * CAP
    for half in range(2):
        (first, second), _ = slot_rows(
            facts_ref[:, half * 2 * HD : (half + 1) * 2 * HD], place, HD
        )
        chosen = jnp.where((index == first) | (index == second), 1.0, 0.0).astype(BF16)
        both = jnp.concatenate([rows[half], rows[2 + half]], axis=0)
        sent = jnp.dot(chosen, both, preferred_element_type=F32).astype(BF16)
        for e in range(EXPERTS):
            for x in range(X):
                at = e * HD + x * 32
                for target in range(X):
                    slots_ref[target * EXPERTS + e, pl.ds(x * SLOTS + half * 32, 32)] = sent[
                        at : at + 32
                    ]
    for x in range(X):
        state_ref[x] = jnp.concatenate(state, axis=0).astype(BF16)
        if x < X - 1:
            part = msg_ref[x].astype(F32)
            for i in range(OWN):
                factor = jnp.exp(joined_log(part, AT_LOGS + 4 * i))
                state[i] = factor * state[i] + part[i * HD : (i + 1) * HD]


def attention_kernel(q_ref, k_ref, v_ref, run_ref, state_ref, gain_ref, out_ref):
    running = run_ref[...]
    columns = running.T
    for pair in range(PAIRS):
        b, cols = pair // HEADS, pl.ds(pair % HEADS * HD, HD)
        q, column = q_ref[b, :, cols], columns[:, pair : pair + 1]
        state = state_ref[pair % HEADS, b * HD : (b + 1) * HD]
        weights = fading_scores(q, k_ref[b, :, cols], column, running[pair : pair + 1])
        decayed = (q.astype(F32) * jnp.exp(column)).astype(BF16)
        o = jnp.dot(
            weights, v_ref[b, :, cols], preferred_element_type=F32
        ) + lax.dot_general(
            decayed, state, (((1,), (1,)), ((), ())), preferred_element_type=F32
        )
        scale = lax.rsqrt(jnp.mean(o * o, axis=1, keepdims=True) + 1e-6)
        out_ref[b, :, cols] = (o * scale * gain_ref[:, cols]).astype(BF16)


def slot_rows(facts, place, slots):
    rows = []
    for j in range(2):
        code = facts[4 + j : 5 + j].astype(jnp.int32)
        rows.append(code // CAP * slots + code % CAP + place)
    return rows, [facts[6:7], facts[7:8]]


def expert_kernel(
    rows_hbm,
    gate_hbm,
    up_hbm,
    down_hbm,
    out_ref,
    rows_ref,
    gate_ref,
    up_ref,
    down_ref,
    semaphores,
):
    copies = []
    for j in range(EXPERTS):
        part = pl.ds(j * COLS, COLS)
        for source, target in (
            (rows_hbm.at[:, j], rows_ref.at[j]),
            (gate_hbm.at[part], gate_ref.at[part]),
            (up_hbm.at[part], up_ref.at[part]),
        ):
            copies.append(pltpu.make_async_copy(source, target, semaphores.at[len(copies)]))
    copies.append(pltpu.make_async_copy(down_hbm, down_ref, semaphores.at[len(copies)]))
    for copy in copies:
        copy.start()
    total = None
    for j in range(EXPERTS):
        part = pl.ds(j * COLS, COLS)
        for copy in copies[3 * j : 3 * j + 3]:
            copy.wait()
        both = jnp.concatenate([gate_ref[part, :], up_ref[part, :]], axis=1)
        rows = jnp.concatenate([rows_ref[j, x] for x in range(X)], axis=1)
        term = jnp.dot(rows, both, preferred_element_type=F32)
        total = term if total is None else total + term
    width = gate_ref.shape[1]
    gate, up = total[:, :width], total[:, width:]
    hidden = (gate / (1.0 + jnp.exp(-gate)) * up).astype(BF16)
    copies[-1].wait()
    for j in range(EXPERTS):
        out = jnp.dot(hidden, down_ref[:, pl.ds(j * COLS, COLS)], preferred_element_type=F32)
        for x in range(X):
            out_ref[x * EXPERTS + j] = out[x * SLOTS : (x + 1) * SLOTS].astype(BF16)


def combine_kernel(parts_ref, facts_ref, out_ref):
    index = lax.broadcasted_iota(jnp.int32, (EXPERTS * SLOTS, GROUP), 0)
    place = lax.broadcasted_iota(jnp.int32, (1, GROUP), 1) // MROWS * CAP
    (first, second), gates = slot_rows(facts_ref[:, 4 * HD :], place, SLOTS)
    mix = jnp.where(index == first, gates[0], 0.0) + jnp.where(index == second, gates[1], 0.0)
    rows = []
    for e in range(EXPERTS):
        total = parts_ref[e].astype(F32)
        for x in range(1, X):
            total = total + parts_ref[x * EXPERTS + e].astype(F32)
        rows.append(total.astype(BF16))
    out_ref[...] = lax.dot_general(
        mix.astype(BF16),
        jnp.concatenate(rows, axis=0),
        (((0,), (0,)), ((), ())),
        preferred_element_type=F32,
    ).astype(BF16)


def sum_kernel(parts_ref, out_ref):
    total = parts_ref[0].astype(F32)
    for i in range(1, parts_ref.shape[0]):
        total = total + parts_ref[i].astype(F32)
    out_ref[...] = total.astype(BF16)


def swap(array, axis):
    return lax.all_to_all(array, axis, 0, 0, tiled=True)


def body(
    queries, keys, values, log_decay, norm_gain, expert_ids, gate_weights, w_gate, w_up, w_down
):
    shape = jax.ShapeDtypeStruct
    decay = jnp.transpose(log_decay, (0, 2, 1))
    gain = norm_gain.reshape(1, COLS)
    running, message = call(
        update_kernel,
        (shape((PAIRS, TOK), F32), shape((X, AT_FACTS + 8, HD), BF16)),
        "update",
        [
            pltpu.VMEM((2, HEADS, TOK), F32),
            pltpu.VMEM((2, FEW, COLS), BF16),
            pltpu.VMEM((2, TOK, COLS), BF16),
            pltpu.VMEM((2, TOK, COLS), BF16),
            pltpu.VMEM((2, MROWS), jnp.int32),
            pltpu.VMEM((2, MROWS), F32),
            pltpu.VMEM((8, HD), F32),
            pltpu.SemaphoreType.DMA((6,)),
        ],
        [True] * 6,
    )(decay, queries, keys, values, expert_ids.T, gate_weights.T)
    message = swap(message, "x")
    groups = call(group_kernel, shape((Z, PART + 24, HD), BF16), "group")(message)
    groups = swap(groups, "z")
    back, facts = call(
        scan_kernel,
        (shape((Z, 3 * PART, HD), BF16), shape((8, 5 * HD), F32)),
        "scan",
    )(groups)
    back = swap(back, "z")
    states, slots = call(
        expand_kernel,
        (shape((X, OWN * HD, HD), BF16), shape((X * EXPERTS, X * SLOTS, HD), BF16)),
        "expand",
    )(back, message, gain, facts)
    slots = swap(slots, ("x", "y", "core"))
    states = swap(states, "x")
    attn_out = call(attention_kernel, shape((2, TOK, COLS), BF16), "attention")(
        queries, keys, values, running, states, gain
    )
    weights = (w_gate[0], w_up[0], w_down[0])
    parts = call(
        expert_kernel,
        shape((X * EXPERTS, SLOTS, COLS), BF16),
        "experts",
        [pltpu.VMEM((EXPERTS, X, X * SLOTS, HD), BF16)]
        + [pltpu.VMEM(w.shape, BF16) for w in weights]
        + [pltpu.SemaphoreType.DMA((3 * EXPERTS + 1,))],
        [True] * 4,
    )(slots.reshape(X, EXPERTS, X * SLOTS, HD), *weights)
    parts = swap(parts, ("x", "y", "core"))
    parts, attn_out = lax.optimization_barrier((parts, attn_out))
    share = call(combine_kernel, shape((GROUP, COLS), BF16), "combine")(parts, facts)
    share = swap(share.reshape(Z, MROWS, COLS), "z")
    moe_out = call(sum_kernel, shape((MROWS, COLS), BF16), "sum_z")(share)
    return (attn_out, moe_out)


def solution(mesh):
    fine = Mesh(mesh.devices.reshape(Z, X, Y, CORE), ("z", "x", "y", "core"))
    seq, expert = ("z", "x"), ("y", "core")
    placed = (
        P(None, seq, expert),
        P(None, seq, expert),
        P(None, seq, expert),
        P(None, seq, expert),
        P(expert),
        P(seq, None),
        P(seq, None),
        P(expert, None, seq),
        P(expert, None, seq),
        P(expert, seq, None),
    )
    return jax.shard_map(
        body,
        mesh=fine,
        in_specs=placed,
        out_specs=(P(None, seq, expert), P(seq, expert)),
        check_vma=False,
    )
```

```python
import jax
import jax.numpy as jnp
from jax import lax
from jax.experimental import pallas as pl
from jax.experimental.pallas import tpu as pltpu
from jax.sharding import Mesh
from jax.sharding import PartitionSpec as P

HD = 128
HEADS = 4
PAIRS = 8
TOK = 256
Z, X, Y, CORE = 16, 4, 4, 2
EXPERTS = Y * CORE
MROWS = 8
CAP = 4
COLS = HEADS * HD
OWN = PAIRS // X
PART = OWN * HD // Z
SLOTS = Z * CAP
HALF = MROWS // 2
FEW = 16
GROUP = Z * MROWS
AT_LOGS = OWN * HD
AT_Q = AT_LOGS + 8
AT_LOCAL = AT_Q + 8
AT_FACTS = AT_LOCAL + 16
AT_ROUTE = 64
AT_MINE = 96
F32 = jnp.float32
BF16 = jnp.bfloat16


def call(kernel, out, name, scratch=(), places=None, results=None):
    vmem, own = pl.BlockSpec(memory_space=pltpu.VMEM), pl.BlockSpec(memory_space=pl.ANY)
    specs = {"out_specs": jax.tree.map(lambda _: vmem, out)}
    if places:
        specs["in_specs"] = [own if p else vmem for p in places]
    if results:
        specs["out_specs"] = tuple(own if p else vmem for p in results)
    return pl.pallas_call(
        kernel,
        out_shape=out,
        scratch_shapes=scratch,
        compiler_params=pltpu.CompilerParams(vmem_limit_bytes=(56 if places else 40) * 2**20),
        name=name,
        **specs,
    )


def split_log(log):
    first = jnp.floor(log * 0.125) * 8.0
    rest = log - first
    second = jnp.floor(rest * 32.0) * (1.0 / 32.0)
    rest = rest - second
    third = jnp.floor(rest * 8192.0) * (1.0 / 8192.0)
    return first, second, third, rest - third


def stacked_rows(rows):
    index = lax.broadcasted_iota(jnp.int32, (8, HD), 0)
    total = jnp.zeros((8, HD), F32)
    for i, row in enumerate(rows):
        total = jnp.where(index == i, jnp.broadcast_to(row, (8, HD)), total)
    return total


def joined_log(rows, first):
    return (rows[first : first + 1] + rows[first + 1 : first + 2]) + (
        rows[first + 2 : first + 3] + rows[first + 3 : first + 4]
    )


def prefix_sums(rows):
    lane = lax.broadcasted_iota(jnp.int32, rows.shape, 1)
    shift = 1
    while shift < TOK:
        rows = rows + jnp.where(lane >= shift, pltpu.roll(rows, shift, 1), 0.0)
        shift *= 2
    return rows


def fading_scores(q, k, column, row):
    scores = lax.dot_general(q, k, (((1,), (1,)), ((), ())), preferred_element_type=F32)
    causal = lax.broadcasted_iota(jnp.int32, scores.shape, 0) >= lax.broadcasted_iota(
        jnp.int32, scores.shape, 1
    )
    fading = jnp.exp(jnp.minimum(column - row, 0.0))
    return jnp.where(causal, scores * fading, 0.0).astype(BF16)


def beside(one, two):
    row = lax.broadcasted_iota(jnp.int32, one.shape, 0)
    return jnp.where(row < HALF, one, pltpu.roll(two, HALF, 0))


def two_parts(array):
    coarse = array.astype(BF16).astype(F32)
    return coarse, array - coarse


def route_facts(ids_ref, gates_ref, facts_ref):
    facts_ref[...] = jnp.zeros((8, HD), F32)
    facts_ref[0:2, 0:MROWS] = ids_ref[...].astype(F32)
    facts_ref[6:8, 0:MROWS] = gates_ref[...]
    names = facts_ref[0:2, :]
    lane = lax.broadcasted_iota(jnp.int32, (2, HD), 1)
    choice = lax.broadcasted_iota(jnp.int32, (2, HD), 0)
    slots = jnp.where((choice == 1) & (names[0:1] == names[1:2]), 1.0, 0.0)
    for t in range(MROWS - 1):
        for c in range(2):
            same = (names[c : c + 1, t : t + 1] == names) & (lane > t)
            slots = slots + jnp.where(same, 1.0, 0.0)
    facts_ref[4:6, :] = jnp.where(lane < MROWS, names * float(CAP) + slots, 0.0)
    facts_ref[0:2, :] = jnp.zeros((2, HD), F32)


def update_kernel(*refs):
    sources, (run_ref, msg_hbm), fetched = refs[:6], refs[6:8], refs[8:14]
    msg_ref, facts_ref, semaphores = refs[14:]

    def copy(i, source, target):
        return pltpu.make_async_copy(source, target, semaphores.at[i])

    decay_ref, q_ref, k_ref, v_ref, ids_ref, gates_ref = fetched
    first = [copy(i, sources[i], fetched[i]) for i in (0, 4, 5)]
    first.append(copy(1, sources[1].at[:, pl.ds(0, FEW)], q_ref))
    heads = []
    for owner in range(X):
        part = (slice(None), slice(None), pl.ds(owner * HD, HD))
        for i in (2, 3):
            heads.append(copy(6 + len(heads), sources[i].at[part], fetched[i].at[part]))
    for fetch in first + heads:
        fetch.start()
    for fetch in first:
        fetch.wait()
    running = prefix_sums(jnp.concatenate([decay_ref[0], decay_ref[1]], axis=0))
    run_ref[...] = running
    end = running[:, TOK - 1 :]
    to_end = jnp.exp(end - running).T
    columns = running.T[:FEW]
    route_facts(ids_ref, gates_ref, facts_ref)
    sent = []
    for owner in range(X):
        for fetch in heads[2 * owner : 2 * owner + 2]:
            fetch.wait()
        parts, logs, qs, locals_ = [], [], [], []
        for i in range(OWN):
            b, pair, cols = i, i * HEADS + owner, pl.ds(owner * HD, HD)
            decayed = (k_ref[b, :, cols].astype(F32) * to_end[:, pair : pair + 1]).astype(BF16)
            parts.append(
                lax.dot_general(
                    v_ref[b, :, cols], decayed, (((0,), (0,)), ((), ())), preferred_element_type=F32
                )
            )
            logs += [jnp.broadcast_to(p, (1, HD)) for p in split_log(end[pair : pair + 1])]
            q, column = q_ref[b, :FEW, cols], columns[:, pair : pair + 1]
            weights = fading_scores(
                q, k_ref[b, :FEW, cols], column, running[pair : pair + 1, :FEW]
            )
            local = jnp.dot(weights, v_ref[b, :FEW, cols], preferred_element_type=F32)
            locals_.append(local[:8])
            qs.append((q.astype(F32) * jnp.exp(column))[:8])
        local = two_parts(beside(*locals_))
        msg_ref[owner] = jnp.concatenate(
            parts + [stacked_rows(logs), beside(*qs), local[0], local[1], facts_ref[...]], axis=0
        ).astype(BF16)
        sent.append(copy(14 + owner, msg_ref.at[owner], msg_hbm.at[owner]))
        sent[-1].start()
    for send in sent:
        send.wait()


def placed(rows, i, x):
    row = lax.broadcasted_iota(jnp.int32, rows.shape, 0)
    moved = rows if i == x % 2 else pltpu.roll(rows, HALF, 0)
    moved = jnp.where(row // HALF == x % 2, moved, 0.0)
    zero = jnp.zeros_like(moved)
    return jnp.concatenate([moved, zero] if x < 2 else [zero, moved], axis=0)


def tall(rows):
    return jnp.concatenate([rows, jnp.zeros((HD - rows.shape[0], HD), F32)], axis=0)


def group_kernel(msg_ref, out_ref):
    lane = lax.broadcasted_iota(jnp.int32, (8, HD), 1)
    facts = jnp.zeros((8, HD), F32)
    for x in range(X):
        own = msg_ref[x].astype(F32)[AT_FACTS:]
        for b in range(2):
            only = jnp.where(lane // HALF == b, own, 0.0)
            shift = b * 16 + x * HALF - b * HALF
            facts = facts + pltpu.roll(only, AT_ROUTE + shift, 1)
        mine = jnp.where((lane < MROWS) & (lax.axis_index("x") == x), own, 0.0)
        facts = facts + pltpu.roll(mine, AT_MINE, 1)
    for i in range(OWN):
        total, log, queries, near, inner = None, None, 0.0, 0.0, 0.0
        for x in range(X):
            part = msg_ref[x].astype(F32)
            update = part[i * HD : (i + 1) * HD]
            own_log = joined_log(part, AT_LOGS + 4 * i)
            q = placed(part[AT_Q : AT_Q + 8], i, x)
            local = part[AT_LOCAL : AT_LOCAL + 8] + part[AT_LOCAL + 8 : AT_LOCAL + 16]
            near = near + placed(local, i, x)
            if x == 0:
                queries = q
                total, log = update, own_log
            else:
                inner = inner + lax.dot_general(
                    total.astype(BF16),
                    tall(q).astype(BF16),
                    (((1,), (1,)), ((), ())),
                    preferred_element_type=F32,
                )
                queries = queries + q * jnp.exp(log)
                total, log = jnp.exp(own_log) * total + update, log + own_log
        coarse, rest = two_parts(inner + tall(near).T)
        rows = coarse + pltpu.roll(rest, 16, 1)
        info = jnp.where(lane < AT_ROUTE, 0.0, stacked_rows(split_log(log)) + facts)
        for g in range(HD // PART):
            at = g * PART
            near = rows[at : at + 8] + pltpu.roll(rows[at + 8 : at + PART], 32, 1)
            out_ref[i * (HD // PART) + g] = jnp.concatenate(
                [total[at : at + PART], info + near, queries], axis=0
            ).astype(BF16)


def scan_kernel(msg_ref, out_ref, facts_ref):
    state = jnp.zeros((PART, HD), F32)
    lane = lax.broadcasted_iota(jnp.int32, (16, HD), 1)
    states, queries = [], []
    near = [jnp.zeros((PART, HD), F32) for _ in range(2)]
    facts = [jnp.zeros((8, HD), F32) for _ in range(5)]
    for z in range(Z):
        states.append(state)
        part = msg_ref[z].astype(F32)
        info = part[16:24]
        queries.append(part[24:40])
        half, shift = z // 8, z % 8 * 16
        rows = jnp.concatenate([info, pltpu.roll(info, HD - 32, 1)], axis=0)
        rows = jnp.where(lane < 16, rows + pltpu.roll(rows, HD - 16, 1), 0.0)
        near[half] = near[half] + (pltpu.roll(rows, shift, 1) if shift else rows)
        for b in range(2):
            only = jnp.where(lane[:8] // 16 == AT_ROUTE // 16 + b, info, 0.0)
            move = (shift - AT_ROUTE - b * 16) % HD
            place = half * 2 + b
            facts[place] = facts[place] + (pltpu.roll(only, move, 1) if move else only)
        only = jnp.where(lane[:8] // MROWS == AT_MINE // MROWS, info, 0.0)
        move = (z * MROWS - AT_MINE) % HD
        facts[4] = facts[4] + (pltpu.roll(only, move, 1) if move else only)
        factor = jnp.exp(joined_log(part, PART))[:, AT_ROUTE : AT_ROUTE + 1]
        state = factor * state + part[:PART]
    far = lax.dot_general(
        jnp.concatenate(states, axis=0).astype(BF16),
        jnp.concatenate(queries, axis=0).astype(BF16),
        (((1,), (1,)), ((), ())),
        preferred_element_type=F32,
    )
    row = lax.broadcasted_iota(jnp.int32, far.shape, 0)
    column = lax.broadcasted_iota(jnp.int32, far.shape, 1)
    far = jnp.where(row // 16 == column // 16, far, 0.0)
    total = jnp.concatenate(near, axis=1)
    for z in range(Z):
        total = total + far[z * PART : (z + 1) * PART]
    for z in range(Z):
        out_ref[z] = jnp.concatenate(
            [states[z], total[:, :HD], total[:, HD:]], axis=0
        ).astype(BF16)
    facts_ref[...] = jnp.concatenate(facts, axis=1)


def expand_kernel(back_ref, msg_ref, gain_ref, facts_ref, state_ref, slots_ref):
    gain = gain_ref[:, :HD]
    for x in range(1, X):
        gain = jnp.where(lax.axis_index("x") == x, gain_ref[:, x * HD : (x + 1) * HD], gain)
    back = [back_ref[c].astype(F32) for c in range(Z)]
    each = Z // OWN
    state, rows = [], []
    for i in range(OWN):
        mine = back[i * each : (i + 1) * each]
        state.append(jnp.concatenate([part[:PART] for part in mine], axis=0))
        for half in range(2):
            first = PART * (1 + half)
            o = jnp.concatenate([part[first : first + PART] for part in mine], axis=0).T
            scale = lax.rsqrt(jnp.mean(o * o, axis=1, keepdims=True) + 1e-6)
            rows.append((o * scale * gain).astype(BF16))
    index = lax.broadcasted_iota(jnp.int32, (EXPERTS * HD, 2 * HD), 0)
    lane = lax.broadcasted_iota(jnp.int32, (1, 2 * HD), 1)
    place = lane // HALF % X * 32 + lane % HD // 16 * CAP
    for half in range(2):
        (first, second), _ = slot_rows(
            facts_ref[:, half * 2 * HD : (half + 1) * 2 * HD], place, HD
        )
        chosen = jnp.where((index == first) | (index == second), 1.0, 0.0).astype(BF16)
        both = jnp.concatenate([rows[half], rows[2 + half]], axis=0)
        sent = jnp.dot(chosen, both, preferred_element_type=F32).astype(BF16)
        for e in range(EXPERTS):
            for x in range(X):
                at = e * HD + x * 32
                for target in range(X):
                    slots_ref[target * EXPERTS + e, pl.ds(x * SLOTS + half * 32, 32)] = sent[
                        at : at + 32
                    ]
    for x in range(X):
        state_ref[x] = jnp.concatenate(state, axis=0).astype(BF16)
        if x < X - 1:
            part = msg_ref[x].astype(F32)
            for i in range(OWN):
                factor = jnp.exp(joined_log(part, AT_LOGS + 4 * i))
                state[i] = factor * state[i] + part[i * HD : (i + 1) * HD]


def attention_kernel(q_ref, k_ref, v_ref, run_ref, state_ref, gain_ref, out_ref):
    running = run_ref[...]
    columns = running.T
    for pair in range(PAIRS):
        b, cols = pair // HEADS, pl.ds(pair % HEADS * HD, HD)
        q, column = q_ref[b, :, cols], columns[:, pair : pair + 1]
        state = state_ref[pair % HEADS, b * HD : (b + 1) * HD]
        weights = fading_scores(q, k_ref[b, :, cols], column, running[pair : pair + 1])
        decayed = (q.astype(F32) * jnp.exp(column)).astype(BF16)
        o = jnp.dot(
            weights, v_ref[b, :, cols], preferred_element_type=F32
        ) + lax.dot_general(
            decayed, state, (((1,), (1,)), ((), ())), preferred_element_type=F32
        )
        scale = lax.rsqrt(jnp.mean(o * o, axis=1, keepdims=True) + 1e-6)
        out_ref[b, :, cols] = (o * scale * gain_ref[:, cols]).astype(BF16)


def slot_rows(facts, place, slots):
    rows = []
    for j in range(2):
        code = facts[4 + j : 5 + j].astype(jnp.int32)
        rows.append(code // CAP * slots + code % CAP + place)
    return rows, [facts[6:7], facts[7:8]]


def expert_kernel(
    rows_hbm,
    gate_hbm,
    up_hbm,
    down_hbm,
    out_ref,
    rows_ref,
    gate_ref,
    up_ref,
    down_ref,
    semaphores,
):
    copies = []
    for j in range(EXPERTS):
        part = pl.ds(j * COLS, COLS)
        for source, target in (
            (rows_hbm.at[:, j], rows_ref.at[j]),
            (gate_hbm.at[part], gate_ref.at[part]),
            (up_hbm.at[part], up_ref.at[part]),
        ):
            copies.append(pltpu.make_async_copy(source, target, semaphores.at[len(copies)]))
    copies.append(pltpu.make_async_copy(down_hbm, down_ref, semaphores.at[len(copies)]))
    for copy in copies:
        copy.start()
    total = None
    for j in range(EXPERTS):
        part = pl.ds(j * COLS, COLS)
        for copy in copies[3 * j : 3 * j + 3]:
            copy.wait()
        both = jnp.concatenate([gate_ref[part, :], up_ref[part, :]], axis=1)
        rows = jnp.concatenate([rows_ref[j, x] for x in range(X)], axis=1)
        term = jnp.dot(rows, both, preferred_element_type=F32)
        total = term if total is None else total + term
    width = gate_ref.shape[1]
    gate, up = total[:, :width], total[:, width:]
    hidden = (gate / (1.0 + jnp.exp(-gate)) * up).astype(BF16)
    copies[-1].wait()
    for j in range(EXPERTS):
        out = jnp.dot(hidden, down_ref[:, pl.ds(j * COLS, COLS)], preferred_element_type=F32)
        for x in range(X):
            out_ref[x * EXPERTS + j] = out[x * SLOTS : (x + 1) * SLOTS].astype(BF16)


def combine_kernel(parts_ref, facts_ref, out_ref):
    index = lax.broadcasted_iota(jnp.int32, (EXPERTS * SLOTS, GROUP), 0)
    place = lax.broadcasted_iota(jnp.int32, (1, GROUP), 1) // MROWS * CAP
    (first, second), gates = slot_rows(facts_ref[:, 4 * HD :], place, SLOTS)
    mix = jnp.where(index == first, gates[0], 0.0) + jnp.where(index == second, gates[1], 0.0)
    rows = []
    for e in range(EXPERTS):
        total = parts_ref[e].astype(F32)
        for x in range(1, X):
            total = total + parts_ref[x * EXPERTS + e].astype(F32)
        rows.append(total.astype(BF16))
    out_ref[...] = lax.dot_general(
        mix.astype(BF16),
        jnp.concatenate(rows, axis=0),
        (((0,), (0,)), ((), ())),
        preferred_element_type=F32,
    ).astype(BF16)


def sum_kernel(parts_ref, out_ref):
    total = parts_ref[0].astype(F32)
    for i in range(1, parts_ref.shape[0]):
        total = total + parts_ref[i].astype(F32)
    out_ref[...] = total.astype(BF16)


def swap(array, axis):
    return lax.all_to_all(array, axis, 0, 0, tiled=True)


def body(
    queries, keys, values, log_decay, norm_gain, expert_ids, gate_weights, w_gate, w_up, w_down
):
    shape = jax.ShapeDtypeStruct
    decay = jnp.transpose(log_decay, (0, 2, 1))
    gain = norm_gain.reshape(1, COLS)
    running, message = call(
        update_kernel,
        (shape((PAIRS, TOK), F32), shape((X, AT_FACTS + 8, HD), BF16)),
        "update",
        [
            pltpu.VMEM((2, HEADS, TOK), F32),
            pltpu.VMEM((2, FEW, COLS), BF16),
            pltpu.VMEM((2, TOK, COLS), BF16),
            pltpu.VMEM((2, TOK, COLS), BF16),
            pltpu.VMEM((2, MROWS), jnp.int32),
            pltpu.VMEM((2, MROWS), F32),
            pltpu.VMEM((X, AT_FACTS + 8, HD), BF16),
            pltpu.VMEM((8, HD), F32),
            pltpu.SemaphoreType.DMA((18,)),
        ],
        [True] * 6,
        [False, True],
    )(decay, queries, keys, values, expert_ids.T, gate_weights.T)
    message = swap(message, "x")
    groups = call(group_kernel, shape((Z, PART + 24, HD), BF16), "group")(message)
    groups = swap(groups, "z")
    back, facts = call(
        scan_kernel,
        (shape((Z, 3 * PART, HD), BF16), shape((8, 5 * HD), F32)),
        "scan",
    )(groups)
    back = swap(back, "z")
    states, slots = call(
        expand_kernel,
        (shape((X, OWN * HD, HD), BF16), shape((X * EXPERTS, X * SLOTS, HD), BF16)),
        "expand",
    )(back, message, gain, facts)
    slots = swap(slots, ("x", "y", "core"))
    states = swap(states, "x")
    weights = (w_gate[0], w_up[0], w_down[0])
    parts = call(
        expert_kernel,
        shape((X * EXPERTS, SLOTS, COLS), BF16),
        "experts",
        [pltpu.VMEM((EXPERTS, X, X * SLOTS, HD), BF16)]
        + [pltpu.VMEM(w.shape, BF16) for w in weights]
        + [pltpu.SemaphoreType.DMA((3 * EXPERTS + 1,))],
        [True] * 4,
    )(slots.reshape(X, EXPERTS, X * SLOTS, HD), *weights)
    parts, states = lax.optimization_barrier((parts, states))
    attn_out = call(attention_kernel, shape((2, TOK, COLS), BF16), "attention")(
        queries, keys, values, running, states, gain
    )
    parts = swap(parts, ("x", "y", "core"))
    share = call(combine_kernel, shape((GROUP, COLS), BF16), "combine")(parts, facts)
    share = swap(share.reshape(Z, MROWS, COLS), "z")
    moe_out = call(sum_kernel, shape((MROWS, COLS), BF16), "sum_z")(share)
    return (attn_out, moe_out)


def solution(mesh):
    fine = Mesh(mesh.devices.reshape(Z, X, Y, CORE), ("z", "x", "y", "core"))
    seq, expert = ("z", "x"), ("y", "core")
    placed = (
        P(None, seq, expert),
        P(None, seq, expert),
        P(None, seq, expert),
        P(None, seq, expert),
        P(expert),
        P(seq, None),
        P(seq, None),
        P(expert, None, seq),
        P(expert, None, seq),
        P(expert, seq, None),
    )
    return jax.shard_map(
        body,
        mesh=fine,
        in_specs=placed,
        out_specs=(P(None, seq, expert), P(seq, expert)),
        check_vma=False,
    )
```

```python
import jax
import jax.numpy as jnp
from jax import lax
from jax.experimental import pallas as pl
from jax.experimental.pallas import tpu as pltpu
from jax.sharding import Mesh
from jax.sharding import PartitionSpec as P

HD = 128
HEADS = 4
PAIRS = 8
TOK = 256
Z, X, Y, CORE = 16, 4, 4, 2
EXPERTS = Y * CORE
MROWS = 8
CAP = 4
COLS = HEADS * HD
OWN = PAIRS // X
PART = OWN * HD // Z
SLOTS = Z * CAP
HALF = MROWS // 2
FEW = 16
GROUP = Z * MROWS
AT_LOGS = OWN * HD
AT_Q = AT_LOGS + 8
AT_LOCAL = AT_Q + 8
AT_FACTS = AT_LOCAL + 16
AT_ROUTE = 64
AT_MINE = 96
F32 = jnp.float32
BF16 = jnp.bfloat16


def call(kernel, out, name, scratch=(), places=None):
    vmem = pl.BlockSpec(memory_space=pltpu.VMEM)
    specs = {}
    if places:
        specs["in_specs"] = [pl.BlockSpec(memory_space=pl.ANY) if p else vmem for p in places]
    return pl.pallas_call(
        kernel,
        out_shape=out,
        out_specs=jax.tree.map(lambda _: vmem, out),
        scratch_shapes=scratch,
        compiler_params=pltpu.CompilerParams(vmem_limit_bytes=(56 if places else 40) * 2**20),
        name=name,
        **specs,
    )


def split_log(log):
    first = jnp.floor(log * 0.125) * 8.0
    rest = log - first
    second = jnp.floor(rest * 32.0) * (1.0 / 32.0)
    rest = rest - second
    third = jnp.floor(rest * 8192.0) * (1.0 / 8192.0)
    return first, second, third, rest - third


def stacked_rows(rows):
    index = lax.broadcasted_iota(jnp.int32, (8, HD), 0)
    total = jnp.zeros((8, HD), F32)
    for i, row in enumerate(rows):
        total = jnp.where(index == i, jnp.broadcast_to(row, (8, HD)), total)
    return total


def joined_log(rows, first):
    return (rows[first : first + 1] + rows[first + 1 : first + 2]) + (
        rows[first + 2 : first + 3] + rows[first + 3 : first + 4]
    )


def prefix_sums(rows):
    lane = lax.broadcasted_iota(jnp.int32, rows.shape, 1)
    shift = 1
    while shift < TOK:
        rows = rows + jnp.where(lane >= shift, pltpu.roll(rows, shift, 1), 0.0)
        shift *= 2
    return rows


def fading_scores(q, k, column, row):
    scores = lax.dot_general(q, k, (((1,), (1,)), ((), ())), preferred_element_type=F32)
    causal = lax.broadcasted_iota(jnp.int32, scores.shape, 0) >= lax.broadcasted_iota(
        jnp.int32, scores.shape, 1
    )
    fading = jnp.exp(jnp.minimum(column - row, 0.0))
    return jnp.where(causal, scores * fading, 0.0).astype(BF16)


def beside(one, two):
    row = lax.broadcasted_iota(jnp.int32, one.shape, 0)
    return jnp.where(row < HALF, one, pltpu.roll(two, HALF, 0))


def two_parts(array):
    coarse = array.astype(BF16).astype(F32)
    return coarse, array - coarse


def route_facts(ids_ref, gates_ref, facts_ref):
    facts_ref[...] = jnp.zeros((8, HD), F32)
    facts_ref[0:2, 0:MROWS] = ids_ref[...].astype(F32)
    facts_ref[6:8, 0:MROWS] = gates_ref[...]
    names = facts_ref[0:2, :]
    lane = lax.broadcasted_iota(jnp.int32, (2, HD), 1)
    choice = lax.broadcasted_iota(jnp.int32, (2, HD), 0)
    slots = jnp.where((choice == 1) & (names[0:1] == names[1:2]), 1.0, 0.0)
    for t in range(MROWS - 1):
        for c in range(2):
            same = (names[c : c + 1, t : t + 1] == names) & (lane > t)
            slots = slots + jnp.where(same, 1.0, 0.0)
    facts_ref[4:6, :] = jnp.where(lane < MROWS, names * float(CAP) + slots, 0.0)
    facts_ref[0:2, :] = jnp.zeros((2, HD), F32)


def update_kernel(*refs):
    sources, (run_ref, msg_ref), fetched = refs[:6], refs[6:8], refs[8:14]
    facts_ref, semaphores = refs[14:]
    copies = []
    for i, (source, target) in enumerate(zip(sources, fetched)):
        part = source.at[:, pl.ds(0, FEW)] if i == 1 else source
        copies.append(pltpu.make_async_copy(part, target, semaphores.at[i]))
    for copy in copies:
        copy.start()
    decay_ref, q_ref, k_ref, v_ref, ids_ref, gates_ref = fetched
    for i in (0, 4, 5):
        copies[i].wait()
    running = prefix_sums(jnp.concatenate([decay_ref[0], decay_ref[1]], axis=0))
    run_ref[...] = running
    end = running[:, TOK - 1 :]
    to_end = jnp.exp(end - running).T
    columns = running.T[:FEW]
    route_facts(ids_ref, gates_ref, facts_ref)
    for i in (1, 2, 3):
        copies[i].wait()
    for owner in range(X):
        parts, logs, qs, locals_ = [], [], [], []
        for i in range(OWN):
            b, pair, cols = i, i * HEADS + owner, pl.ds(owner * HD, HD)
            decayed = (k_ref[b, :, cols].astype(F32) * to_end[:, pair : pair + 1]).astype(BF16)
            parts.append(
                lax.dot_general(
                    v_ref[b, :, cols], decayed, (((0,), (0,)), ((), ())), preferred_element_type=F32
                )
            )
            logs += [jnp.broadcast_to(p, (1, HD)) for p in split_log(end[pair : pair + 1])]
            q, column = q_ref[b, :FEW, cols], columns[:, pair : pair + 1]
            weights = fading_scores(
                q, k_ref[b, :FEW, cols], column, running[pair : pair + 1, :FEW]
            )
            local = jnp.dot(weights, v_ref[b, :FEW, cols], preferred_element_type=F32)
            locals_.append(local[:8])
            qs.append((q.astype(F32) * jnp.exp(column))[:8])
        local = two_parts(beside(*locals_))
        msg_ref[owner] = jnp.concatenate(
            parts + [stacked_rows(logs), beside(*qs), local[0], local[1], facts_ref[...]], axis=0
        ).astype(BF16)


def placed(rows, i, x):
    row = lax.broadcasted_iota(jnp.int32, rows.shape, 0)
    moved = rows if i == x % 2 else pltpu.roll(rows, HALF, 0)
    moved = jnp.where(row // HALF == x % 2, moved, 0.0)
    zero = jnp.zeros_like(moved)
    return jnp.concatenate([moved, zero] if x < 2 else [zero, moved], axis=0)


def tall(rows):
    return jnp.concatenate([rows, jnp.zeros((HD - rows.shape[0], HD), F32)], axis=0)


def group_kernel(msg_ref, out_ref):
    lane = lax.broadcasted_iota(jnp.int32, (8, HD), 1)
    facts = jnp.zeros((8, HD), F32)
    for x in range(X):
        own = msg_ref[x].astype(F32)[AT_FACTS:]
        for b in range(2):
            only = jnp.where(lane // HALF == b, own, 0.0)
            shift = b * 16 + x * HALF - b * HALF
            facts = facts + pltpu.roll(only, AT_ROUTE + shift, 1)
        mine = jnp.where((lane < MROWS) & (lax.axis_index("x") == x), own, 0.0)
        facts = facts + pltpu.roll(mine, AT_MINE, 1)
    for i in range(OWN):
        total, log, queries, near, inner = None, None, 0.0, 0.0, 0.0
        for x in range(X):
            part = msg_ref[x].astype(F32)
            update = part[i * HD : (i + 1) * HD]
            own_log = joined_log(part, AT_LOGS + 4 * i)
            q = placed(part[AT_Q : AT_Q + 8], i, x)
            local = part[AT_LOCAL : AT_LOCAL + 8] + part[AT_LOCAL + 8 : AT_LOCAL + 16]
            near = near + placed(local, i, x)
            if x == 0:
                queries = q
                total, log = update, own_log
            else:
                inner = inner + lax.dot_general(
                    total.astype(BF16),
                    tall(q).astype(BF16),
                    (((1,), (1,)), ((), ())),
                    preferred_element_type=F32,
                )
                queries = queries + q * jnp.exp(log)
                total, log = jnp.exp(own_log) * total + update, log + own_log
        coarse, rest = two_parts(inner + tall(near).T)
        rows = coarse + pltpu.roll(rest, 16, 1)
        info = jnp.where(lane < AT_ROUTE, 0.0, stacked_rows(split_log(log)) + facts)
        for g in range(HD // PART):
            at = g * PART
            near = rows[at : at + 8] + pltpu.roll(rows[at + 8 : at + PART], 32, 1)
            out_ref[i * (HD // PART) + g] = jnp.concatenate(
                [total[at : at + PART], info + near, queries], axis=0
            ).astype(BF16)


def scan_kernel(msg_ref, out_ref, facts_ref):
    state = jnp.zeros((PART, HD), F32)
    lane = lax.broadcasted_iota(jnp.int32, (16, HD), 1)
    states, queries = [], []
    near = [jnp.zeros((PART, HD), F32) for _ in range(2)]
    facts = [jnp.zeros((8, HD), F32) for _ in range(5)]
    for z in range(Z):
        states.append(state)
        part = msg_ref[z].astype(F32)
        info = part[16:24]
        queries.append(part[24:40])
        half, shift = z // 8, z % 8 * 16
        rows = jnp.concatenate([info, pltpu.roll(info, HD - 32, 1)], axis=0)
        rows = jnp.where(lane < 16, rows + pltpu.roll(rows, HD - 16, 1), 0.0)
        near[half] = near[half] + (pltpu.roll(rows, shift, 1) if shift else rows)
        for b in range(2):
            only = jnp.where(lane[:8] // 16 == AT_ROUTE // 16 + b, info, 0.0)
            move = (shift - AT_ROUTE - b * 16) % HD
            place = half * 2 + b
            facts[place] = facts[place] + (pltpu.roll(only, move, 1) if move else only)
        only = jnp.where(lane[:8] // MROWS == AT_MINE // MROWS, info, 0.0)
        move = (z * MROWS - AT_MINE) % HD
        facts[4] = facts[4] + (pltpu.roll(only, move, 1) if move else only)
        factor = jnp.exp(joined_log(part, PART))[:, AT_ROUTE : AT_ROUTE + 1]
        state = factor * state + part[:PART]
    far = lax.dot_general(
        jnp.concatenate(states, axis=0).astype(BF16),
        jnp.concatenate(queries, axis=0).astype(BF16),
        (((1,), (1,)), ((), ())),
        preferred_element_type=F32,
    )
    row = lax.broadcasted_iota(jnp.int32, far.shape, 0)
    column = lax.broadcasted_iota(jnp.int32, far.shape, 1)
    far = jnp.where(row // 16 == column // 16, far, 0.0)
    total = jnp.concatenate(near, axis=1)
    for z in range(Z):
        total = total + far[z * PART : (z + 1) * PART]
    for z in range(Z):
        out_ref[z] = jnp.concatenate(
            [states[z], total[:, :HD], total[:, HD:]], axis=0
        ).astype(BF16)
    facts_ref[...] = jnp.concatenate(facts, axis=1)


def expand_kernel(back_ref, msg_ref, gain_ref, facts_ref, state_ref, slots_ref):
    gain = gain_ref[:, :HD]
    for x in range(1, X):
        gain = jnp.where(lax.axis_index("x") == x, gain_ref[:, x * HD : (x + 1) * HD], gain)
    back = [back_ref[c].astype(F32) for c in range(Z)]
    each = Z // OWN
    state, rows = [], []
    for i in range(OWN):
        mine = back[i * each : (i + 1) * each]
        state.append(jnp.concatenate([part[:PART] for part in mine], axis=0))
        for half in range(2):
            first = PART * (1 + half)
            o = jnp.concatenate([part[first : first + PART] for part in mine], axis=0).T
            scale = lax.rsqrt(jnp.mean(o * o, axis=1, keepdims=True) + 1e-6)
            rows.append((o * scale * gain).astype(BF16))
    index = lax.broadcasted_iota(jnp.int32, (EXPERTS * HD, 2 * HD), 0)
    lane = lax.broadcasted_iota(jnp.int32, (1, 2 * HD), 1)
    place = lane // HALF % X * 32 + lane % HD // 16 * CAP
    for half in range(2):
        (first, second), _ = slot_rows(
            facts_ref[:, half * 2 * HD : (half + 1) * 2 * HD], place, HD
        )
        chosen = jnp.where((index == first) | (index == second), 1.0, 0.0).astype(BF16)
        both = jnp.concatenate([rows[half], rows[2 + half]], axis=0)
        sent = jnp.dot(chosen, both, preferred_element_type=F32).astype(BF16)
        for e in range(EXPERTS):
            for x in range(X):
                at = e * HD + x * 32
                slots_ref[e, pl.ds(x * SLOTS + half * 32, 32)] = sent[at : at + 32]
    for x in range(X):
        state_ref[x] = jnp.concatenate(state, axis=0).astype(BF16)
        if x < X - 1:
            part = msg_ref[x].astype(F32)
            for i in range(OWN):
                factor = jnp.exp(joined_log(part, AT_LOGS + 4 * i))
                state[i] = factor * state[i] + part[i * HD : (i + 1) * HD]


def attention_kernel(q_ref, k_ref, v_ref, run_ref, state_ref, gain_ref, out_ref):
    running = run_ref[...]
    columns = running.T
    for pair in range(PAIRS):
        b, cols = pair // HEADS, pl.ds(pair % HEADS * HD, HD)
        q, column = q_ref[b, :, cols], columns[:, pair : pair + 1]
        state = state_ref[pair % HEADS, b * HD : (b + 1) * HD]
        weights = fading_scores(q, k_ref[b, :, cols], column, running[pair : pair + 1])
        decayed = (q.astype(F32) * jnp.exp(column)).astype(BF16)
        o = jnp.dot(
            weights, v_ref[b, :, cols], preferred_element_type=F32
        ) + lax.dot_general(
            decayed, state, (((1,), (1,)), ((), ())), preferred_element_type=F32
        )
        scale = lax.rsqrt(jnp.mean(o * o, axis=1, keepdims=True) + 1e-6)
        out_ref[b, :, cols] = (o * scale * gain_ref[:, cols]).astype(BF16)


def slot_rows(facts, place, slots):
    rows = []
    for j in range(2):
        code = facts[4 + j : 5 + j].astype(jnp.int32)
        rows.append(code // CAP * slots + code % CAP + place)
    return rows, [facts[6:7], facts[7:8]]


def share_of_hidden(rows, where, step, gate_ref, up_ref):
    x = lax.rem(lax.axis_index("x") + step, X)
    total = None
    for j in range(0, len(rows), 2):
        parts = [pl.ds(pl.multiple_of((where + i) * COLS + x * HD, HD), HD) for i in (j, j + 1)]
        both = jnp.concatenate(
            [jnp.concatenate([gate_ref[p, :], up_ref[p, :]], axis=1) for p in parts], axis=0
        )
        term = jnp.dot(
            jnp.concatenate(rows[j : j + 2], axis=1), both, preferred_element_type=F32
        )
        total = term if total is None else total + term
    return total


def near_kernel(own_ref, left_ref, right_ref, gate_ref, up_ref, out_ref):
    total = None
    for step, ref in ((0, own_ref), (1, right_ref), (X - 1, left_ref)):
        rows = [ref[e] for e in range(EXPERTS)]
        term = share_of_hidden(rows, 0, step, gate_ref, up_ref)
        total = term if total is None else total + term
    out_ref[...] = total


def expert_kernel(sum_ref, first_ref, second_ref, gate_ref, up_ref, down_ref, out_ref):
    half = EXPERTS // 2
    total = sum_ref[...]
    for where, ref in ((0, first_ref), (half, second_ref)):
        rows = [ref[e] for e in range(half)]
        total = total + share_of_hidden(rows, where, 2, gate_ref, up_ref)
    width = gate_ref.shape[1]
    gate, up = total[:, :width], total[:, width:]
    hidden = (gate / (1.0 + jnp.exp(-gate)) * up).astype(BF16)
    for j in range(EXPERTS):
        out = jnp.dot(hidden, down_ref[:, pl.ds(j * COLS, COLS)], preferred_element_type=F32)
        for x in range(X):
            out_ref[x * EXPERTS + j] = out[x * SLOTS : (x + 1) * SLOTS].astype(BF16)


def combine_kernel(parts_ref, facts_ref, out_ref):
    index = lax.broadcasted_iota(jnp.int32, (EXPERTS * SLOTS, GROUP), 0)
    place = lax.broadcasted_iota(jnp.int32, (1, GROUP), 1) // MROWS * CAP
    (first, second), gates = slot_rows(facts_ref[:, 4 * HD :], place, SLOTS)
    mix = jnp.where(index == first, gates[0], 0.0) + jnp.where(index == second, gates[1], 0.0)
    rows = []
    for e in range(EXPERTS):
        total = parts_ref[e].astype(F32)
        for x in range(1, X):
            total = total + parts_ref[x * EXPERTS + e].astype(F32)
        rows.append(total.astype(BF16))
    out_ref[...] = lax.dot_general(
        mix.astype(BF16),
        jnp.concatenate(rows, axis=0),
        (((0,), (0,)), ((), ())),
        preferred_element_type=F32,
    ).astype(BF16)


def sum_kernel(parts_ref, out_ref):
    total = parts_ref[0].astype(F32)
    for i in range(1, parts_ref.shape[0]):
        total = total + parts_ref[i].astype(F32)
    out_ref[...] = total.astype(BF16)


def swap(array, axis):
    return lax.all_to_all(array, axis, 0, 0, tiled=True)


def shift(array, step):
    return lax.ppermute(array, "x", [(x, (x + step) % X) for x in range(X)])


def body(
    queries, keys, values, log_decay, norm_gain, expert_ids, gate_weights, w_gate, w_up, w_down
):
    shape = jax.ShapeDtypeStruct
    decay = jnp.transpose(log_decay, (0, 2, 1))
    gain = norm_gain.reshape(1, COLS)
    running, message = call(
        update_kernel,
        (shape((PAIRS, TOK), F32), shape((X, AT_FACTS + 8, HD), BF16)),
        "update",
        [
            pltpu.VMEM((2, HEADS, TOK), F32),
            pltpu.VMEM((2, FEW, COLS), BF16),
            pltpu.VMEM((2, TOK, COLS), BF16),
            pltpu.VMEM((2, TOK, COLS), BF16),
            pltpu.VMEM((2, MROWS), jnp.int32),
            pltpu.VMEM((2, MROWS), F32),
            pltpu.VMEM((8, HD), F32),
            pltpu.SemaphoreType.DMA((6,)),
        ],
        [True] * 6,
    )(decay, queries, keys, values, expert_ids.T, gate_weights.T)
    message = swap(message, "x")
    groups = call(group_kernel, shape((Z, PART + 24, HD), BF16), "group")(message)
    groups = swap(groups, "z")
    back, facts = call(
        scan_kernel,
        (shape((Z, 3 * PART, HD), BF16), shape((8, 5 * HD), F32)),
        "scan",
    )(groups)
    back = swap(back, "z")
    states, slots = call(
        expand_kernel,
        (shape((X, OWN * HD, HD), BF16), shape((EXPERTS, X * SLOTS, HD), BF16)),
        "expand",
    )(back, message, gain, facts)
    slots = swap(slots, ("y", "core"))
    slots, states = lax.optimization_barrier((slots, states))
    left, right = shift(slots, 1), shift(slots, -1)
    states = swap(states, "x")
    left, right, states = lax.optimization_barrier((left, right, states))
    half = EXPERTS // 2
    first, second = shift(right[:half], -1), shift(left[half:], 1)
    weights = (w_gate[0], w_up[0])
    near = call(near_kernel, shape((X * SLOTS, 2 * HD), F32), "near")(slots, left, right, *weights)
    parts = call(expert_kernel, shape((X * EXPERTS, SLOTS, COLS), BF16), "experts")(
        near, first, second, *weights, w_down[0]
    )
    attn_out = call(attention_kernel, shape((2, TOK, COLS), BF16), "attention")(
        queries, keys, values, running, states, gain
    )
    parts = swap(parts, ("x", "y", "core"))
    parts, attn_out = lax.optimization_barrier((parts, attn_out))
    share = call(combine_kernel, shape((GROUP, COLS), BF16), "combine")(parts, facts)
    share = swap(share.reshape(Z, MROWS, COLS), "z")
    moe_out = call(sum_kernel, shape((MROWS, COLS), BF16), "sum_z")(share)
    return (attn_out, moe_out)


def solution(mesh):
    fine = Mesh(mesh.devices.reshape(Z, X, Y, CORE), ("z", "x", "y", "core"))
    seq, expert = ("z", "x"), ("y", "core")
    placed = (
        P(None, seq, expert),
        P(None, seq, expert),
        P(None, seq, expert),
        P(None, seq, expert),
        P(expert),
        P(seq, None),
        P(seq, None),
        P(expert, None, seq),
        P(expert, None, seq),
        P(expert, seq, None),
    )
    return jax.shard_map(
        body,
        mesh=fine,
        in_specs=placed,
        out_specs=(P(None, seq, expert), P(seq, expert)),
        check_vma=False,
    )
```

```python
import jax
import jax.numpy as jnp
from jax import lax
from jax.experimental import pallas as pl
from jax.experimental.pallas import tpu as pltpu
from jax.sharding import Mesh
from jax.sharding import PartitionSpec as P

HD = 128
HEADS = 4
PAIRS = 8
TOK = 256
Z, X, Y, CORE = 16, 4, 4, 2
EXPERTS = Y * CORE
MROWS = 8
CAP = 4
COLS = HEADS * HD
OWN = PAIRS // X
PART = OWN * HD // Z
SLOTS = Z * CAP
PIECE = OWN * HD // (X * EXPERTS)
HALF = MROWS // 2
FEW = 16
GROUP = Z * MROWS
AT_LOGS = OWN * HD
AT_Q = AT_LOGS + 8
AT_LOCAL = AT_Q + 8
AT_FACTS = AT_LOCAL + 16
AT_ROUTE = 64
AT_MINE = 96
F32 = jnp.float32
BF16 = jnp.bfloat16


def call(kernel, out, name, scratch=(), places=None):
    vmem = pl.BlockSpec(memory_space=pltpu.VMEM)
    specs = {}
    if places:
        specs["in_specs"] = [pl.BlockSpec(memory_space=pl.ANY) if p else vmem for p in places]
    return pl.pallas_call(
        kernel,
        out_shape=out,
        out_specs=jax.tree.map(lambda _: vmem, out),
        scratch_shapes=scratch,
        compiler_params=pltpu.CompilerParams(vmem_limit_bytes=(56 if places else 40) * 2**20),
        name=name,
        **specs,
    )


def split_log(log):
    first = jnp.floor(log * 0.125) * 8.0
    rest = log - first
    second = jnp.floor(rest * 32.0) * (1.0 / 32.0)
    rest = rest - second
    third = jnp.floor(rest * 8192.0) * (1.0 / 8192.0)
    return first, second, third, rest - third


def stacked_rows(rows):
    index = lax.broadcasted_iota(jnp.int32, (8, HD), 0)
    total = jnp.zeros((8, HD), F32)
    for i, row in enumerate(rows):
        total = jnp.where(index == i, jnp.broadcast_to(row, (8, HD)), total)
    return total


def joined_log(rows, first):
    return (rows[first : first + 1] + rows[first + 1 : first + 2]) + (
        rows[first + 2 : first + 3] + rows[first + 3 : first + 4]
    )


def prefix_sums(rows):
    lane = lax.broadcasted_iota(jnp.int32, rows.shape, 1)
    shift = 1
    while shift < TOK:
        rows = rows + jnp.where(lane >= shift, pltpu.roll(rows, shift, 1), 0.0)
        shift *= 2
    return rows


def fading_scores(q, k, column, row):
    scores = lax.dot_general(q, k, (((1,), (1,)), ((), ())), preferred_element_type=F32)
    causal = lax.broadcasted_iota(jnp.int32, scores.shape, 0) >= lax.broadcasted_iota(
        jnp.int32, scores.shape, 1
    )
    fading = jnp.exp(jnp.minimum(column - row, 0.0))
    return jnp.where(causal, scores * fading, 0.0).astype(BF16)


def beside(one, two):
    row = lax.broadcasted_iota(jnp.int32, one.shape, 0)
    return jnp.where(row < HALF, one, pltpu.roll(two, HALF, 0))


def two_parts(array):
    coarse = array.astype(BF16).astype(F32)
    return coarse, array - coarse


def route_facts(ids_ref, gates_ref, facts_ref):
    facts_ref[...] = jnp.zeros((8, HD), F32)
    facts_ref[0:2, 0:MROWS] = ids_ref[...].astype(F32)
    facts_ref[6:8, 0:MROWS] = gates_ref[...]
    names = facts_ref[0:2, :]
    lane = lax.broadcasted_iota(jnp.int32, (2, HD), 1)
    choice = lax.broadcasted_iota(jnp.int32, (2, HD), 0)
    slots = jnp.where((choice == 1) & (names[0:1] == names[1:2]), 1.0, 0.0)
    for t in range(MROWS - 1):
        for c in range(2):
            same = (names[c : c + 1, t : t + 1] == names) & (lane > t)
            slots = slots + jnp.where(same, 1.0, 0.0)
    facts_ref[4:6, :] = jnp.where(lane < MROWS, names * float(CAP) + slots, 0.0)
    facts_ref[0:2, :] = jnp.zeros((2, HD), F32)


def update_kernel(*refs):
    sources, (run_ref, msg_ref), fetched = refs[:6], refs[6:8], refs[8:14]
    facts_ref, semaphores = refs[14:]
    copies = []
    for i, (source, target) in enumerate(zip(sources, fetched)):
        part = source.at[:, pl.ds(0, FEW)] if i == 1 else source
        copies.append(pltpu.make_async_copy(part, target, semaphores.at[i]))
    for copy in copies:
        copy.start()
    decay_ref, q_ref, k_ref, v_ref, ids_ref, gates_ref = fetched
    for i in (0, 4, 5):
        copies[i].wait()
    running = prefix_sums(jnp.concatenate([decay_ref[0], decay_ref[1]], axis=0))
    run_ref[...] = running
    end = running[:, TOK - 1 :]
    to_end = jnp.exp(end - running).T
    columns = running.T[:FEW]
    route_facts(ids_ref, gates_ref, facts_ref)
    for i in (1, 2, 3):
        copies[i].wait()
    for owner in range(X):
        parts, logs, qs, locals_ = [], [], [], []
        for i in range(OWN):
            b, pair, cols = i, i * HEADS + owner, pl.ds(owner * HD, HD)
            decayed = (k_ref[b, :, cols].astype(F32) * to_end[:, pair : pair + 1]).astype(BF16)
            parts.append(
                lax.dot_general(
                    v_ref[b, :, cols], decayed, (((0,), (0,)), ((), ())), preferred_element_type=F32
                )
            )
            logs += [jnp.broadcast_to(p, (1, HD)) for p in split_log(end[pair : pair + 1])]
            q, column = q_ref[b, :FEW, cols], columns[:, pair : pair + 1]
            weights = fading_scores(
                q, k_ref[b, :FEW, cols], column, running[pair : pair + 1, :FEW]
            )
            local = jnp.dot(weights, v_ref[b, :FEW, cols], preferred_element_type=F32)
            locals_.append(local[:8])
            qs.append((q.astype(F32) * jnp.exp(column))[:8])
        local = two_parts(beside(*locals_))
        msg_ref[owner] = jnp.concatenate(
            parts + [stacked_rows(logs), beside(*qs), local[0], local[1], facts_ref[...]], axis=0
        ).astype(BF16)


def placed(rows, i, x):
    row = lax.broadcasted_iota(jnp.int32, rows.shape, 0)
    moved = rows if i == x % 2 else pltpu.roll(rows, HALF, 0)
    moved = jnp.where(row // HALF == x % 2, moved, 0.0)
    zero = jnp.zeros_like(moved)
    return jnp.concatenate([moved, zero] if x < 2 else [zero, moved], axis=0)


def tall(rows):
    return jnp.concatenate([rows, jnp.zeros((HD - rows.shape[0], HD), F32)], axis=0)


def group_kernel(msg_ref, out_ref):
    lane = lax.broadcasted_iota(jnp.int32, (8, HD), 1)
    facts = jnp.zeros((8, HD), F32)
    for x in range(X):
        own = msg_ref[x].astype(F32)[AT_FACTS:]
        for b in range(2):
            only = jnp.where(lane // HALF == b, own, 0.0)
            shift = b * 16 + x * HALF - b * HALF
            facts = facts + pltpu.roll(only, AT_ROUTE + shift, 1)
        mine = jnp.where((lane < MROWS) & (lax.axis_index("x") == x), own, 0.0)
        facts = facts + pltpu.roll(mine, AT_MINE, 1)
    for i in range(OWN):
        total, log, queries, near, inner = None, None, 0.0, 0.0, 0.0
        for x in range(X):
            part = msg_ref[x].astype(F32)
            update = part[i * HD : (i + 1) * HD]
            own_log = joined_log(part, AT_LOGS + 4 * i)
            q = placed(part[AT_Q : AT_Q + 8], i, x)
            local = part[AT_LOCAL : AT_LOCAL + 8] + part[AT_LOCAL + 8 : AT_LOCAL + 16]
            near = near + placed(local, i, x)
            if x == 0:
                queries = q
                total, log = update, own_log
            else:
                inner = inner + lax.dot_general(
                    total.astype(BF16),
                    tall(q).astype(BF16),
                    (((1,), (1,)), ((), ())),
                    preferred_element_type=F32,
                )
                queries = queries + q * jnp.exp(log)
                total, log = jnp.exp(own_log) * total + update, log + own_log
        coarse, rest = two_parts(inner + tall(near).T)
        rows = coarse + pltpu.roll(rest, 16, 1)
        info = jnp.where(lane < AT_ROUTE, 0.0, stacked_rows(split_log(log)) + facts)
        for g in range(HD // PART):
            at = g * PART
            near = rows[at : at + 8] + pltpu.roll(rows[at + 8 : at + PART], 32, 1)
            out_ref[i * (HD // PART) + g] = jnp.concatenate(
                [total[at : at + PART], info + near, queries], axis=0
            ).astype(BF16)


def scan_kernel(msg_ref, out_ref, facts_ref):
    state = jnp.zeros((PART, HD), F32)
    lane = lax.broadcasted_iota(jnp.int32, (16, HD), 1)
    states, queries = [], []
    near = [jnp.zeros((PART, HD), F32) for _ in range(2)]
    facts = [jnp.zeros((8, HD), F32) for _ in range(5)]
    for z in range(Z):
        states.append(state)
        part = msg_ref[z].astype(F32)
        info = part[16:24]
        queries.append(part[24:40])
        half, shift = z // 8, z % 8 * 16
        rows = jnp.concatenate([info, pltpu.roll(info, HD - 32, 1)], axis=0)
        rows = jnp.where(lane < 16, rows + pltpu.roll(rows, HD - 16, 1), 0.0)
        near[half] = near[half] + (pltpu.roll(rows, shift, 1) if shift else rows)
        for b in range(2):
            only = jnp.where(lane[:8] // 16 == AT_ROUTE // 16 + b, info, 0.0)
            move = (shift - AT_ROUTE - b * 16) % HD
            place = half * 2 + b
            facts[place] = facts[place] + (pltpu.roll(only, move, 1) if move else only)
        only = jnp.where(lane[:8] // MROWS == AT_MINE // MROWS, info, 0.0)
        move = (z * MROWS - AT_MINE) % HD
        facts[4] = facts[4] + (pltpu.roll(only, move, 1) if move else only)
        factor = jnp.exp(joined_log(part, PART))[:, AT_ROUTE : AT_ROUTE + 1]
        state = factor * state + part[:PART]
    far = lax.dot_general(
        jnp.concatenate(states, axis=0).astype(BF16),
        jnp.concatenate(queries, axis=0).astype(BF16),
        (((1,), (1,)), ((), ())),
        preferred_element_type=F32,
    )
    row = lax.broadcasted_iota(jnp.int32, far.shape, 0)
    column = lax.broadcasted_iota(jnp.int32, far.shape, 1)
    far = jnp.where(row // 16 == column // 16, far, 0.0)
    total = jnp.concatenate(near, axis=1)
    for z in range(Z):
        total = total + far[z * PART : (z + 1) * PART]
    for z in range(Z):
        out_ref[z] = jnp.concatenate(
            [states[z], total[:, :HD], total[:, HD:]], axis=0
        ).astype(BF16)
    facts_ref[...] = jnp.concatenate(facts, axis=1)


def expand_kernel(back_ref, msg_ref, gain_ref, facts_ref, slots_ref):
    gain = gain_ref[:, :HD]
    for x in range(1, X):
        gain = jnp.where(lax.axis_index("x") == x, gain_ref[:, x * HD : (x + 1) * HD], gain)
    back = [back_ref[c].astype(F32) for c in range(Z)]
    each = Z // OWN
    state, rows = [], []
    for i in range(OWN):
        mine = back[i * each : (i + 1) * each]
        state.append(jnp.concatenate([part[:PART] for part in mine], axis=0))
        for half in range(2):
            first = PART * (1 + half)
            o = jnp.concatenate([part[first : first + PART] for part in mine], axis=0).T
            scale = lax.rsqrt(jnp.mean(o * o, axis=1, keepdims=True) + 1e-6)
            rows.append((o * scale * gain).astype(BF16))
    index = lax.broadcasted_iota(jnp.int32, (EXPERTS * HD, 2 * HD), 0)
    lane = lax.broadcasted_iota(jnp.int32, (1, 2 * HD), 1)
    place = lane // HALF % X * 32 + lane % HD // 16 * CAP
    for half in range(2):
        (first, second), _ = slot_rows(
            facts_ref[:, half * 2 * HD : (half + 1) * 2 * HD], place, HD
        )
        chosen = jnp.where((index == first) | (index == second), 1.0, 0.0).astype(BF16)
        both = jnp.concatenate([rows[half], rows[2 + half]], axis=0)
        sent = jnp.dot(chosen, both, preferred_element_type=F32).astype(BF16)
        for e in range(EXPERTS):
            for x in range(X):
                at = e * HD + x * 32
                for target in range(X):
                    slots_ref[target * EXPERTS + e, pl.ds(x * SLOTS + half * 32, 32)] = sent[
                        at : at + 32
                    ]
    entering = []
    for x in range(X):
        entering.append(jnp.concatenate(state, axis=0))
        if x < X - 1:
            part = msg_ref[x].astype(F32)
            for i in range(OWN):
                factor = jnp.exp(joined_log(part, AT_LOGS + 4 * i))
                state[i] = factor * state[i] + part[i * HD : (i + 1) * HD]
    for m in range(X * EXPERTS):
        pieces = [own[m * PIECE : (m + 1) * PIECE] for own in entering]
        slots_ref[m, pl.ds(X * SLOTS, X * PIECE)] = jnp.concatenate(pieces, axis=0).astype(BF16)


def attention_kernel(q_ref, k_ref, v_ref, run_ref, parts_ref, gain_ref, out_ref):
    running = run_ref[...]
    columns = running.T
    pieces = [parts_ref[m].astype(F32)[SLOTS:] for m in range(X * EXPERTS)]
    each = len(pieces) // 2
    states = [
        jnp.concatenate(pieces[b * each : (b + 1) * each], axis=0).astype(BF16) for b in range(2)
    ]
    for pair in range(PAIRS):
        b, cols = pair // HEADS, pl.ds(pair % HEADS * HD, HD)
        q, column = q_ref[b, :, cols], columns[:, pair : pair + 1]
        state = states[b][:, pair % HEADS * HD : (pair % HEADS + 1) * HD]
        weights = fading_scores(q, k_ref[b, :, cols], column, running[pair : pair + 1])
        decayed = (q.astype(F32) * jnp.exp(column)).astype(BF16)
        o = jnp.dot(
            weights, v_ref[b, :, cols], preferred_element_type=F32
        ) + lax.dot_general(
            decayed, state, (((1,), (1,)), ((), ())), preferred_element_type=F32
        )
        scale = lax.rsqrt(jnp.mean(o * o, axis=1, keepdims=True) + 1e-6)
        out_ref[b, :, cols] = (o * scale * gain_ref[:, cols]).astype(BF16)


def slot_rows(facts, place, slots):
    rows = []
    for j in range(2):
        code = facts[4 + j : 5 + j].astype(jnp.int32)
        rows.append(code // CAP * slots + code % CAP + place)
    return rows, [facts[6:7], facts[7:8]]


def expert_kernel(rows_ref, gate_ref, up_ref, down_ref, out_ref):
    total = None
    for j in range(EXPERTS):
        part = pl.ds(j * COLS, COLS)
        both = jnp.concatenate([gate_ref[part, :], up_ref[part, :]], axis=1)
        rows = [rows_ref[x * EXPERTS + j, : X * SLOTS] for x in range(X)]
        term = jnp.dot(jnp.concatenate(rows, axis=1), both, preferred_element_type=F32)
        total = term if total is None else total + term
    width = gate_ref.shape[1]
    gate, up = total[:, :width], total[:, width:]
    hidden = (gate / (1.0 + jnp.exp(-gate)) * up).astype(BF16)
    for j in range(EXPERTS):
        out = jnp.dot(hidden, down_ref[:, pl.ds(j * COLS, COLS)], preferred_element_type=F32)
        passing = jnp.concatenate(
            [rows_ref[x * EXPERTS + j, X * SLOTS :].astype(F32) for x in range(X)], axis=1
        )
        for x in range(X):
            out_ref[x * EXPERTS + j] = jnp.concatenate(
                [out[x * SLOTS : (x + 1) * SLOTS], passing[x * PIECE : (x + 1) * PIECE]], axis=0
            ).astype(BF16)


def combine_kernel(parts_ref, facts_ref, out_ref):
    index = lax.broadcasted_iota(jnp.int32, (EXPERTS * SLOTS, GROUP), 0)
    place = lax.broadcasted_iota(jnp.int32, (1, GROUP), 1) // MROWS * CAP
    (first, second), gates = slot_rows(facts_ref[:, 4 * HD :], place, SLOTS)
    mix = jnp.where(index == first, gates[0], 0.0) + jnp.where(index == second, gates[1], 0.0)
    rows = []
    for e in range(EXPERTS):
        total = parts_ref[e, :SLOTS].astype(F32)
        for x in range(1, X):
            total = total + parts_ref[x * EXPERTS + e, :SLOTS].astype(F32)
        rows.append(total.astype(BF16))
    out_ref[...] = lax.dot_general(
        mix.astype(BF16),
        jnp.concatenate(rows, axis=0),
        (((0,), (0,)), ((), ())),
        preferred_element_type=F32,
    ).astype(BF16)


def sum_kernel(parts_ref, out_ref):
    total = parts_ref[0].astype(F32)
    for i in range(1, parts_ref.shape[0]):
        total = total + parts_ref[i].astype(F32)
    out_ref[...] = total.astype(BF16)


def swap(array, axis):
    return lax.all_to_all(array, axis, 0, 0, tiled=True)


def body(
    queries, keys, values, log_decay, norm_gain, expert_ids, gate_weights, w_gate, w_up, w_down
):
    shape = jax.ShapeDtypeStruct
    decay = jnp.transpose(log_decay, (0, 2, 1))
    gain = norm_gain.reshape(1, COLS)
    running, message = call(
        update_kernel,
        (shape((PAIRS, TOK), F32), shape((X, AT_FACTS + 8, HD), BF16)),
        "update",
        [
            pltpu.VMEM((2, HEADS, TOK), F32),
            pltpu.VMEM((2, FEW, COLS), BF16),
            pltpu.VMEM((2, TOK, COLS), BF16),
            pltpu.VMEM((2, TOK, COLS), BF16),
            pltpu.VMEM((2, MROWS), jnp.int32),
            pltpu.VMEM((2, MROWS), F32),
            pltpu.VMEM((8, HD), F32),
            pltpu.SemaphoreType.DMA((6,)),
        ],
        [True] * 6,
    )(decay, queries, keys, values, expert_ids.T, gate_weights.T)
    message = swap(message, "x")
    groups = call(group_kernel, shape((Z, PART + 24, HD), BF16), "group")(message)
    groups = swap(groups, "z")
    back, facts = call(
        scan_kernel,
        (shape((Z, 3 * PART, HD), BF16), shape((8, 5 * HD), F32)),
        "scan",
    )(groups)
    back = swap(back, "z")
    slots = call(
        expand_kernel, shape((X * EXPERTS, X * SLOTS + X * PIECE, HD), BF16), "expand"
    )(back, message, gain, facts)
    slots = swap(slots, ("x", "y", "core"))
    parts = call(expert_kernel, shape((X * EXPERTS, SLOTS + PIECE, COLS), BF16), "experts")(
        slots, w_gate[0], w_up[0], w_down[0]
    )
    parts = swap(parts, ("x", "y", "core"))
    attn_out = call(attention_kernel, shape((2, TOK, COLS), BF16), "attention")(
        queries, keys, values, running, parts, gain
    )
    share = call(combine_kernel, shape((GROUP, COLS), BF16), "combine")(parts, facts)
    share = swap(share.reshape(Z, MROWS, COLS), "z")
    moe_out = call(sum_kernel, shape((MROWS, COLS), BF16), "sum_z")(share)
    return (attn_out, moe_out)


def solution(mesh):
    fine = Mesh(mesh.devices.reshape(Z, X, Y, CORE), ("z", "x", "y", "core"))
    seq, expert = ("z", "x"), ("y", "core")
    placed = (
        P(None, seq, expert),
        P(None, seq, expert),
        P(None, seq, expert),
        P(None, seq, expert),
        P(expert),
        P(seq, None),
        P(seq, None),
        P(expert, None, seq),
        P(expert, None, seq),
        P(expert, seq, None),
    )
    return jax.shard_map(
        body,
        mesh=fine,
        in_specs=placed,
        out_specs=(P(None, seq, expert), P(seq, expert)),
        check_vma=False,
    )
```

```python
import jax
import jax.numpy as jnp
from jax import lax
from jax.experimental import pallas as pl
from jax.experimental.pallas import tpu as pltpu
from jax.sharding import Mesh
from jax.sharding import PartitionSpec as P

HD = 128
HEADS = 4
PAIRS = 8
TOK = 256
Z, X, Y, CORE = 16, 4, 4, 2
EXPERTS = Y * CORE
MROWS = 8
CAP = 4
COLS = HEADS * HD
OWN = PAIRS // X
PART = OWN * HD // Z
SLOTS = Z * CAP
PIECE = OWN * HD // (X * EXPERTS)
HALF = MROWS // 2
FEW = 16
GROUP = Z * MROWS
AT_LOGS = OWN * HD
AT_Q = AT_LOGS + 8
AT_LOCAL = AT_Q + 8
AT_FACTS = AT_LOCAL + 16
MSG = AT_FACTS + 16
AT_ROUTE = 64
AT_MINE = 96
F32 = jnp.float32
BF16 = jnp.bfloat16


def call(kernel, out, name, scratch=(), places=None, results=None):
    vmem, own = pl.BlockSpec(memory_space=pltpu.VMEM), pl.BlockSpec(memory_space=pl.ANY)
    specs = {"out_specs": jax.tree.map(lambda _: vmem, out)}
    if places:
        specs["in_specs"] = [own if p else vmem for p in places]
    if results:
        specs["out_specs"] = tuple(own if p else vmem for p in results)
    return pl.pallas_call(
        kernel,
        out_shape=out,
        scratch_shapes=scratch,
        compiler_params=pltpu.CompilerParams(vmem_limit_bytes=(56 if places else 40) * 2**20),
        name=name,
        **specs,
    )


def split_log(log):
    first = jnp.floor(log * 0.125) * 8.0
    rest = log - first
    second = jnp.floor(rest * 32.0) * (1.0 / 32.0)
    rest = rest - second
    third = jnp.floor(rest * 8192.0) * (1.0 / 8192.0)
    return first, second, third, rest - third


def stacked_rows(rows):
    index = lax.broadcasted_iota(jnp.int32, (8, HD), 0)
    total = jnp.zeros((8, HD), F32)
    for i, row in enumerate(rows):
        total = jnp.where(index == i, jnp.broadcast_to(row, (8, HD)), total)
    return total


def joined_log(rows, first):
    return (rows[first : first + 1] + rows[first + 1 : first + 2]) + (
        rows[first + 2 : first + 3] + rows[first + 3 : first + 4]
    )


def prefix_sums(rows):
    lane = lax.broadcasted_iota(jnp.int32, rows.shape, 1)
    shift = 1
    while shift < TOK:
        rows = rows + jnp.where(lane >= shift, pltpu.roll(rows, shift, 1), 0.0)
        shift *= 2
    return rows


def fading_scores(q, k, column, row):
    scores = lax.dot_general(q, k, (((1,), (1,)), ((), ())), preferred_element_type=F32)
    causal = lax.broadcasted_iota(jnp.int32, scores.shape, 0) >= lax.broadcasted_iota(
        jnp.int32, scores.shape, 1
    )
    fading = jnp.exp(jnp.minimum(column - row, 0.0))
    return jnp.where(causal, scores * fading, 0.0).astype(BF16)


def beside(one, two):
    row = lax.broadcasted_iota(jnp.int32, one.shape, 0)
    return jnp.where(row < HALF, one, pltpu.roll(two, HALF, 0))


def two_parts(array):
    coarse = array.astype(BF16).astype(F32)
    return coarse, array - coarse


def route_facts(ids_ref, gates_ref, facts_ref):
    facts_ref[...] = jnp.zeros((8, HD), F32)
    facts_ref[0:2, 0:MROWS] = ids_ref[...].astype(F32)
    facts_ref[6:8, 0:MROWS] = gates_ref[...]
    names = facts_ref[0:2, :]
    lane = lax.broadcasted_iota(jnp.int32, (2, HD), 1)
    choice = lax.broadcasted_iota(jnp.int32, (2, HD), 0)
    slots = jnp.where((choice == 1) & (names[0:1] == names[1:2]), 1.0, 0.0)
    for t in range(MROWS - 1):
        for c in range(2):
            same = (names[c : c + 1, t : t + 1] == names) & (lane > t)
            slots = slots + jnp.where(same, 1.0, 0.0)
    facts_ref[4:6, :] = jnp.where(lane < MROWS, names * float(CAP) + slots, 0.0)
    facts_ref[0:2, :] = jnp.zeros((2, HD), F32)


def update_kernel(*refs):
    sources, (run_ref, msg_hbm), fetched = refs[:6], refs[6:8], refs[8:14]
    msg_ref, facts_ref, semaphores = refs[14:]

    def copy(i, source, target):
        return pltpu.make_async_copy(source, target, semaphores.at[i])

    decay_ref, q_ref, k_ref, v_ref, ids_ref, gates_ref = fetched
    first = [copy(i, sources[i], fetched[i]) for i in (0, 4, 5)]
    first.append(copy(1, sources[1].at[:, pl.ds(0, FEW)], q_ref))
    halves = [
        [copy(6 + 2 * b + j, sources[2 + j].at[b], fetched[2 + j].at[b]) for j in range(2)]
        for b in range(2)
    ]
    for fetch in first + halves[0] + halves[1]:
        fetch.start()
    for fetch in first:
        fetch.wait()
    running = prefix_sums(jnp.concatenate([decay_ref[0], decay_ref[1]], axis=0))
    run_ref[...] = running
    end = running[:, TOK - 1 :]
    to_end = jnp.exp(end - running).T
    columns = running.T[:FEW]
    route_facts(ids_ref, gates_ref, facts_ref)
    logs, qs, locals_ = ([[] for _ in range(X)] for _ in range(3))
    sent = []
    for b in range(OWN):
        for fetch in halves[b]:
            fetch.wait()
        for owner in range(X):
            pair, cols = b * HEADS + owner, pl.ds(owner * HD, HD)
            decayed = (k_ref[b, :, cols].astype(F32) * to_end[:, pair : pair + 1]).astype(BF16)
            msg_ref[owner, pl.ds(b * HD, HD)] = lax.dot_general(
                v_ref[b, :, cols], decayed, (((0,), (0,)), ((), ())), preferred_element_type=F32
            ).astype(BF16)
            logs[owner] += [jnp.broadcast_to(p, (1, HD)) for p in split_log(end[pair : pair + 1])]
            q, column = q_ref[b, :, cols], columns[:, pair : pair + 1]
            weights = fading_scores(
                q, k_ref[b, :FEW, cols], column, running[pair : pair + 1, :FEW]
            )
            local = jnp.dot(weights, v_ref[b, :FEW, cols], preferred_element_type=F32)
            locals_[owner].append(local[:8])
            qs[owner].append((q.astype(F32) * jnp.exp(column))[:8])
        if b == OWN - 1:
            for owner in range(X):
                local = two_parts(beside(*locals_[owner]))
                facts = facts_ref[...]
                msg_ref[owner, pl.ds(AT_LOGS, MSG - AT_LOGS)] = jnp.concatenate(
                    [
                        stacked_rows(logs[owner]),
                        beside(*qs[owner]),
                        local[0],
                        local[1],
                        facts,
                        jnp.zeros_like(facts),
                    ],
                    axis=0,
                ).astype(BF16)
        rows = pl.ds(b * HD, HD if b < OWN - 1 else MSG - b * HD)
        sent.append(copy(10 + b, msg_ref.at[:, rows], msg_hbm.at[:, rows]))
        sent[-1].start()
    for send in sent:
        send.wait()


def placed(rows, i, x):
    row = lax.broadcasted_iota(jnp.int32, rows.shape, 0)
    moved = rows if i == x % 2 else pltpu.roll(rows, HALF, 0)
    moved = jnp.where(row // HALF == x % 2, moved, 0.0)
    zero = jnp.zeros_like(moved)
    return jnp.concatenate([moved, zero] if x < 2 else [zero, moved], axis=0)


def tall(rows):
    return jnp.concatenate([rows, jnp.zeros((HD - rows.shape[0], HD), F32)], axis=0)


def group_kernel(msg_ref, out_ref):
    lane = lax.broadcasted_iota(jnp.int32, (8, HD), 1)
    facts = jnp.zeros((8, HD), F32)
    for x in range(X):
        own = msg_ref[x].astype(F32)[AT_FACTS : AT_FACTS + 8]
        for b in range(2):
            only = jnp.where(lane // HALF == b, own, 0.0)
            shift = b * 16 + x * HALF - b * HALF
            facts = facts + pltpu.roll(only, AT_ROUTE + shift, 1)
        mine = jnp.where((lane < MROWS) & (lax.axis_index("x") == x), own, 0.0)
        facts = facts + pltpu.roll(mine, AT_MINE, 1)
    for i in range(OWN):
        total, log, queries, near, inner = None, None, 0.0, 0.0, 0.0
        for x in range(X):
            part = msg_ref[x].astype(F32)
            update = part[i * HD : (i + 1) * HD]
            own_log = joined_log(part, AT_LOGS + 4 * i)
            q = placed(part[AT_Q : AT_Q + 8], i, x)
            local = part[AT_LOCAL : AT_LOCAL + 8] + part[AT_LOCAL + 8 : AT_LOCAL + 16]
            near = near + placed(local, i, x)
            if x == 0:
                queries = q
                total, log = update, own_log
            else:
                inner = inner + lax.dot_general(
                    total.astype(BF16),
                    tall(q).astype(BF16),
                    (((1,), (1,)), ((), ())),
                    preferred_element_type=F32,
                )
                queries = queries + q * jnp.exp(log)
                total, log = jnp.exp(own_log) * total + update, log + own_log
        coarse, rest = two_parts(inner + tall(near).T)
        rows = coarse + pltpu.roll(rest, 16, 1)
        info = jnp.where(lane < AT_ROUTE, 0.0, stacked_rows(split_log(log)) + facts)
        for g in range(HD // PART):
            at = g * PART
            near = rows[at : at + 8] + pltpu.roll(rows[at + 8 : at + PART], 32, 1)
            out_ref[i * (HD // PART) + g] = jnp.concatenate(
                [total[at : at + PART], info + near, queries], axis=0
            ).astype(BF16)


def scan_kernel(msg_ref, out_ref, facts_ref):
    state = jnp.zeros((PART, HD), F32)
    lane = lax.broadcasted_iota(jnp.int32, (16, HD), 1)
    states, queries = [], []
    near = [jnp.zeros((PART, HD), F32) for _ in range(2)]
    facts = [jnp.zeros((8, HD), F32) for _ in range(5)]
    for z in range(Z):
        states.append(state)
        part = msg_ref[z].astype(F32)
        info = part[16:24]
        queries.append(part[24:40])
        half, shift = z // 8, z % 8 * 16
        rows = jnp.concatenate([info, pltpu.roll(info, HD - 32, 1)], axis=0)
        rows = jnp.where(lane < 16, rows + pltpu.roll(rows, HD - 16, 1), 0.0)
        near[half] = near[half] + (pltpu.roll(rows, shift, 1) if shift else rows)
        for b in range(2):
            only = jnp.where(lane[:8] // 16 == AT_ROUTE // 16 + b, info, 0.0)
            move = (shift - AT_ROUTE - b * 16) % HD
            place = half * 2 + b
            facts[place] = facts[place] + (pltpu.roll(only, move, 1) if move else only)
        only = jnp.where(lane[:8] // MROWS == AT_MINE // MROWS, info, 0.0)
        move = (z * MROWS - AT_MINE) % HD
        facts[4] = facts[4] + (pltpu.roll(only, move, 1) if move else only)
        factor = jnp.exp(joined_log(part, PART))[:, AT_ROUTE : AT_ROUTE + 1]
        state = factor * state + part[:PART]
    far = lax.dot_general(
        jnp.concatenate(states, axis=0).astype(BF16),
        jnp.concatenate(queries, axis=0).astype(BF16),
        (((1,), (1,)), ((), ())),
        preferred_element_type=F32,
    )
    row = lax.broadcasted_iota(jnp.int32, far.shape, 0)
    column = lax.broadcasted_iota(jnp.int32, far.shape, 1)
    far = jnp.where(row // 16 == column // 16, far, 0.0)
    total = jnp.concatenate(near, axis=1)
    for z in range(Z):
        total = total + far[z * PART : (z + 1) * PART]
    for z in range(Z):
        out_ref[z] = jnp.concatenate(
            [states[z], total[:, :HD], total[:, HD:]], axis=0
        ).astype(BF16)
    facts_ref[...] = jnp.concatenate(facts, axis=1)


def expand_kernel(back_ref, msg_ref, gain_ref, facts_ref, slots_ref):
    gain = gain_ref[:, :HD]
    for x in range(1, X):
        gain = jnp.where(lax.axis_index("x") == x, gain_ref[:, x * HD : (x + 1) * HD], gain)
    back = [back_ref[c].astype(F32) for c in range(Z)]
    each = Z // OWN
    state, rows = [], []
    for i in range(OWN):
        mine = back[i * each : (i + 1) * each]
        state.append(jnp.concatenate([part[:PART] for part in mine], axis=0))
        for half in range(2):
            first = PART * (1 + half)
            o = jnp.concatenate([part[first : first + PART] for part in mine], axis=0).T
            scale = lax.rsqrt(jnp.mean(o * o, axis=1, keepdims=True) + 1e-6)
            rows.append((o * scale * gain).astype(BF16))
    index = lax.broadcasted_iota(jnp.int32, (EXPERTS * HD, 2 * HD), 0)
    lane = lax.broadcasted_iota(jnp.int32, (1, 2 * HD), 1)
    place = lane // HALF % X * 32 + lane % HD // 16 * CAP
    for half in range(2):
        (first, second), _ = slot_rows(
            facts_ref[:, half * 2 * HD : (half + 1) * 2 * HD], place, HD
        )
        chosen = jnp.where((index == first) | (index == second), 1.0, 0.0).astype(BF16)
        both = jnp.concatenate([rows[half], rows[2 + half]], axis=0)
        sent = jnp.dot(chosen, both, preferred_element_type=F32).astype(BF16)
        for e in range(EXPERTS):
            for x in range(X):
                at = e * HD + x * 32
                for target in range(X):
                    slots_ref[target * EXPERTS + e, pl.ds(x * SLOTS + half * 32, 32)] = sent[
                        at : at + 32
                    ]
    entering = []
    for x in range(X):
        entering.append(jnp.concatenate(state, axis=0))
        if x < X - 1:
            part = msg_ref[x].astype(F32)
            for i in range(OWN):
                factor = jnp.exp(joined_log(part, AT_LOGS + 4 * i))
                state[i] = factor * state[i] + part[i * HD : (i + 1) * HD]
    for m in range(X * EXPERTS):
        pieces = [own[m * PIECE : (m + 1) * PIECE] for own in entering]
        slots_ref[m, pl.ds(X * SLOTS, X * PIECE)] = jnp.concatenate(pieces, axis=0).astype(BF16)


def attention_kernel(q_ref, k_ref, v_ref, run_ref, parts_ref, gain_ref, out_ref):
    running = run_ref[...]
    columns = running.T
    pieces = [parts_ref[m].astype(F32)[SLOTS:] for m in range(X * EXPERTS)]
    each = len(pieces) // 2
    states = [
        jnp.concatenate(pieces[b * each : (b + 1) * each], axis=0).astype(BF16) for b in range(2)
    ]
    for pair in range(PAIRS):
        b, cols = pair // HEADS, pl.ds(pair % HEADS * HD, HD)
        q, column = q_ref[b, :, cols], columns[:, pair : pair + 1]
        state = states[b][:, pair % HEADS * HD : (pair % HEADS + 1) * HD]
        weights = fading_scores(q, k_ref[b, :, cols], column, running[pair : pair + 1])
        decayed = (q.astype(F32) * jnp.exp(column)).astype(BF16)
        o = jnp.dot(
            weights, v_ref[b, :, cols], preferred_element_type=F32
        ) + lax.dot_general(
            decayed, state, (((1,), (1,)), ((), ())), preferred_element_type=F32
        )
        scale = lax.rsqrt(jnp.mean(o * o, axis=1, keepdims=True) + 1e-6)
        out_ref[b, :, cols] = (o * scale * gain_ref[:, cols]).astype(BF16)


def slot_rows(facts, place, slots):
    rows = []
    for j in range(2):
        code = facts[4 + j : 5 + j].astype(jnp.int32)
        rows.append(code // CAP * slots + code % CAP + place)
    return rows, [facts[6:7], facts[7:8]]


def expert_kernel(rows_ref, gate_ref, up_ref, down_ref, out_ref):
    total = None
    for j in range(EXPERTS):
        part = pl.ds(j * COLS, COLS)
        both = jnp.concatenate([gate_ref[part, :], up_ref[part, :]], axis=1)
        rows = [rows_ref[x * EXPERTS + j, : X * SLOTS] for x in range(X)]
        term = jnp.dot(jnp.concatenate(rows, axis=1), both, preferred_element_type=F32)
        total = term if total is None else total + term
    width = gate_ref.shape[1]
    gate, up = total[:, :width], total[:, width:]
    hidden = (gate / (1.0 + jnp.exp(-gate)) * up).astype(BF16)
    for j in range(EXPERTS):
        out = jnp.dot(hidden, down_ref[:, pl.ds(j * COLS, COLS)], preferred_element_type=F32)
        passing = jnp.concatenate(
            [rows_ref[x * EXPERTS + j, X * SLOTS :].astype(F32) for x in range(X)], axis=1
        )
        for x in range(X):
            out_ref[x * EXPERTS + j] = jnp.concatenate(
                [out[x * SLOTS : (x + 1) * SLOTS], passing[x * PIECE : (x + 1) * PIECE]], axis=0
            ).astype(BF16)


def combine_kernel(parts_ref, facts_ref, out_ref):
    index = lax.broadcasted_iota(jnp.int32, (EXPERTS * SLOTS, GROUP), 0)
    place = lax.broadcasted_iota(jnp.int32, (1, GROUP), 1) // MROWS * CAP
    (first, second), gates = slot_rows(facts_ref[:, 4 * HD :], place, SLOTS)
    mix = jnp.where(index == first, gates[0], 0.0) + jnp.where(index == second, gates[1], 0.0)
    rows = []
    for e in range(EXPERTS):
        total = parts_ref[e, :SLOTS].astype(F32)
        for x in range(1, X):
            total = total + parts_ref[x * EXPERTS + e, :SLOTS].astype(F32)
        rows.append(total.astype(BF16))
    out_ref[...] = lax.dot_general(
        mix.astype(BF16),
        jnp.concatenate(rows, axis=0),
        (((0,), (0,)), ((), ())),
        preferred_element_type=F32,
    ).astype(BF16)


def sum_kernel(parts_ref, out_ref):
    total = parts_ref[0].astype(F32)
    for i in range(1, parts_ref.shape[0]):
        total = total + parts_ref[i].astype(F32)
    out_ref[...] = total.astype(BF16)


def swap(array, axis):
    return lax.all_to_all(array, axis, 0, 0, tiled=True)


def body(
    queries, keys, values, log_decay, norm_gain, expert_ids, gate_weights, w_gate, w_up, w_down
):
    shape = jax.ShapeDtypeStruct
    decay = jnp.transpose(log_decay, (0, 2, 1))
    gain = norm_gain.reshape(1, COLS)
    running, message = call(
        update_kernel,
        (shape((PAIRS, TOK), F32), shape((X, MSG, HD), BF16)),
        "update",
        [
            pltpu.VMEM((2, HEADS, TOK), F32),
            pltpu.VMEM((2, FEW, COLS), BF16),
            pltpu.VMEM((2, TOK, COLS), BF16),
            pltpu.VMEM((2, TOK, COLS), BF16),
            pltpu.VMEM((2, MROWS), jnp.int32),
            pltpu.VMEM((2, MROWS), F32),
            pltpu.VMEM((X, MSG, HD), BF16),
            pltpu.VMEM((8, HD), F32),
            pltpu.SemaphoreType.DMA((12,)),
        ],
        [True] * 6,
        [False, True],
    )(decay, queries, keys, values, expert_ids.T, gate_weights.T)
    message = swap(message, "x")
    groups = call(group_kernel, shape((Z, PART + 24, HD), BF16), "group")(message)
    groups = swap(groups, "z")
    back, facts = call(
        scan_kernel,
        (shape((Z, 3 * PART, HD), BF16), shape((8, 5 * HD), F32)),
        "scan",
    )(groups)
    back = swap(back, "z")
    slots = call(
        expand_kernel, shape((X * EXPERTS, X * SLOTS + X * PIECE, HD), BF16), "expand"
    )(back, message, gain, facts)
    slots = swap(slots, ("x", "y", "core"))
    parts = call(expert_kernel, shape((X * EXPERTS, SLOTS + PIECE, COLS), BF16), "experts")(
        slots, w_gate[0], w_up[0], w_down[0]
    )
    parts = swap(parts, ("x", "y", "core"))
    attn_out = call(attention_kernel, shape((2, TOK, COLS), BF16), "attention")(
        queries, keys, values, running, parts, gain
    )
    share = call(combine_kernel, shape((GROUP, COLS), BF16), "combine")(parts, facts)
    share = swap(share.reshape(Z, MROWS, COLS), "z")
    moe_out = call(sum_kernel, shape((MROWS, COLS), BF16), "sum_z")(share)
    return (attn_out, moe_out)


def solution(mesh):
    fine = Mesh(mesh.devices.reshape(Z, X, Y, CORE), ("z", "x", "y", "core"))
    seq, expert = ("z", "x"), ("y", "core")
    placed = (
        P(None, seq, expert),
        P(None, seq, expert),
        P(None, seq, expert),
        P(None, seq, expert),
        P(expert),
        P(seq, None),
        P(seq, None),
        P(expert, None, seq),
        P(expert, None, seq),
        P(expert, seq, None),
    )
    return jax.shard_map(
        body,
        mesh=fine,
        in_specs=placed,
        out_specs=(P(None, seq, expert), P(seq, expert)),
        check_vma=False,
    )
```

```python
import jax
import jax.numpy as jnp
from jax import lax
from jax.experimental import pallas as pl
from jax.experimental.pallas import tpu as pltpu
from jax.sharding import Mesh
from jax.sharding import PartitionSpec as P

HD = 128
HEADS = 4
PAIRS = 8
TOK = 256
Z, X, Y, CORE = 16, 4, 4, 2
EXPERTS = Y * CORE
MROWS = 8
CAP = 4
COLS = HEADS * HD
OWN = PAIRS // X
PART = OWN * HD // Z
SLOTS = Z * CAP
PIECE = OWN * HD // (X * EXPERTS)
HALF = MROWS // 2
FEW = 16
GROUP = Z * MROWS
AT_LOGS = OWN * HD
AT_Q = AT_LOGS + 8
AT_LOCAL = AT_Q + 8
AT_FACTS = AT_LOCAL + 16
AT_ROUTE = 64
AT_MINE = 96
F32 = jnp.float32
BF16 = jnp.bfloat16


def call(kernel, out, name, scratch=(), places=None):
    vmem = pl.BlockSpec(memory_space=pltpu.VMEM)
    specs = {}
    if places:
        specs["in_specs"] = [pl.BlockSpec(memory_space=pl.ANY) if p else vmem for p in places]
    return pl.pallas_call(
        kernel,
        out_shape=out,
        out_specs=jax.tree.map(lambda _: vmem, out),
        scratch_shapes=scratch,
        compiler_params=pltpu.CompilerParams(vmem_limit_bytes=(56 if places else 40) * 2**20),
        name=name,
        **specs,
    )


def split_log(log):
    first = jnp.floor(log * 0.125) * 8.0
    rest = log - first
    second = jnp.floor(rest * 32.0) * (1.0 / 32.0)
    rest = rest - second
    third = jnp.floor(rest * 8192.0) * (1.0 / 8192.0)
    return first, second, third, rest - third


def stacked_rows(rows):
    index = lax.broadcasted_iota(jnp.int32, (8, HD), 0)
    total = jnp.zeros((8, HD), F32)
    for i, row in enumerate(rows):
        total = jnp.where(index == i, jnp.broadcast_to(row, (8, HD)), total)
    return total


def joined_log(rows, first):
    return (rows[first : first + 1] + rows[first + 1 : first + 2]) + (
        rows[first + 2 : first + 3] + rows[first + 3 : first + 4]
    )


def prefix_sums(rows):
    lane = lax.broadcasted_iota(jnp.int32, rows.shape, 1)
    shift = 1
    while shift < TOK:
        rows = rows + jnp.where(lane >= shift, pltpu.roll(rows, shift, 1), 0.0)
        shift *= 2
    return rows


def fading_scores(q, k, column, row):
    scores = lax.dot_general(q, k, (((1,), (1,)), ((), ())), preferred_element_type=F32)
    causal = lax.broadcasted_iota(jnp.int32, scores.shape, 0) >= lax.broadcasted_iota(
        jnp.int32, scores.shape, 1
    )
    fading = jnp.exp(jnp.minimum(column - row, 0.0))
    return jnp.where(causal, scores * fading, 0.0).astype(BF16)


def beside(one, two):
    row = lax.broadcasted_iota(jnp.int32, one.shape, 0)
    return jnp.where(row < HALF, one, pltpu.roll(two, HALF, 0))


def two_parts(array):
    coarse = array.astype(BF16).astype(F32)
    return coarse, array - coarse


def route_facts(ids_ref, gates_ref, facts_ref):
    facts_ref[...] = jnp.zeros((8, HD), F32)
    facts_ref[0:2, 0:MROWS] = ids_ref[...].astype(F32)
    facts_ref[6:8, 0:MROWS] = gates_ref[...]
    names = facts_ref[0:2, :]
    lane = lax.broadcasted_iota(jnp.int32, (2, HD), 1)
    choice = lax.broadcasted_iota(jnp.int32, (2, HD), 0)
    slots = jnp.where((choice == 1) & (names[0:1] == names[1:2]), 1.0, 0.0)
    for t in range(MROWS - 1):
        for c in range(2):
            same = (names[c : c + 1, t : t + 1] == names) & (lane > t)
            slots = slots + jnp.where(same, 1.0, 0.0)
    facts_ref[4:6, :] = jnp.where(lane < MROWS, names * float(CAP) + slots, 0.0)
    facts_ref[0:2, :] = jnp.zeros((2, HD), F32)


def update_kernel(*refs):
    sources, (run_ref, msg_ref), fetched = refs[:6], refs[6:8], refs[8:14]
    facts_ref, semaphores = refs[14:]
    copies = []
    for i, (source, target) in enumerate(zip(sources, fetched)):
        part = source.at[:, pl.ds(0, FEW)] if i == 1 else source
        copies.append(pltpu.make_async_copy(part, target, semaphores.at[i]))
    for copy in copies:
        copy.start()
    decay_ref, q_ref, k_ref, v_ref, ids_ref, gates_ref = fetched
    for i in (0, 4, 5):
        copies[i].wait()
    running = prefix_sums(jnp.concatenate([decay_ref[0], decay_ref[1]], axis=0))
    run_ref[...] = running
    end = running[:, TOK - 1 :]
    to_end = jnp.exp(end - running).T
    columns = running.T[:FEW]
    route_facts(ids_ref, gates_ref, facts_ref)
    for i in (1, 2, 3):
        copies[i].wait()
    for owner in range(X):
        parts, logs, qs, locals_ = [], [], [], []
        for i in range(OWN):
            b, pair, cols = i, i * HEADS + owner, pl.ds(owner * HD, HD)
            decayed = (k_ref[b, :, cols].astype(F32) * to_end[:, pair : pair + 1]).astype(BF16)
            parts.append(
                lax.dot_general(
                    v_ref[b, :, cols], decayed, (((0,), (0,)), ((), ())), preferred_element_type=F32
                )
            )
            logs += [jnp.broadcast_to(p, (1, HD)) for p in split_log(end[pair : pair + 1])]
            q, column = q_ref[b, :FEW, cols], columns[:, pair : pair + 1]
            weights = fading_scores(
                q, k_ref[b, :FEW, cols], column, running[pair : pair + 1, :FEW]
            )
            local = jnp.dot(weights, v_ref[b, :FEW, cols], preferred_element_type=F32)
            locals_.append(local[:8])
            qs.append((q.astype(F32) * jnp.exp(column))[:8])
        local = two_parts(beside(*locals_))
        msg_ref[owner] = jnp.concatenate(
            parts + [stacked_rows(logs), beside(*qs), local[0], local[1], facts_ref[...]], axis=0
        ).astype(BF16)


def placed(rows, i, x):
    row = lax.broadcasted_iota(jnp.int32, rows.shape, 0)
    moved = rows if i == x % 2 else pltpu.roll(rows, HALF, 0)
    moved = jnp.where(row // HALF == x % 2, moved, 0.0)
    zero = jnp.zeros_like(moved)
    return jnp.concatenate([moved, zero] if x < 2 else [zero, moved], axis=0)


def tall(rows):
    return jnp.concatenate([rows, jnp.zeros((HD - rows.shape[0], HD), F32)], axis=0)


def group_kernel(msg_ref, out_ref):
    lane = lax.broadcasted_iota(jnp.int32, (8, HD), 1)
    facts = jnp.zeros((8, HD), F32)
    for x in range(X):
        own = msg_ref[x].astype(F32)[AT_FACTS:]
        for b in range(2):
            only = jnp.where(lane // HALF == b, own, 0.0)
            shift = b * 16 + x * HALF - b * HALF
            facts = facts + pltpu.roll(only, AT_ROUTE + shift, 1)
        mine = jnp.where((lane < MROWS) & (lax.axis_index("x") == x), own, 0.0)
        facts = facts + pltpu.roll(mine, AT_MINE, 1)
    for i in range(OWN):
        total, log, queries, near, inner = None, None, 0.0, 0.0, 0.0
        for x in range(X):
            part = msg_ref[x].astype(F32)
            update = part[i * HD : (i + 1) * HD]
            own_log = joined_log(part, AT_LOGS + 4 * i)
            q = placed(part[AT_Q : AT_Q + 8], i, x)
            local = part[AT_LOCAL : AT_LOCAL + 8] + part[AT_LOCAL + 8 : AT_LOCAL + 16]
            near = near + placed(local, i, x)
            if x == 0:
                queries = q
                total, log = update, own_log
            else:
                inner = inner + lax.dot_general(
                    total.astype(BF16),
                    tall(q).astype(BF16),
                    (((1,), (1,)), ((), ())),
                    preferred_element_type=F32,
                )
                queries = queries + q * jnp.exp(log)
                total, log = jnp.exp(own_log) * total + update, log + own_log
        coarse, rest = two_parts(inner + tall(near).T)
        rows = coarse + pltpu.roll(rest, 16, 1)
        info = jnp.where(lane < AT_ROUTE, 0.0, stacked_rows(split_log(log)) + facts)
        for g in range(HD // PART):
            at = g * PART
            near = rows[at : at + 8] + pltpu.roll(rows[at + 8 : at + PART], 32, 1)
            out_ref[i * (HD // PART) + g] = jnp.concatenate(
                [total[at : at + PART], info + near, queries], axis=0
            ).astype(BF16)


def scan_kernel(msg_ref, out_ref, facts_ref):
    state = jnp.zeros((PART, HD), F32)
    lane = lax.broadcasted_iota(jnp.int32, (16, HD), 1)
    states, queries = [], []
    near = [jnp.zeros((PART, HD), F32) for _ in range(2)]
    facts = [jnp.zeros((8, HD), F32) for _ in range(5)]
    for z in range(Z):
        states.append(state)
        part = msg_ref[z].astype(F32)
        info = part[16:24]
        queries.append(part[24:40])
        half, shift = z // 8, z % 8 * 16
        rows = jnp.concatenate([info, pltpu.roll(info, HD - 32, 1)], axis=0)
        rows = jnp.where(lane < 16, rows + pltpu.roll(rows, HD - 16, 1), 0.0)
        near[half] = near[half] + (pltpu.roll(rows, shift, 1) if shift else rows)
        for b in range(2):
            only = jnp.where(lane[:8] // 16 == AT_ROUTE // 16 + b, info, 0.0)
            move = (shift - AT_ROUTE - b * 16) % HD
            place = half * 2 + b
            facts[place] = facts[place] + (pltpu.roll(only, move, 1) if move else only)
        only = jnp.where(lane[:8] // MROWS == AT_MINE // MROWS, info, 0.0)
        move = (z * MROWS - AT_MINE) % HD
        facts[4] = facts[4] + (pltpu.roll(only, move, 1) if move else only)
        factor = jnp.exp(joined_log(part, PART))[:, AT_ROUTE : AT_ROUTE + 1]
        state = factor * state + part[:PART]
    far = lax.dot_general(
        jnp.concatenate(states, axis=0).astype(BF16),
        jnp.concatenate(queries, axis=0).astype(BF16),
        (((1,), (1,)), ((), ())),
        preferred_element_type=F32,
    )
    row = lax.broadcasted_iota(jnp.int32, far.shape, 0)
    column = lax.broadcasted_iota(jnp.int32, far.shape, 1)
    far = jnp.where(row // 16 == column // 16, far, 0.0)
    total = jnp.concatenate(near, axis=1)
    for z in range(Z):
        total = total + far[z * PART : (z + 1) * PART]
    for z in range(Z):
        out_ref[z] = jnp.concatenate(
            [states[z], total[:, :HD], total[:, HD:]], axis=0
        ).astype(BF16)
    facts_ref[...] = jnp.concatenate(facts, axis=1)


def expand_kernel(back_ref, msg_ref, gain_ref, facts_ref, slots_ref):
    gain = gain_ref[:, :HD]
    for x in range(1, X):
        gain = jnp.where(lax.axis_index("x") == x, gain_ref[:, x * HD : (x + 1) * HD], gain)
    back = [back_ref[c].astype(F32) for c in range(Z)]
    each = Z // OWN
    state, rows = [], []
    for i in range(OWN):
        mine = back[i * each : (i + 1) * each]
        state.append(jnp.concatenate([part[:PART] for part in mine], axis=0))
        for half in range(2):
            first = PART * (1 + half)
            o = jnp.concatenate([part[first : first + PART] for part in mine], axis=0).T
            scale = lax.rsqrt(jnp.mean(o * o, axis=1, keepdims=True) + 1e-6)
            rows.append((o * scale * gain).astype(BF16))
    index = lax.broadcasted_iota(jnp.int32, (EXPERTS * HD, 2 * HD), 0)
    lane = lax.broadcasted_iota(jnp.int32, (1, 2 * HD), 1)
    place = lane // HALF % X * 32 + lane % HD // 16 * CAP
    for half in range(2):
        (first, second), _ = slot_rows(
            facts_ref[:, half * 2 * HD : (half + 1) * 2 * HD], place, HD
        )
        chosen = jnp.where((index == first) | (index == second), 1.0, 0.0).astype(BF16)
        both = jnp.concatenate([rows[half], rows[2 + half]], axis=0)
        sent = jnp.dot(chosen, both, preferred_element_type=F32).astype(BF16)
        for e in range(EXPERTS):
            for x in range(X):
                at = e * HD + x * 32
                for target in range(X):
                    slots_ref[e * X + target, pl.ds(x * SLOTS + half * 32, 32)] = sent[
                        at : at + 32
                    ]
    entering = []
    for x in range(X):
        entering.append(jnp.concatenate(state, axis=0))
        if x < X - 1:
            part = msg_ref[x].astype(F32)
            for i in range(OWN):
                factor = jnp.exp(joined_log(part, AT_LOGS + 4 * i))
                state[i] = factor * state[i] + part[i * HD : (i + 1) * HD]
    for m in range(X * EXPERTS):
        pieces = [own[m * PIECE : (m + 1) * PIECE] for own in entering]
        slots_ref[m, pl.ds(X * SLOTS, X * PIECE)] = jnp.concatenate(pieces, axis=0).astype(BF16)


def attention_kernel(q_ref, k_ref, v_ref, run_ref, parts_ref, gain_ref, out_ref):
    running = run_ref[...]
    columns = running.T
    pieces = [parts_ref[m].astype(F32)[SLOTS:] for m in range(X * EXPERTS)]
    each = len(pieces) // 2
    states = [
        jnp.concatenate(pieces[b * each : (b + 1) * each], axis=0).astype(BF16) for b in range(2)
    ]
    for pair in range(PAIRS):
        b, cols = pair // HEADS, pl.ds(pair % HEADS * HD, HD)
        q, column = q_ref[b, :, cols], columns[:, pair : pair + 1]
        state = states[b][:, pair % HEADS * HD : (pair % HEADS + 1) * HD]
        weights = fading_scores(q, k_ref[b, :, cols], column, running[pair : pair + 1])
        decayed = (q.astype(F32) * jnp.exp(column)).astype(BF16)
        o = jnp.dot(
            weights, v_ref[b, :, cols], preferred_element_type=F32
        ) + lax.dot_general(
            decayed, state, (((1,), (1,)), ((), ())), preferred_element_type=F32
        )
        scale = lax.rsqrt(jnp.mean(o * o, axis=1, keepdims=True) + 1e-6)
        out_ref[b, :, cols] = (o * scale * gain_ref[:, cols]).astype(BF16)


def slot_rows(facts, place, slots):
    rows = []
    for j in range(2):
        code = facts[4 + j : 5 + j].astype(jnp.int32)
        rows.append(code // CAP * slots + code % CAP + place)
    return rows, [facts[6:7], facts[7:8]]


def expert_kernel(rows_ref, gate_ref, up_ref, down_ref, out_ref):
    total = None
    for j in range(EXPERTS):
        part = pl.ds(j * COLS, COLS)
        both = jnp.concatenate([gate_ref[part, :], up_ref[part, :]], axis=1)
        rows = [rows_ref[j * X + x, : X * SLOTS] for x in range(X)]
        term = jnp.dot(jnp.concatenate(rows, axis=1), both, preferred_element_type=F32)
        total = term if total is None else total + term
    width = gate_ref.shape[1]
    gate, up = total[:, :width], total[:, width:]
    hidden = (gate / (1.0 + jnp.exp(-gate)) * up).astype(BF16)
    for j in range(EXPERTS):
        out = jnp.dot(hidden, down_ref[:, pl.ds(j * COLS, COLS)], preferred_element_type=F32)
        passing = jnp.concatenate(
            [rows_ref[j * X + x, X * SLOTS :].astype(F32) for x in range(X)], axis=1
        )
        for x in range(X):
            out_ref[j * X + x] = jnp.concatenate(
                [out[x * SLOTS : (x + 1) * SLOTS], passing[x * PIECE : (x + 1) * PIECE]], axis=0
            ).astype(BF16)


def combine_kernel(parts_ref, facts_ref, out_ref):
    index = lax.broadcasted_iota(jnp.int32, (EXPERTS * SLOTS, GROUP), 0)
    place = lax.broadcasted_iota(jnp.int32, (1, GROUP), 1) // MROWS * CAP
    (first, second), gates = slot_rows(facts_ref[:, 4 * HD :], place, SLOTS)
    mix = jnp.where(index == first, gates[0], 0.0) + jnp.where(index == second, gates[1], 0.0)
    rows = []
    for e in range(EXPERTS):
        total = parts_ref[e * X, :SLOTS].astype(F32)
        for x in range(1, X):
            total = total + parts_ref[e * X + x, :SLOTS].astype(F32)
        rows.append(total.astype(BF16))
    out_ref[...] = lax.dot_general(
        mix.astype(BF16),
        jnp.concatenate(rows, axis=0),
        (((0,), (0,)), ((), ())),
        preferred_element_type=F32,
    ).astype(BF16)


def sum_kernel(parts_ref, out_ref):
    total = parts_ref[0].astype(F32)
    for i in range(1, parts_ref.shape[0]):
        total = total + parts_ref[i].astype(F32)
    out_ref[...] = total.astype(BF16)


def swap(array, axis):
    return lax.all_to_all(array, axis, 0, 0, tiled=True)


def body(
    queries, keys, values, log_decay, norm_gain, expert_ids, gate_weights, w_gate, w_up, w_down
):
    shape = jax.ShapeDtypeStruct
    decay = jnp.transpose(log_decay, (0, 2, 1))
    gain = norm_gain.reshape(1, COLS)
    running, message = call(
        update_kernel,
        (shape((PAIRS, TOK), F32), shape((X, AT_FACTS + 8, HD), BF16)),
        "update",
        [
            pltpu.VMEM((2, HEADS, TOK), F32),
            pltpu.VMEM((2, FEW, COLS), BF16),
            pltpu.VMEM((2, TOK, COLS), BF16),
            pltpu.VMEM((2, TOK, COLS), BF16),
            pltpu.VMEM((2, MROWS), jnp.int32),
            pltpu.VMEM((2, MROWS), F32),
            pltpu.VMEM((8, HD), F32),
            pltpu.SemaphoreType.DMA((6,)),
        ],
        [True] * 6,
    )(decay, queries, keys, values, expert_ids.T, gate_weights.T)
    message = swap(message, "x")
    groups = call(group_kernel, shape((Z, PART + 24, HD), BF16), "group")(message)
    groups = swap(groups, "z")
    back, facts = call(
        scan_kernel,
        (shape((Z, 3 * PART, HD), BF16), shape((8, 5 * HD), F32)),
        "scan",
    )(groups)
    back = swap(back, "z")
    slots = call(
        expand_kernel, shape((X * EXPERTS, X * SLOTS + X * PIECE, HD), BF16), "expand"
    )(back, message, gain, facts)
    slots = swap(slots, ("y", "core", "x"))
    parts = call(expert_kernel, shape((X * EXPERTS, SLOTS + PIECE, COLS), BF16), "experts")(
        slots, w_gate[0], w_up[0], w_down[0]
    )
    parts = swap(parts, ("y", "core", "x"))
    attn_out = call(attention_kernel, shape((2, TOK, COLS), BF16), "attention")(
        queries, keys, values, running, parts, gain
    )
    share = call(combine_kernel, shape((GROUP, COLS), BF16), "combine")(parts, facts)
    share = swap(share.reshape(Z, MROWS, COLS), "z")
    moe_out = call(sum_kernel, shape((MROWS, COLS), BF16), "sum_z")(share)
    return (attn_out, moe_out)


def solution(mesh):
    fine = Mesh(mesh.devices.reshape(Z, X, Y, CORE), ("z", "x", "y", "core"))
    seq, expert = ("z", "x"), ("y", "core")
    placed = (
        P(None, seq, expert),
        P(None, seq, expert),
        P(None, seq, expert),
        P(None, seq, expert),
        P(expert),
        P(seq, None),
        P(seq, None),
        P(expert, None, seq),
        P(expert, None, seq),
        P(expert, seq, None),
    )
    return jax.shard_map(
        body,
        mesh=fine,
        in_specs=placed,
        out_specs=(P(None, seq, expert), P(seq, expert)),
        check_vma=False,
    )
```

```python
import jax
import jax.numpy as jnp
from jax import lax
from jax.experimental import pallas as pl
from jax.experimental.pallas import tpu as pltpu
from jax.sharding import Mesh
from jax.sharding import PartitionSpec as P

HD = 128
HEADS = 4
PAIRS = 8
TOK = 256
Z, X, Y, CORE = 16, 4, 4, 2
EXPERTS = Y * CORE
MROWS = 8
CAP = 4
COLS = HEADS * HD
OWN = PAIRS // X
PART = OWN * HD // Z
SLOTS = Z * CAP
PIECE = OWN * HD // (X * EXPERTS)
HALF = MROWS // 2
FEW = 16
GROUP = Z * MROWS
AT_LOGS = OWN * HD
AT_Q = AT_LOGS + 8
AT_LOCAL = AT_Q + 8
AT_FACTS = AT_LOCAL + 16
AT_ROUTE = 64
AT_MINE = 96
F32 = jnp.float32
BF16 = jnp.bfloat16


def call(kernel, out, name, scratch=(), places=None):
    vmem = pl.BlockSpec(memory_space=pltpu.VMEM)
    specs = {}
    if places:
        specs["in_specs"] = [pl.BlockSpec(memory_space=pl.ANY) if p else vmem for p in places]
    return pl.pallas_call(
        kernel,
        out_shape=out,
        out_specs=jax.tree.map(lambda _: vmem, out),
        scratch_shapes=scratch,
        compiler_params=pltpu.CompilerParams(vmem_limit_bytes=(56 if places else 40) * 2**20),
        name=name,
        **specs,
    )


def split_log(log):
    first = jnp.floor(log * 0.125) * 8.0
    rest = log - first
    second = jnp.floor(rest * 32.0) * (1.0 / 32.0)
    rest = rest - second
    third = jnp.floor(rest * 8192.0) * (1.0 / 8192.0)
    return first, second, third, rest - third


def stacked_rows(rows):
    index = lax.broadcasted_iota(jnp.int32, (8, HD), 0)
    total = jnp.zeros((8, HD), F32)
    for i, row in enumerate(rows):
        total = jnp.where(index == i, jnp.broadcast_to(row, (8, HD)), total)
    return total


def joined_log(rows, first):
    return (rows[first : first + 1] + rows[first + 1 : first + 2]) + (
        rows[first + 2 : first + 3] + rows[first + 3 : first + 4]
    )


def prefix_sums(rows):
    lane = lax.broadcasted_iota(jnp.int32, rows.shape, 1)
    shift = 1
    while shift < TOK:
        rows = rows + jnp.where(lane >= shift, pltpu.roll(rows, shift, 1), 0.0)
        shift *= 2
    return rows


def fading_scores(q, k, column, row):
    scores = lax.dot_general(q, k, (((1,), (1,)), ((), ())), preferred_element_type=F32)
    causal = lax.broadcasted_iota(jnp.int32, scores.shape, 0) >= lax.broadcasted_iota(
        jnp.int32, scores.shape, 1
    )
    fading = jnp.exp(jnp.minimum(column - row, 0.0))
    return jnp.where(causal, scores * fading, 0.0).astype(BF16)


def beside(one, two):
    row = lax.broadcasted_iota(jnp.int32, one.shape, 0)
    return jnp.where(row < HALF, one, pltpu.roll(two, HALF, 0))


def two_parts(array):
    coarse = array.astype(BF16).astype(F32)
    return coarse, array - coarse


def route_facts(ids_ref, gates_ref, facts_ref):
    facts_ref[...] = jnp.zeros((8, HD), F32)
    facts_ref[0:2, 0:MROWS] = ids_ref[...].astype(F32)
    facts_ref[6:8, 0:MROWS] = gates_ref[...]
    names = facts_ref[0:2, :]
    lane = lax.broadcasted_iota(jnp.int32, (2, HD), 1)
    choice = lax.broadcasted_iota(jnp.int32, (2, HD), 0)
    slots = jnp.where((choice == 1) & (names[0:1] == names[1:2]), 1.0, 0.0)
    for t in range(MROWS - 1):
        for c in range(2):
            same = (names[c : c + 1, t : t + 1] == names) & (lane > t)
            slots = slots + jnp.where(same, 1.0, 0.0)
    facts_ref[4:6, :] = jnp.where(lane < MROWS, names * float(CAP) + slots, 0.0)
    facts_ref[0:2, :] = jnp.zeros((2, HD), F32)


def update_kernel(*refs):
    sources, (run_ref, msg_ref), fetched = refs[:6], refs[6:8], refs[8:14]
    facts_ref, semaphores = refs[14:]
    copies = []
    for i, (source, target) in enumerate(zip(sources, fetched)):
        part = source.at[:, pl.ds(0, FEW)] if i == 1 else source
        copies.append(pltpu.make_async_copy(part, target, semaphores.at[i]))
    for copy in copies:
        copy.start()
    decay_ref, q_ref, k_ref, v_ref, ids_ref, gates_ref = fetched
    for i in (0, 4, 5):
        copies[i].wait()
    running = prefix_sums(jnp.concatenate([decay_ref[0], decay_ref[1]], axis=0))
    run_ref[...] = running
    end = running[:, TOK - 1 :]
    to_end = jnp.exp(end - running).T
    columns = running.T[:FEW]
    route_facts(ids_ref, gates_ref, facts_ref)
    for i in (1, 2, 3):
        copies[i].wait()
    for owner in range(X):
        parts, logs, qs, locals_ = [], [], [], []
        for i in range(OWN):
            b, pair, cols = i, i * HEADS + owner, pl.ds(owner * HD, HD)
            decayed = (k_ref[b, :, cols].astype(F32) * to_end[:, pair : pair + 1]).astype(BF16)
            parts.append(
                lax.dot_general(
                    v_ref[b, :, cols], decayed, (((0,), (0,)), ((), ())), preferred_element_type=F32
                )
            )
            logs += [jnp.broadcast_to(p, (1, HD)) for p in split_log(end[pair : pair + 1])]
            q, column = q_ref[b, :FEW, cols], columns[:, pair : pair + 1]
            weights = fading_scores(
                q, k_ref[b, :FEW, cols], column, running[pair : pair + 1, :FEW]
            )
            local = jnp.dot(weights, v_ref[b, :FEW, cols], preferred_element_type=F32)
            locals_.append(local[:8])
            qs.append((q.astype(F32) * jnp.exp(column))[:8])
        local = two_parts(beside(*locals_))
        msg_ref[owner] = jnp.concatenate(
            parts + [stacked_rows(logs), beside(*qs), local[0], local[1], facts_ref[...]], axis=0
        ).astype(BF16)


def placed(rows, i, x):
    row = lax.broadcasted_iota(jnp.int32, rows.shape, 0)
    moved = rows if i == x % 2 else pltpu.roll(rows, HALF, 0)
    moved = jnp.where(row // HALF == x % 2, moved, 0.0)
    zero = jnp.zeros_like(moved)
    return jnp.concatenate([moved, zero] if x < 2 else [zero, moved], axis=0)


def tall(rows):
    return jnp.concatenate([rows, jnp.zeros((HD - rows.shape[0], HD), F32)], axis=0)


def group_kernel(msg_ref, out_ref):
    lane = lax.broadcasted_iota(jnp.int32, (8, HD), 1)
    facts = jnp.zeros((8, HD), F32)
    for x in range(X):
        own = msg_ref[x].astype(F32)[AT_FACTS:]
        for b in range(2):
            only = jnp.where(lane // HALF == b, own, 0.0)
            shift = b * 16 + x * HALF - b * HALF
            facts = facts + pltpu.roll(only, AT_ROUTE + shift, 1)
        mine = jnp.where((lane < MROWS) & (lax.axis_index("x") == x), own, 0.0)
        facts = facts + pltpu.roll(mine, AT_MINE, 1)
    for i in range(OWN):
        total, log, queries, near, inner = None, None, 0.0, 0.0, 0.0
        for x in range(X):
            part = msg_ref[x].astype(F32)
            update = part[i * HD : (i + 1) * HD]
            own_log = joined_log(part, AT_LOGS + 4 * i)
            q = placed(part[AT_Q : AT_Q + 8], i, x)
            local = part[AT_LOCAL : AT_LOCAL + 8] + part[AT_LOCAL + 8 : AT_LOCAL + 16]
            near = near + placed(local, i, x)
            if x == 0:
                queries = q
                total, log = update, own_log
            else:
                inner = inner + lax.dot_general(
                    total.astype(BF16),
                    tall(q).astype(BF16),
                    (((1,), (1,)), ((), ())),
                    preferred_element_type=F32,
                )
                queries = queries + q * jnp.exp(log)
                total, log = jnp.exp(own_log) * total + update, log + own_log
        coarse, rest = two_parts(inner + tall(near).T)
        rows = coarse + pltpu.roll(rest, 16, 1)
        info = jnp.where(lane < AT_ROUTE, 0.0, stacked_rows(split_log(log)) + facts)
        for g in range(HD // PART):
            at = g * PART
            near = rows[at : at + 8] + pltpu.roll(rows[at + 8 : at + PART], 32, 1)
            out_ref[i * (HD // PART) + g] = jnp.concatenate(
                [total[at : at + PART], info + near, queries], axis=0
            ).astype(BF16)


def scan_kernel(msg_ref, out_ref, facts_ref):
    state = jnp.zeros((PART, HD), F32)
    lane = lax.broadcasted_iota(jnp.int32, (16, HD), 1)
    states, queries = [], []
    near = [jnp.zeros((PART, HD), F32) for _ in range(2)]
    facts = [jnp.zeros((8, HD), F32) for _ in range(5)]
    for z in range(Z):
        states.append(state)
        part = msg_ref[z].astype(F32)
        info = part[16:24]
        queries.append(part[24:40])
        half, shift = z // 8, z % 8 * 16
        rows = jnp.concatenate([info, pltpu.roll(info, HD - 32, 1)], axis=0)
        rows = jnp.where(lane < 16, rows + pltpu.roll(rows, HD - 16, 1), 0.0)
        near[half] = near[half] + (pltpu.roll(rows, shift, 1) if shift else rows)
        for b in range(2):
            only = jnp.where(lane[:8] // 16 == AT_ROUTE // 16 + b, info, 0.0)
            move = (shift - AT_ROUTE - b * 16) % HD
            place = half * 2 + b
            facts[place] = facts[place] + (pltpu.roll(only, move, 1) if move else only)
        only = jnp.where(lane[:8] // MROWS == AT_MINE // MROWS, info, 0.0)
        move = (z * MROWS - AT_MINE) % HD
        facts[4] = facts[4] + (pltpu.roll(only, move, 1) if move else only)
        factor = jnp.exp(joined_log(part, PART))[:, AT_ROUTE : AT_ROUTE + 1]
        state = factor * state + part[:PART]
    far = lax.dot_general(
        jnp.concatenate(states, axis=0).astype(BF16),
        jnp.concatenate(queries, axis=0).astype(BF16),
        (((1,), (1,)), ((), ())),
        preferred_element_type=F32,
    )
    row = lax.broadcasted_iota(jnp.int32, far.shape, 0)
    column = lax.broadcasted_iota(jnp.int32, far.shape, 1)
    far = jnp.where(row // 16 == column // 16, far, 0.0)
    total = jnp.concatenate(near, axis=1)
    for z in range(Z):
        total = total + far[z * PART : (z + 1) * PART]
    for z in range(Z):
        out_ref[z] = jnp.concatenate(
            [states[z], total[:, :HD], total[:, HD:]], axis=0
        ).astype(BF16)
    facts_ref[...] = jnp.concatenate(facts, axis=1)


def expand_kernel(back_ref, msg_ref, gain_ref, facts_ref, own_ref, slots_ref):
    gain = gain_ref[:, :HD]
    for x in range(1, X):
        gain = jnp.where(lax.axis_index("x") == x, gain_ref[:, x * HD : (x + 1) * HD], gain)
    back = [back_ref[c].astype(F32) for c in range(Z)]
    each = Z // OWN
    state, rows = [], []
    for i in range(OWN):
        mine = back[i * each : (i + 1) * each]
        state.append(jnp.concatenate([part[:PART] for part in mine], axis=0))
        for half in range(2):
            first = PART * (1 + half)
            o = jnp.concatenate([part[first : first + PART] for part in mine], axis=0).T
            scale = lax.rsqrt(jnp.mean(o * o, axis=1, keepdims=True) + 1e-6)
            rows.append((o * scale * gain).astype(BF16))
    index = lax.broadcasted_iota(jnp.int32, (EXPERTS * HD, 2 * HD), 0)
    lane = lax.broadcasted_iota(jnp.int32, (1, 2 * HD), 1)
    place = lane // HALF % X * 32 + lane % HD // 16 * CAP
    for half in range(2):
        (first, second), _ = slot_rows(
            facts_ref[:, half * 2 * HD : (half + 1) * 2 * HD], place, HD
        )
        chosen = jnp.where((index == first) | (index == second), 1.0, 0.0).astype(BF16)
        both = jnp.concatenate([rows[half], rows[2 + half]], axis=0)
        sent = jnp.dot(chosen, both, preferred_element_type=F32).astype(BF16)
        for e in range(EXPERTS):
            for x in range(X):
                at = e * HD + x * 32
                for target in range(X):
                    slots_ref[target * EXPERTS + e, pl.ds(x * SLOTS + half * 32, 32)] = sent[
                        at : at + 32
                    ]
    entering = []
    for x in range(X):
        entering.append(jnp.concatenate(state, axis=0))
        if x < X - 1:
            part = msg_ref[x].astype(F32)
            for i in range(OWN):
                factor = jnp.exp(joined_log(part, AT_LOGS + 4 * i))
                state[i] = factor * state[i] + part[i * HD : (i + 1) * HD]
    here = lax.axis_index("x")

    def state_on(step):
        there = lax.rem(here + step, X)
        found = entering[0]
        for x in range(1, X):
            found = jnp.where(there == x, entering[x], found)
        return found

    own_ref[...] = state_on(0).astype(BF16)
    others = [state_on(step) for step in range(1, X)]
    for m in range(X * EXPERTS):
        pieces = [other[m * PIECE : (m + 1) * PIECE] for other in others]
        slots_ref[m, pl.ds(X * SLOTS, (X - 1) * PIECE)] = jnp.concatenate(pieces, axis=0).astype(
            BF16
        )


def attention_kernel(q_ref, k_ref, v_ref, run_ref, parts_ref, own_ref, gain_ref, out_ref):
    running = run_ref[...]
    columns = running.T
    here = lax.axis_index("x")
    pieces = [parts_ref[m].astype(F32)[SLOTS:] for m in range(X * EXPERTS)]
    each = len(pieces) // 2
    states = [
        jnp.concatenate(pieces[b * each : (b + 1) * each], axis=0).astype(BF16) for b in range(2)
    ]
    for pair in range(PAIRS):
        b, cols = pair // HEADS, pl.ds(pair % HEADS * HD, HD)
        q, column = q_ref[b, :, cols], columns[:, pair : pair + 1]
        head = pair % HEADS
        state = states[b][:, head * HD : (head + 1) * HD]
        state = jnp.where(here == head, own_ref[b * HD : (b + 1) * HD], state)
        weights = fading_scores(q, k_ref[b, :, cols], column, running[pair : pair + 1])
        decayed = (q.astype(F32) * jnp.exp(column)).astype(BF16)
        o = jnp.dot(
            weights, v_ref[b, :, cols], preferred_element_type=F32
        ) + lax.dot_general(
            decayed, state, (((1,), (1,)), ((), ())), preferred_element_type=F32
        )
        scale = lax.rsqrt(jnp.mean(o * o, axis=1, keepdims=True) + 1e-6)
        out_ref[b, :, cols] = (o * scale * gain_ref[:, cols]).astype(BF16)


def slot_rows(facts, place, slots):
    rows = []
    for j in range(2):
        code = facts[4 + j : 5 + j].astype(jnp.int32)
        rows.append(code // CAP * slots + code % CAP + place)
    return rows, [facts[6:7], facts[7:8]]


def expert_kernel(rows_ref, gate_ref, up_ref, down_ref, out_ref):
    total = None
    for j in range(EXPERTS):
        part = pl.ds(j * COLS, COLS)
        both = jnp.concatenate([gate_ref[part, :], up_ref[part, :]], axis=1)
        rows = [rows_ref[x * EXPERTS + j, : X * SLOTS] for x in range(X)]
        term = jnp.dot(jnp.concatenate(rows, axis=1), both, preferred_element_type=F32)
        total = term if total is None else total + term
    width = gate_ref.shape[1]
    gate, up = total[:, :width], total[:, width:]
    hidden = (gate / (1.0 + jnp.exp(-gate)) * up).astype(BF16)
    for j in range(EXPERTS):
        out = jnp.dot(hidden, down_ref[:, pl.ds(j * COLS, COLS)], preferred_element_type=F32)
        parts = [rows_ref[x * EXPERTS + j, X * SLOTS :].astype(F32) for x in range(X)]
        for x in range(X):
            passing = []
            for source in range(X):
                at = (x - source - 1) % X * PIECE
                piece = parts[source][at : at + PIECE] if source != x else jnp.zeros((PIECE, HD), F32)
                passing.append(piece)
            out_ref[x * EXPERTS + j] = jnp.concatenate(
                [out[x * SLOTS : (x + 1) * SLOTS], jnp.concatenate(passing, axis=1)], axis=0
            ).astype(BF16)


def combine_kernel(parts_ref, facts_ref, out_ref):
    index = lax.broadcasted_iota(jnp.int32, (EXPERTS * SLOTS, GROUP), 0)
    place = lax.broadcasted_iota(jnp.int32, (1, GROUP), 1) // MROWS * CAP
    (first, second), gates = slot_rows(facts_ref[:, 4 * HD :], place, SLOTS)
    mix = jnp.where(index == first, gates[0], 0.0) + jnp.where(index == second, gates[1], 0.0)
    mix = mix.astype(BF16)
    total = None
    for x in range(X):
        rows = jnp.concatenate(
            [parts_ref[x * EXPERTS + e, :SLOTS] for e in range(EXPERTS)], axis=0
        )
        term = lax.dot_general(mix, rows, (((0,), (0,)), ((), ())), preferred_element_type=F32)
        total = term if total is None else total + term
    out_ref[...] = total.astype(BF16)


def sum_kernel(parts_ref, out_ref):
    total = parts_ref[0].astype(F32)
    for i in range(1, parts_ref.shape[0]):
        total = total + parts_ref[i].astype(F32)
    out_ref[...] = total.astype(BF16)


def swap(array, axis):
    return lax.all_to_all(array, axis, 0, 0, tiled=True)


def body(
    queries, keys, values, log_decay, norm_gain, expert_ids, gate_weights, w_gate, w_up, w_down
):
    shape = jax.ShapeDtypeStruct
    decay = jnp.transpose(log_decay, (0, 2, 1))
    gain = norm_gain.reshape(1, COLS)
    running, message = call(
        update_kernel,
        (shape((PAIRS, TOK), F32), shape((X, AT_FACTS + 8, HD), BF16)),
        "update",
        [
            pltpu.VMEM((2, HEADS, TOK), F32),
            pltpu.VMEM((2, FEW, COLS), BF16),
            pltpu.VMEM((2, TOK, COLS), BF16),
            pltpu.VMEM((2, TOK, COLS), BF16),
            pltpu.VMEM((2, MROWS), jnp.int32),
            pltpu.VMEM((2, MROWS), F32),
            pltpu.VMEM((8, HD), F32),
            pltpu.SemaphoreType.DMA((6,)),
        ],
        [True] * 6,
    )(decay, queries, keys, values, expert_ids.T, gate_weights.T)
    message = swap(message, "x")
    groups = call(group_kernel, shape((Z, PART + 24, HD), BF16), "group")(message)
    groups = swap(groups, "z")
    back, facts = call(
        scan_kernel,
        (shape((Z, 3 * PART, HD), BF16), shape((8, 5 * HD), F32)),
        "scan",
    )(groups)
    back = swap(back, "z")
    own, slots = call(
        expand_kernel,
        (
            shape((OWN * HD, HD), BF16),
            shape((X * EXPERTS, X * SLOTS + (X - 1) * PIECE, HD), BF16),
        ),
        "expand",
    )(back, message, gain, facts)
    slots = swap(slots, ("x", "y", "core"))
    parts = call(expert_kernel, shape((X * EXPERTS, SLOTS + PIECE, COLS), BF16), "experts")(
        slots, w_gate[0], w_up[0], w_down[0]
    )
    parts = swap(parts, ("x", "y", "core"))
    attn_out = call(attention_kernel, shape((2, TOK, COLS), BF16), "attention")(
        queries, keys, values, running, parts, own, gain
    )
    share = call(combine_kernel, shape((GROUP, COLS), BF16), "combine")(parts, facts)
    share = swap(share.reshape(Z, MROWS, COLS), "z")
    moe_out = call(sum_kernel, shape((MROWS, COLS), BF16), "sum_z")(share)
    return (attn_out, moe_out)


def solution(mesh):
    fine = Mesh(mesh.devices.reshape(Z, X, Y, CORE), ("z", "x", "y", "core"))
    seq, expert = ("z", "x"), ("y", "core")
    placed = (
        P(None, seq, expert),
        P(None, seq, expert),
        P(None, seq, expert),
        P(None, seq, expert),
        P(expert),
        P(seq, None),
        P(seq, None),
        P(expert, None, seq),
        P(expert, None, seq),
        P(expert, seq, None),
    )
    return jax.shard_map(
        body,
        mesh=fine,
        in_specs=placed,
        out_specs=(P(None, seq, expert), P(seq, expert)),
        check_vma=False,
    )
```

```python
import jax
import jax.numpy as jnp
from jax import lax
from jax.experimental import pallas as pl
from jax.experimental.pallas import tpu as pltpu
from jax.sharding import Mesh
from jax.sharding import PartitionSpec as P

HD = 128
HEADS = 4
PAIRS = 8
TOK = 256
Z, X, Y, CORE = 16, 4, 4, 2
EXPERTS = Y * CORE
MROWS = 8
CAP = 4
COLS = HEADS * HD
OWN = PAIRS // X
PART = OWN * HD // Z
SLOTS = Z * CAP
PIECE = OWN * HD // (X * EXPERTS)
HALF = MROWS // 2
FEW = 16
GROUP = Z * MROWS
AT_LOGS = OWN * HD
AT_Q = AT_LOGS + 8
AT_LOCAL = AT_Q + 8
AT_FACTS = AT_LOCAL + 16
AT_ROUTE = 64
AT_MINE = 96
F32 = jnp.float32
BF16 = jnp.bfloat16


def call(kernel, out, name, scratch=(), places=None):
    vmem = pl.BlockSpec(memory_space=pltpu.VMEM)
    specs = {}
    if places:
        specs["in_specs"] = [pl.BlockSpec(memory_space=pl.ANY) if p else vmem for p in places]
    return pl.pallas_call(
        kernel,
        out_shape=out,
        out_specs=jax.tree.map(lambda _: vmem, out),
        scratch_shapes=scratch,
        compiler_params=pltpu.CompilerParams(vmem_limit_bytes=(56 if places else 40) * 2**20),
        name=name,
        **specs,
    )


def split_log(log):
    first = jnp.floor(log * 0.125) * 8.0
    rest = log - first
    second = jnp.floor(rest * 32.0) * (1.0 / 32.0)
    rest = rest - second
    third = jnp.floor(rest * 8192.0) * (1.0 / 8192.0)
    return first, second, third, rest - third


def stacked_rows(rows):
    index = lax.broadcasted_iota(jnp.int32, (8, HD), 0)
    total = jnp.zeros((8, HD), F32)
    for i, row in enumerate(rows):
        total = jnp.where(index == i, jnp.broadcast_to(row, (8, HD)), total)
    return total


def joined_log(rows, first):
    return (rows[first : first + 1] + rows[first + 1 : first + 2]) + (
        rows[first + 2 : first + 3] + rows[first + 3 : first + 4]
    )


def prefix_sums(rows):
    lane = lax.broadcasted_iota(jnp.int32, rows.shape, 1)
    shift = 1
    while shift < TOK:
        rows = rows + jnp.where(lane >= shift, pltpu.roll(rows, shift, 1), 0.0)
        shift *= 2
    return rows


def fading_scores(q, k, column, row):
    scores = lax.dot_general(q, k, (((1,), (1,)), ((), ())), preferred_element_type=F32)
    causal = lax.broadcasted_iota(jnp.int32, scores.shape, 0) >= lax.broadcasted_iota(
        jnp.int32, scores.shape, 1
    )
    fading = jnp.exp(jnp.minimum(column - row, 0.0))
    return jnp.where(causal, scores * fading, 0.0).astype(BF16)


def beside(one, two):
    row = lax.broadcasted_iota(jnp.int32, one.shape, 0)
    return jnp.where(row < HALF, one, pltpu.roll(two, HALF, 0))


def two_parts(array):
    coarse = array.astype(BF16).astype(F32)
    return coarse, array - coarse


def route_facts(ids_ref, gates_ref, facts_ref):
    facts_ref[...] = jnp.zeros((8, HD), F32)
    facts_ref[0:2, 0:MROWS] = ids_ref[...].astype(F32)
    facts_ref[6:8, 0:MROWS] = gates_ref[...]
    names = facts_ref[0:2, :]
    lane = lax.broadcasted_iota(jnp.int32, (2, HD), 1)
    choice = lax.broadcasted_iota(jnp.int32, (2, HD), 0)
    slots = jnp.where((choice == 1) & (names[0:1] == names[1:2]), 1.0, 0.0)
    for t in range(MROWS - 1):
        for c in range(2):
            same = (names[c : c + 1, t : t + 1] == names) & (lane > t)
            slots = slots + jnp.where(same, 1.0, 0.0)
    facts_ref[4:6, :] = jnp.where(lane < MROWS, names * float(CAP) + slots, 0.0)
    facts_ref[0:2, :] = jnp.zeros((2, HD), F32)


def update_kernel(*refs):
    sources, (run_ref, msg_ref), fetched = refs[:6], refs[6:8], refs[8:14]
    facts_ref, semaphores = refs[14:]
    copies = []
    for i, (source, target) in enumerate(zip(sources, fetched)):
        part = source.at[:, pl.ds(0, FEW)] if i == 1 else source
        copies.append(pltpu.make_async_copy(part, target, semaphores.at[i]))
    for i in (0, 4, 5, 2, 3, 1):
        copies[i].start()
    decay_ref, q_ref, k_ref, v_ref, ids_ref, gates_ref = fetched
    for i in (0, 4, 5):
        copies[i].wait()
    running = prefix_sums(jnp.concatenate([decay_ref[0], decay_ref[1]], axis=0))
    run_ref[...] = running
    end = running[:, TOK - 1 :]
    to_end = jnp.exp(end - running).T
    columns = running.T[:FEW]
    route_facts(ids_ref, gates_ref, facts_ref)
    for i in (1, 2, 3):
        copies[i].wait()
    for owner in range(X):
        parts, logs, qs, locals_ = [], [], [], []
        for i in range(OWN):
            b, pair, cols = i, i * HEADS + owner, pl.ds(owner * HD, HD)
            decayed = (k_ref[b, :, cols].astype(F32) * to_end[:, pair : pair + 1]).astype(BF16)
            parts.append(
                lax.dot_general(
                    v_ref[b, :, cols], decayed, (((0,), (0,)), ((), ())), preferred_element_type=F32
                )
            )
            logs += [jnp.broadcast_to(p, (1, HD)) for p in split_log(end[pair : pair + 1])]
            q, column = q_ref[b, :FEW, cols], columns[:, pair : pair + 1]
            weights = fading_scores(
                q, k_ref[b, :FEW, cols], column, running[pair : pair + 1, :FEW]
            )
            local = jnp.dot(weights, v_ref[b, :FEW, cols], preferred_element_type=F32)
            locals_.append(local[:8])
            qs.append((q.astype(F32) * jnp.exp(column))[:8])
        local = two_parts(beside(*locals_))
        msg_ref[owner] = jnp.concatenate(
            parts + [stacked_rows(logs), beside(*qs), local[0], local[1], facts_ref[...]], axis=0
        ).astype(BF16)


def placed(rows, i, x):
    row = lax.broadcasted_iota(jnp.int32, rows.shape, 0)
    moved = rows if i == x % 2 else pltpu.roll(rows, HALF, 0)
    moved = jnp.where(row // HALF == x % 2, moved, 0.0)
    zero = jnp.zeros_like(moved)
    return jnp.concatenate([moved, zero] if x < 2 else [zero, moved], axis=0)


def tall(rows):
    return jnp.concatenate([rows, jnp.zeros((HD - rows.shape[0], HD), F32)], axis=0)


def group_kernel(msg_ref, out_ref):
    lane = lax.broadcasted_iota(jnp.int32, (8, HD), 1)
    facts = jnp.zeros((8, HD), F32)
    for x in range(X):
        own = msg_ref[x].astype(F32)[AT_FACTS:]
        for b in range(2):
            only = jnp.where(lane // HALF == b, own, 0.0)
            shift = b * 16 + x * HALF - b * HALF
            facts = facts + pltpu.roll(only, AT_ROUTE + shift, 1)
        mine = jnp.where((lane < MROWS) & (lax.axis_index("x") == x), own, 0.0)
        facts = facts + pltpu.roll(mine, AT_MINE, 1)
    for i in range(OWN):
        total, log, queries, near, inner = None, None, 0.0, 0.0, 0.0
        for x in range(X):
            part = msg_ref[x].astype(F32)
            update = part[i * HD : (i + 1) * HD]
            own_log = joined_log(part, AT_LOGS + 4 * i)
            q = placed(part[AT_Q : AT_Q + 8], i, x)
            local = part[AT_LOCAL : AT_LOCAL + 8] + part[AT_LOCAL + 8 : AT_LOCAL + 16]
            near = near + placed(local, i, x)
            if x == 0:
                queries = q
                total, log = update, own_log
            else:
                inner = inner + lax.dot_general(
                    total.astype(BF16),
                    tall(q).astype(BF16),
                    (((1,), (1,)), ((), ())),
                    preferred_element_type=F32,
                )
                queries = queries + q * jnp.exp(log)
                total, log = jnp.exp(own_log) * total + update, log + own_log
        coarse, rest = two_parts(inner + tall(near).T)
        rows = coarse + pltpu.roll(rest, 16, 1)
        info = jnp.where(lane < AT_ROUTE, 0.0, stacked_rows(split_log(log)) + facts)
        for g in range(HD // PART):
            at = g * PART
            near = rows[at : at + 8] + pltpu.roll(rows[at + 8 : at + PART], 32, 1)
            out_ref[i * (HD // PART) + g] = jnp.concatenate(
                [total[at : at + PART], info + near, queries], axis=0
            ).astype(BF16)


def scan_kernel(msg_ref, out_ref, facts_ref):
    state = jnp.zeros((PART, HD), F32)
    lane = lax.broadcasted_iota(jnp.int32, (16, HD), 1)
    states, queries = [], []
    near = [jnp.zeros((PART, HD), F32) for _ in range(2)]
    facts = [jnp.zeros((8, HD), F32) for _ in range(5)]
    for z in range(Z):
        states.append(state)
        part = msg_ref[z].astype(F32)
        info = part[16:24]
        queries.append(part[24:40])
        half, shift = z // 8, z % 8 * 16
        rows = jnp.concatenate([info, pltpu.roll(info, HD - 32, 1)], axis=0)
        rows = jnp.where(lane < 16, rows + pltpu.roll(rows, HD - 16, 1), 0.0)
        near[half] = near[half] + (pltpu.roll(rows, shift, 1) if shift else rows)
        for b in range(2):
            only = jnp.where(lane[:8] // 16 == AT_ROUTE // 16 + b, info, 0.0)
            move = (shift - AT_ROUTE - b * 16) % HD
            place = half * 2 + b
            facts[place] = facts[place] + (pltpu.roll(only, move, 1) if move else only)
        only = jnp.where(lane[:8] // MROWS == AT_MINE // MROWS, info, 0.0)
        move = (z * MROWS - AT_MINE) % HD
        facts[4] = facts[4] + (pltpu.roll(only, move, 1) if move else only)
        factor = jnp.exp(joined_log(part, PART))[:, AT_ROUTE : AT_ROUTE + 1]
        state = factor * state + part[:PART]
    far = lax.dot_general(
        jnp.concatenate(states, axis=0).astype(BF16),
        jnp.concatenate(queries, axis=0).astype(BF16),
        (((1,), (1,)), ((), ())),
        preferred_element_type=F32,
    )
    row = lax.broadcasted_iota(jnp.int32, far.shape, 0)
    column = lax.broadcasted_iota(jnp.int32, far.shape, 1)
    far = jnp.where(row // 16 == column // 16, far, 0.0)
    total = jnp.concatenate(near, axis=1)
    for z in range(Z):
        total = total + far[z * PART : (z + 1) * PART]
    for z in range(Z):
        out_ref[z] = jnp.concatenate(
            [states[z], total[:, :HD], total[:, HD:]], axis=0
        ).astype(BF16)
    facts_ref[...] = jnp.concatenate(facts, axis=1)


def expand_kernel(back_ref, msg_ref, gain_ref, facts_ref, own_ref, slots_ref):
    gain = gain_ref[:, :HD]
    for x in range(1, X):
        gain = jnp.where(lax.axis_index("x") == x, gain_ref[:, x * HD : (x + 1) * HD], gain)
    back = [back_ref[c].astype(F32) for c in range(Z)]
    each = Z // OWN
    state, rows = [], []
    for i in range(OWN):
        mine = back[i * each : (i + 1) * each]
        state.append(jnp.concatenate([part[:PART] for part in mine], axis=0))
        for half in range(2):
            first = PART * (1 + half)
            o = jnp.concatenate([part[first : first + PART] for part in mine], axis=0).T
            scale = lax.rsqrt(jnp.mean(o * o, axis=1, keepdims=True) + 1e-6)
            rows.append((o * scale * gain).astype(BF16))
    index = lax.broadcasted_iota(jnp.int32, (EXPERTS * HD, 2 * HD), 0)
    lane = lax.broadcasted_iota(jnp.int32, (1, 2 * HD), 1)
    place = lane // HALF % X * 32 + lane % HD // 16 * CAP
    for half in range(2):
        (first, second), _ = slot_rows(
            facts_ref[:, half * 2 * HD : (half + 1) * 2 * HD], place, HD
        )
        chosen = jnp.where((index == first) | (index == second), 1.0, 0.0).astype(BF16)
        both = jnp.concatenate([rows[half], rows[2 + half]], axis=0)
        sent = jnp.dot(chosen, both, preferred_element_type=F32).astype(BF16)
        for e in range(EXPERTS):
            for x in range(X):
                at = e * HD + x * 32
                for target in range(X):
                    slots_ref[target * EXPERTS + e, pl.ds(x * SLOTS + half * 32, 32)] = sent[
                        at : at + 32
                    ]
    entering = []
    for x in range(X):
        entering.append(jnp.concatenate(state, axis=0))
        if x < X - 1:
            part = msg_ref[x].astype(F32)
            for i in range(OWN):
                factor = jnp.exp(joined_log(part, AT_LOGS + 4 * i))
                state[i] = factor * state[i] + part[i * HD : (i + 1) * HD]
    here = lax.axis_index("x")

    def state_on(step):
        there = lax.rem(here + step, X)
        found = entering[0]
        for x in range(1, X):
            found = jnp.where(there == x, entering[x], found)
        return found

    own_ref[...] = state_on(0).astype(BF16)
    others = [state_on(step) for step in range(1, X)]
    for m in range(X * EXPERTS):
        pieces = [other[m * PIECE : (m + 1) * PIECE] for other in others]
        slots_ref[m, pl.ds(X * SLOTS, (X - 1) * PIECE)] = jnp.concatenate(pieces, axis=0).astype(
            BF16
        )


def attention_kernel(q_ref, k_ref, v_ref, run_ref, parts_ref, own_ref, gain_ref, out_ref):
    running = run_ref[...]
    columns = running.T
    here = lax.axis_index("x")
    pieces = [parts_ref[m].astype(F32)[SLOTS:] for m in range(X * EXPERTS)]
    each = len(pieces) // 2
    states = [
        jnp.concatenate(pieces[b * each : (b + 1) * each], axis=0).astype(BF16) for b in range(2)
    ]
    for pair in range(PAIRS):
        b, cols = pair // HEADS, pl.ds(pair % HEADS * HD, HD)
        q, column = q_ref[b, :, cols], columns[:, pair : pair + 1]
        head = pair % HEADS
        state = states[b][:, head * HD : (head + 1) * HD]
        state = jnp.where(here == head, own_ref[b * HD : (b + 1) * HD], state)
        weights = fading_scores(q, k_ref[b, :, cols], column, running[pair : pair + 1])
        decayed = (q.astype(F32) * jnp.exp(column)).astype(BF16)
        o = jnp.dot(
            weights, v_ref[b, :, cols], preferred_element_type=F32
        ) + lax.dot_general(
            decayed, state, (((1,), (1,)), ((), ())), preferred_element_type=F32
        )
        scale = lax.rsqrt(jnp.mean(o * o, axis=1, keepdims=True) + 1e-6)
        out_ref[b, :, cols] = (o * scale * gain_ref[:, cols]).astype(BF16)


def slot_rows(facts, place, slots):
    rows = []
    for j in range(2):
        code = facts[4 + j : 5 + j].astype(jnp.int32)
        rows.append(code // CAP * slots + code % CAP + place)
    return rows, [facts[6:7], facts[7:8]]


def expert_kernel(rows_ref, gate_ref, up_ref, down_ref, out_ref):
    total = None
    for j in range(EXPERTS):
        part = pl.ds(j * COLS, COLS)
        both = jnp.concatenate([gate_ref[part, :], up_ref[part, :]], axis=1)
        rows = [rows_ref[x * EXPERTS + j, : X * SLOTS] for x in range(X)]
        term = jnp.dot(jnp.concatenate(rows, axis=1), both, preferred_element_type=F32)
        total = term if total is None else total + term
    width = gate_ref.shape[1]
    gate, up = total[:, :width], total[:, width:]
    hidden = (gate / (1.0 + jnp.exp(-gate)) * up).astype(BF16)
    for j in range(EXPERTS):
        out = jnp.dot(hidden, down_ref[:, pl.ds(j * COLS, COLS)], preferred_element_type=F32)
        parts = [rows_ref[x * EXPERTS + j, X * SLOTS :].astype(F32) for x in range(X)]
        for x in range(X):
            passing = []
            for source in range(X):
                at = (x - source - 1) % X * PIECE
                piece = parts[source][at : at + PIECE] if source != x else jnp.zeros((PIECE, HD), F32)
                passing.append(piece)
            out_ref[x * EXPERTS + j] = jnp.concatenate(
                [out[x * SLOTS : (x + 1) * SLOTS], jnp.concatenate(passing, axis=1)], axis=0
            ).astype(BF16)


def combine_kernel(parts_ref, facts_ref, out_ref):
    index = lax.broadcasted_iota(jnp.int32, (EXPERTS * SLOTS, GROUP), 0)
    place = lax.broadcasted_iota(jnp.int32, (1, GROUP), 1) // MROWS * CAP
    (first, second), gates = slot_rows(facts_ref[:, 4 * HD :], place, SLOTS)
    mix = jnp.where(index == first, gates[0], 0.0) + jnp.where(index == second, gates[1], 0.0)
    mix = mix.astype(BF16)
    total = None
    for x in range(X):
        rows = jnp.concatenate(
            [parts_ref[x * EXPERTS + e, :SLOTS] for e in range(EXPERTS)], axis=0
        )
        term = lax.dot_general(mix, rows, (((0,), (0,)), ((), ())), preferred_element_type=F32)
        total = term if total is None else total + term
    out_ref[...] = total.astype(BF16)


def sum_kernel(parts_ref, out_ref):
    total = parts_ref[0].astype(F32)
    for i in range(1, parts_ref.shape[0]):
        total = total + parts_ref[i].astype(F32)
    out_ref[...] = total.astype(BF16)


def swap(array, axis):
    return lax.all_to_all(array, axis, 0, 0, tiled=True)


def body(
    queries, keys, values, log_decay, norm_gain, expert_ids, gate_weights, w_gate, w_up, w_down
):
    shape = jax.ShapeDtypeStruct
    decay = jnp.transpose(log_decay, (0, 2, 1))
    gain = norm_gain.reshape(1, COLS)
    running, message = call(
        update_kernel,
        (shape((PAIRS, TOK), F32), shape((X, AT_FACTS + 8, HD), BF16)),
        "update",
        [
            pltpu.VMEM((2, HEADS, TOK), F32),
            pltpu.VMEM((2, FEW, COLS), BF16),
            pltpu.VMEM((2, TOK, COLS), BF16),
            pltpu.VMEM((2, TOK, COLS), BF16),
            pltpu.VMEM((2, MROWS), jnp.int32),
            pltpu.VMEM((2, MROWS), F32),
            pltpu.VMEM((8, HD), F32),
            pltpu.SemaphoreType.DMA((6,)),
        ],
        [True] * 6,
    )(decay, queries, keys, values, expert_ids.T, gate_weights.T)
    message = swap(message, "x")
    groups = call(group_kernel, shape((Z, PART + 24, HD), BF16), "group")(message)
    groups = swap(groups, "z")
    back, facts = call(
        scan_kernel,
        (shape((Z, 3 * PART, HD), BF16), shape((8, 5 * HD), F32)),
        "scan",
    )(groups)
    back = swap(back, "z")
    own, slots = call(
        expand_kernel,
        (
            shape((OWN * HD, HD), BF16),
            shape((X * EXPERTS, X * SLOTS + (X - 1) * PIECE, HD), BF16),
        ),
        "expand",
    )(back, message, gain, facts)
    slots = swap(slots, ("x", "y", "core"))
    parts = call(expert_kernel, shape((X * EXPERTS, SLOTS + PIECE, COLS), BF16), "experts")(
        slots, w_gate[0], w_up[0], w_down[0]
    )
    parts = swap(parts, ("x", "y", "core"))
    attn_out = call(attention_kernel, shape((2, TOK, COLS), BF16), "attention")(
        queries, keys, values, running, parts, own, gain
    )
    share = call(combine_kernel, shape((GROUP, COLS), BF16), "combine")(parts, facts)
    share = swap(share.reshape(Z, MROWS, COLS), "z")
    moe_out = call(sum_kernel, shape((MROWS, COLS), BF16), "sum_z")(share)
    return (attn_out, moe_out)


def solution(mesh):
    fine = Mesh(mesh.devices.reshape(Z, X, Y, CORE), ("z", "x", "y", "core"))
    seq, expert = ("z", "x"), ("y", "core")
    placed = (
        P(None, seq, expert),
        P(None, seq, expert),
        P(None, seq, expert),
        P(None, seq, expert),
        P(expert),
        P(seq, None),
        P(seq, None),
        P(expert, None, seq),
        P(expert, None, seq),
        P(expert, seq, None),
    )
    return jax.shard_map(
        body,
        mesh=fine,
        in_specs=placed,
        out_specs=(P(None, seq, expert), P(seq, expert)),
        check_vma=False,
    )
```
